32 devices in a mesh: batch: 16 (over z, x, core), seg: 2 (over y).
Axes of the slice: x: 2, y: 2, z: 4, core: 2. Of those that a mesh axis runs over, the one named last changes fastest.
Arguments:
- tokens: bfloat16 [32, 2, 512, 768], P('batch', 'seg'), may hold values from -6 to 6
- start_memory: float32 [32, 256, 768], P('batch', None, 'seg'), may hold values from -6 to 6
- has_memory: int32 [32], P('batch'), may hold values 0 or 1
- sticky: int32 [32, 2, 512], P('batch', 'seg'), may hold values from 0 to 4095
- w_qkv: bfloat16 [768, 2304], replicated, may hold values from -0.21875 to 0.21875
- w_out: bfloat16 [768, 768], replicated, may hold values from -3 to 3
- w_in: bfloat16 [768, 3072], replicated, may hold values from -0.21875 to 0.21875
- w_back: bfloat16 [3072, 768], replicated, may hold values from -0.109375 to 0.109375
- q_bias: float32 [768], replicated, may hold values from -3 to 3
- v_bias: float32 [768], replicated, may hold values from -3 to 3
- out_bias: float32 [768], replicated, may hold values from -3 to 3
- in_bias: float32 [3072], replicated, may hold values from -3 to 3
- back_bias: float32 [768], replicated, may hold values from -3 to 3
- ln1_gain: float32 [768], replicated, may hold values from 0.5 to 1.5
- ln1_bias: float32 [768], replicated, may hold values from -2 to 2
- ln2_gain: float32 [768], replicated, may hold values from 0.5 to 1.5
- ln2_bias: float32 [768], replicated, may hold values from -2 to 2
- cotangent: bfloat16 [32, 2, 512, 768], P('batch', 'seg'), may hold values from -6 to 6
Outputs:
- result: bfloat16 [32, 2, 512, 768], P('batch', 'seg')
- input_grad: bfloat16 [32, 2, 512, 768], P('batch', 'seg')
- start_memory_grad: float32 [32, 256, 768], P('batch', None, 'seg')
- grad_qkv: float32 [768, 2304], P('batch')
- grad_out: float32 [768, 768], P('batch')
- grad_in: float32 [768, 3072], P('batch')
- grad_back: float32 [3072, 768], P('batch')
- grad_q_bias: float32 [768], P('batch')
- grad_v_bias: float32 [768], P('batch')
- grad_out_bias: float32 [768], P('batch')
- grad_in_bias: float32 [3072], P('batch')
- grad_back_bias: float32 [768], P('batch')
- grad_ln1_gain: float32 [768], P('batch')
- grad_ln1_bias: float32 [768], P('batch')
- grad_ln2_gain: float32 [768], P('batch')
- grad_ln2_bias: float32 [768], P('batch')
The draws below stay inside these ranges and needn't reach their ends.
Inputs may be any that keep to these rules, and one draw needn't show every extreme that they name: `sticky`: grid indices of the 512 points at which each segment samples the previous memory signal. `has_memory`: 1 where a document begins with its given memory coefficients, 0 where its memory begins empty.
All inputs are finite; a program needn't handle non-finite values. No bound on the sum of `has_memory` on one device may be relied on, other than what follows from the above.
Results may differ from the reference program's by a relative error of at most 0.012.
Values sent between devices are 32-bit elements; how exact they have to be, the bound alone decides.
A program may use at most 256 MiB of HBM per device.

```python
import jax
import jax.numpy as jnp
from jax import lax

D = 768
HEADS = 12
HD = 64
FF = 3072
NB = 256
L = 512
STICKY = 512
GRID = 4096
DOCS = 32
SEGS = 2


def touch_ends(values, stream_key, least, top_value):
    longest = values.shape.index(max(values.shape))
    spots = []
    for shift in (0, 1):
        where = [jax.random.randint(jax.random.fold_in(stream_key, axis), (), 0, length) for axis, length in enumerate(values.shape)]
        where[longest] = (where[longest] + shift) % values.shape[longest]
        spots.append(tuple(where))
    return values.at[spots[0]].set(least).at[spots[1]].set(top_value)


def shard_levels(key, shape, split, smallest, top_value):
    level = 1.0
    for position, blocks in split:
        steps = jax.random.uniform(jax.random.fold_in(jax.random.fold_in(key, 6), position), (blocks,), jnp.float32, smallest / len(split), top_value / len(split))
        level = level * jnp.repeat(jnp.exp(steps), shape[position] // blocks).reshape((-1,) + (1,) * (len(shape) - 1 - position))
    return level


def normal_values(key, shape, scale, most, cuts=(), kind=jnp.bfloat16):
    entries = scale * jax.random.normal(key, shape, jnp.float32)
    if cuts:
        entries = entries * shard_levels(key, shape, cuts, -0.22, 0.18)
    return jnp.clip(entries, -most, most).astype(kind)


def setup_inputs(seed: int = 0) -> dict:
    streams_of = jax.random.split(jax.random.key(seed), 19)
    return {
        "tokens": normal_values(streams_of[0], (DOCS, SEGS, L, D), 1.0, 6.0, ((0, 16), (1, 2))),
        "start_memory": normal_values(streams_of[1], (DOCS, NB, D), 1.0, 6.0, ((0, 16), (2, 2)), jnp.float32),
        "has_memory": touch_ends((jax.random.randint(streams_of[2], (DOCS,), 0, 2) < 1).astype(jnp.int32), jax.random.fold_in(streams_of[2], 1), 0, 1),
        "sticky": touch_ends(jax.random.randint(streams_of[3], (DOCS, SEGS, STICKY), 0, GRID), jax.random.fold_in(streams_of[3], 1), 0, GRID - 1).astype(jnp.int32),
        "w_qkv": normal_values(streams_of[4], (D, 3 * D), D ** -0.5, 0.21875),
        "w_out": normal_values(streams_of[5], (D, D), (4 * D // (L + NB)) ** -0.5, 3.0),
        "w_in": normal_values(streams_of[6], (D, FF), D ** -0.5, 0.21875),
        "w_back": normal_values(streams_of[7], (FF, D), FF ** -0.5, 0.109375),
        "q_bias": normal_values(streams_of[8], (D,), 0.5, 3.0, (), jnp.float32),
        "v_bias": normal_values(streams_of[9], (D,), 0.5, 3.0, (), jnp.float32),
        "out_bias": normal_values(streams_of[10], (D,), 0.5, 3.0, (), jnp.float32),
        "in_bias": normal_values(streams_of[11], (FF,), 0.5, 3.0, (), jnp.float32),
        "back_bias": normal_values(streams_of[12], (D,), 0.5, 3.0, (), jnp.float32),
        "ln1_gain": jnp.clip(1.0 + 0.1 * jax.random.normal(streams_of[13], (D,), jnp.float32), 0.5, 1.5),
        "ln1_bias": normal_values(streams_of[14], (D,), 0.3, 2.0, (), jnp.float32),
        "ln2_gain": jnp.clip(1.0 + 0.1 * jax.random.normal(streams_of[15], (D,), jnp.float32), 0.5, 1.5),
        "ln2_bias": normal_values(streams_of[16], (D,), 0.3, 2.0, (), jnp.float32),
        "cotangent": normal_values(streams_of[17], (DOCS, SEGS, L, D), 1.0, 6.0, ((0, 16), (1, 2))),
    }


EPSILON = 1e-05
RIDGE = 0.5
MASKED = -1e+30
PRECISE = lax.Precision.HIGHEST

@jax.custom_vjp
def low(v):
    return lax.optimization_barrier(v.astype(jnp.bfloat16)).astype(jnp.float32)

@jax.custom_vjp
def low_back(v):
    return v

def low_keep(v):
    return (low(v), None)

def low_pass(kept, grad):
    return (grad,)

def back_keep(v):
    return (v, None)

def back_low(kept, grad):
    return (low(grad),)
low.defvjp(low_keep, low_pass)
low_back.defvjp(back_keep, back_low)

def precise(left, right):
    return jnp.dot(left, right, precision=PRECISE)

def layer_norm(values, gain, offset):
    center = lax.optimization_barrier(jnp.mean(values, -1, keepdims=True))
    shifted = values - center
    spread = lax.optimization_barrier(jnp.mean(shifted * shifted, -1, keepdims=True))
    return shifted * lax.rsqrt(spread + EPSILON) * gain + offset

def basis_at(points):
    centers = (jnp.arange(NB, dtype=jnp.float32) + 0.5) / NB
    scaled = (points[None, :] - centers[:, None]) * NB
    return jnp.exp(-0.5 * scaled * scaled)

def memory_maps(positions):
    old_times = (positions.astype(jnp.float32) + 0.5) / GRID
    new_times = 0.5 + 0.5 * (jnp.arange(L, dtype=jnp.float32) + 0.5) / L
    design = jnp.concatenate([basis_at(0.5 * old_times), basis_at(new_times)], axis=1)
    gram = precise(design, design.T) + RIDGE * jnp.eye(NB, dtype=jnp.float32)
    factor = jnp.linalg.cholesky(gram)
    solved = jax.scipy.linalg.cho_solve((factor, True), design)
    carry_map = precise(solved[:, :STICKY], basis_at(old_times).T)
    return (carry_map, solved[:, STICKY:])

def visible():
    row_ids = jnp.arange(L)[:, None]
    col_ids = jnp.arange(L + NB)[None, :]
    return (col_ids >= L) | (col_ids <= row_ids)

def segment(weights, seg_tokens, memory, carry_map, data_map):
    w_qkv, w_out, w_in, w_back, q_bias, v_bias, out_bias, in_bias, back_bias, ln1_gain, ln1_bias, ln2_gain, ln2_bias = weights
    hidden = low(layer_norm(seg_tokens, ln1_gain, ln1_bias))
    new_memory = precise(carry_map, memory) + precise(data_map, hidden)
    projected = precise(hidden, w_qkv)
    mem_in = low(memory)
    mem_proj = precise(mem_in, w_qkv[:, D:])
    query = low(low_back(projected[:, :D] + q_bias))
    keys = low(low_back(jnp.concatenate([projected[:, D:2 * D], mem_proj[:, :D]], axis=0)))
    values = low(low_back(jnp.concatenate([projected[:, 2 * D:], mem_proj[:, D:]], axis=0) + v_bias))
    query_heads = query.reshape(L, HEADS, HD)
    key_heads = keys.reshape(L + NB, HEADS, HD)
    value_heads = values.reshape(L + NB, HEADS, HD)
    scale_factor = HD ** (-0.5)
    scores = low_back(jnp.einsum('lhd,khd->hlk', query_heads, key_heads, precision=PRECISE) * scale_factor)
    scores = jnp.where(visible()[None], scores, MASKED)
    row_peak = lax.optimization_barrier(jnp.max(scores, -1, keepdims=True))
    weight = jnp.exp(scores - row_peak)
    probabilities = low(weight / lax.optimization_barrier(jnp.sum(weight, -1, keepdims=True)))
    attended = jnp.einsum('hlk,khd->lhd', probabilities, value_heads, precision=PRECISE).reshape(L, D)
    mixed = low(low_back(attended))
    residual = seg_tokens + low_back(precise(mixed, w_out) + out_bias)
    normed = low(layer_norm(residual, ln2_gain, ln2_bias))
    activated = low(jax.nn.gelu(low_back(precise(normed, w_in) + in_bias), approximate=True))
    return (residual + low_back(precise(activated, w_back) + back_bias), new_memory)

def reference(tokens, start_memory, has_memory, sticky, w_qkv, w_out, w_in, w_back, q_bias, v_bias, out_bias, in_bias, back_bias, ln1_gain, ln1_bias, ln2_gain, ln2_bias, cotangent):
    params = tuple((p.astype(jnp.float32) for p in (w_qkv, w_out, w_in, w_back, q_bias, v_bias, out_bias, in_bias, back_bias, ln1_gain, ln1_bias, ln2_gain, ln2_bias)))
    empty_grads = tuple((jnp.zeros(p.shape, jnp.float32) for p in params))

    def one_doc(totals, inputs):
        doc_tokens, begin, flag, doc_sticky, doc_cot = inputs
        carry_maps, data_maps = lax.map(memory_maps, doc_sticky)

        def forward(weights, doc_values, first_memory):
            start = flag.astype(jnp.float32) * first_memory

            def advance(memory, pieces):
                seg_tokens, carry_map, data_map = pieces
                output, new_memory = jax.checkpoint(segment)(weights, seg_tokens, memory, carry_map, data_map)
                return (new_memory, output)
            _, outputs = lax.scan(advance, start, (doc_values, carry_maps, data_maps))
            return outputs
        outputs, pullback = jax.vjp(forward, params, doc_tokens.astype(jnp.float32), begin.astype(jnp.float32))
        grads, token_grads, begin_grad = pullback(doc_cot.astype(jnp.float32))
        totals = tuple((a + b for a, b in zip(totals, grads)))
        return (totals, (outputs.astype(jnp.bfloat16), token_grads.astype(jnp.bfloat16), begin_grad))
    totals, (outputs, token_grads, begin_grads) = lax.scan(one_doc, empty_grads, (tokens, start_memory, has_memory, sticky, cotangent))
    return (outputs, token_grads, begin_grads) + totals
```

```python
import math

import jax
import jax.numpy as jnp
from jax import lax
from jax.sharding import PartitionSpec as P

HEADS = 12
HD = 64
NB = 256
L = 512
STICKY = 512
GRID = 4096

EPSILON = 1e-05
RIDGE = 0.5
MASKED = -1e30
PRECISE = lax.Precision.HIGHEST
F32 = jnp.float32
BF16 = jnp.bfloat16


def shifted_2(block, axis, distance):
    devices = range(lax.axis_size(axis))
    route = [(i - distance, i) for i in devices if i - distance in devices]
    return lax.ppermute(block, axis, route)


def precise(left, right):
    return jnp.matmul(left, right, precision=PRECISE)


def layer_norm(values, gain, offset):
    center = jnp.mean(values, -1, keepdims=True)
    shifted = values - center
    spread = jnp.mean(shifted * shifted, -1, keepdims=True)
    return shifted * lax.rsqrt(spread + EPSILON) * gain + offset


def gelu_tanh(values):
    return jax.nn.gelu(values, approximate=True)


def basis_at(points):
    centers = (jnp.arange(NB, dtype=jnp.float32) + 0.5) / NB
    scaled = (points[None, :] - centers[:, None]) * NB
    return jnp.exp(-0.5 * scaled * scaled)


def memory_maps(positions):
    old_times = (positions.astype(jnp.float32) + 0.5) / GRID
    new_times = 0.5 + 0.5 * (jnp.arange(L, dtype=jnp.float32) + 0.5) / L
    design = jnp.concatenate([basis_at(0.5 * old_times), basis_at(new_times)], axis=1)
    gram = precise(design, design.T) + RIDGE * jnp.eye(NB, dtype=jnp.float32)
    factor = jnp.linalg.cholesky(gram)
    solved = jax.scipy.linalg.cho_solve((factor, True), design)
    carry_map = precise(solved[:, :STICKY], basis_at(old_times).T)
    return (carry_map, solved[:, STICKY:])


def visible():
    row_ids = jnp.arange(L)[:, None]
    col_ids = jnp.arange(L + NB)[None, :]
    return (col_ids >= L) | (col_ids <= row_ids)


def mm(a, b):
    return jnp.dot(a, b, preferred_element_type=F32)


def outer(a, b):
    return lax.dot_general(a, b, (((0,), (0,)), ((), ())), preferred_element_type=F32)


def swap(block, axis, distance):
    n = lax.axis_size(axis)
    return lax.ppermute(block, axis, [(i, i ^ distance) for i in range(n)])


def halve(block, axis, distance, dim):
    bit = (lax.axis_index(axis) // distance) % 2
    send = lax.dynamic_index_in_dim(block, 1 - bit, dim, keepdims=False)
    keep = lax.dynamic_index_in_dim(block, bit, dim, keepdims=False)
    return keep + swap(send, axis, distance)


def spread(grad, seg_place):
    n, s = lax.axis_size("batch"), lax.axis_size("seg")
    bits = n.bit_length() - 1
    rows, cols = grad.shape
    own = rows // n
    split = s if seg_place < bits and own % s == 0 else 1
    work = grad.reshape((2,) * bits + (split, own // split, cols))
    for k in range(bits + 1):
        if k == seg_place:
            if split == 1:
                d = 1
                while d < s:
                    work = work + swap(work, "seg", d)
                    d *= 2
            else:
                left = bits - k
                work = work.reshape((2,) * left + (2,) * (s.bit_length() - 1) + (own // split, cols))
                d = 1
                while d < s:
                    work = halve(work, "seg", d, work.ndim - 3)
                    d *= 2
        if k < bits:
            work = halve(work, "batch", 1 << k, bits - 1 - k)
    if split > 1:
        d = s // 2
        while d >= 1:
            bit = (lax.axis_index("seg") // d) % 2
            other = swap(work, "seg", d)
            work = jnp.where(bit == 0, jnp.concatenate([work, other], 0), jnp.concatenate([other, work], 0))
            d //= 2
    return work.reshape(own, cols)


def shards(
    tokens,
    start_memory,
    has_memory,
    sticky,
    w_qkv,
    w_out,
    w_in,
    w_back,
    q_bias,
    v_bias,
    out_bias,
    in_bias,
    back_bias,
    ln1_gain,
    ln1_bias,
    ln2_gain,
    ln2_bias,
    cotangent,
):
    width = w_qkv.shape[0]
    docs = tokens.shape[0]
    scale = HD ** (-0.5)
    is_first = lax.axis_index("seg") == 0
    chain = lax.axis_size("seg")
    flags = has_memory.astype(F32)[:, None, None]
    allowed = visible()

    full_start = lax.all_gather(start_memory, "seg", axis=2, tiled=True)
    own_start = jnp.where(is_first, flags * full_start, 0.0)

    x = tokens[:, 0].astype(F32)
    cot = cotangent[:, 0].reshape(docs * L, width)
    carry_map, data_map = jax.vmap(memory_maps)(sticky[:, 0])
    hidden = layer_norm(x, ln1_gain, ln1_bias).astype(BF16)
    fresh = precise(data_map, hidden.astype(F32))

    def down_step(_, incoming):
        return shifted_2(precise(carry_map, incoming) + fresh, "seg", 1) + own_start

    memory = own_start
    for i in range(chain - 1):
        memory = down_step(i, memory)

    hidden_rows = hidden.reshape(docs * L, width)
    projected = mm(hidden_rows, w_qkv)
    act_grad = mm(cot, w_back.T)
    mem_in = memory.astype(BF16)
    mem_rows = mem_in.reshape(docs * NB, width)
    mem_proj = mm(mem_rows, w_qkv[:, width:]).reshape(docs, NB, 2 * width)
    projected = projected.reshape(docs, L, 3 * width)
    query = (projected[..., :width] + q_bias).astype(BF16)
    keys = jnp.concatenate([projected[..., width : 2 * width], mem_proj[..., :width]], 1).astype(BF16)
    values = (jnp.concatenate([projected[..., 2 * width :], mem_proj[..., width:]], 1) + v_bias).astype(BF16)
    qh = query.reshape(docs, L, HEADS, HD)
    kh = keys.reshape(docs, L + NB, HEADS, HD)
    vh = values.reshape(docs, L + NB, HEADS, HD)

    def scores_of():
        s = jnp.einsum("blhd,bkhd->bhlk", qh, kh, preferred_element_type=F32) * scale
        return jnp.where(allowed[None, None], s, MASKED)

    scores = scores_of()
    peak = jnp.max(scores, -1, keepdims=True)
    weight = jnp.exp(scores - peak)
    total = jnp.sum(weight, -1, keepdims=True)
    log_total = peak + jnp.log(total)
    probs = (weight / total).astype(BF16)
    mixed = jnp.einsum("bhlk,bkhd->blhd", probs, vh, preferred_element_type=F32).astype(BF16)
    mixed = mixed.reshape(docs * L, width)
    x_rows = x.reshape(docs * L, width)
    residual = x_rows + (mm(mixed, w_out) + out_bias)
    normed = layer_norm(residual, ln2_gain, ln2_bias).astype(BF16)
    pre_act = mm(normed, w_in) + in_bias
    activated, gelu_back = jax.vjp(gelu_tanh, pre_act)
    act_low = activated.astype(BF16)
    grad_back = spread(outer(act_low, cot), 2)
    output = (residual + (mm(act_low, w_back) + back_bias)).astype(BF16)
    out_grad = cot.astype(F32)
    (pre_grad,) = gelu_back(act_grad)
    pre_low = pre_grad.astype(BF16)
    grad_in = spread(outer(normed, pre_low), 1)
    normed_grad = mm(pre_low, w_in.T)
    _, norm_two_back = jax.vjp(layer_norm, residual, ln2_gain, ln2_bias)
    residual_part, gain_two, bias_two = norm_two_back(normed_grad)
    residual_grad = out_grad + residual_part
    branch = residual_grad.astype(BF16)
    grad_out = spread(outer(mixed, branch), 2)
    mixed_grad = mm(branch, w_out.T).astype(BF16)
    mh = mixed_grad.reshape(docs, L, HEADS, HD)
    chances = jnp.exp(scores_of() - log_total)
    prob_grad = jnp.einsum("blhd,bkhd->bhlk", mh, vh, preferred_element_type=F32)
    delta = jnp.sum(chances * prob_grad, -1, keepdims=True)
    score_low = (chances * (prob_grad - delta)).astype(BF16)
    query_grad = (jnp.einsum("bhlk,bkhd->blhd", score_low, kh, preferred_element_type=F32) * scale).astype(BF16)
    key_grad = (jnp.einsum("bhlk,blhd->bkhd", score_low, qh, preferred_element_type=F32) * scale).astype(BF16)
    value_grad = jnp.einsum("bhlk,blhd->bkhd", probs, mh, preferred_element_type=F32).astype(BF16)
    query_grad = query_grad.reshape(docs, L, width)
    key_grad = key_grad.reshape(docs, L + NB, width)
    value_grad = value_grad.reshape(docs, L + NB, width)
    token_proj = jnp.concatenate([query_grad, key_grad[:, :L], value_grad[:, :L]], 2).reshape(docs * L, 3 * width)
    memory_proj = jnp.concatenate([key_grad[:, L:], value_grad[:, L:]], 2).reshape(docs * NB, 2 * width)
    local_grad = mm(memory_proj, w_qkv[:, width:].T).reshape(docs, NB, width)
    carry_back = carry_map.swapaxes(1, 2)
    incoming = jnp.zeros_like(local_grad)
    for i in range(chain - 1):
        incoming = shifted_2(precise(carry_back, incoming) + local_grad, "seg", -1)
    key_rows = token_proj[:, width : 2 * width]
    value_rows = token_proj[:, 2 * width :]
    grad_q = spread(outer(hidden_rows, token_proj[:, :width]), 1)
    grad_k = spread(outer(hidden_rows, key_rows) + outer(mem_rows, memory_proj[:, :width]), 2)
    grad_v = spread(outer(hidden_rows, value_rows) + outer(mem_rows, memory_proj[:, width:]), 1)
    hidden_grad = mm(token_proj, w_qkv.T)
    hidden_grad = hidden_grad + precise(data_map.swapaxes(1, 2), incoming).reshape(docs * L, width)
    _, norm_one_back = jax.vjp(layer_norm, x_rows, ln1_gain, ln1_bias)
    token_part, gain_one, bias_one = norm_one_back(hidden_grad)
    input_grad = (residual_grad + token_part).astype(BF16)
    start_grad = jnp.where(is_first, flags * (local_grad + precise(carry_back, incoming)), 0.0)
    start_share = lax.psum_scatter(start_grad, "seg", scatter_dimension=2, tiled=True)

    batch = lax.axis_size("batch")
    small = [
        jnp.sum(query_grad.astype(F32), (0, 1)),
        jnp.sum(value_grad.astype(F32), (0, 1)),
        jnp.sum(branch.astype(F32), 0),
        jnp.sum(pre_low.astype(F32), 0),
        jnp.sum(out_grad, 0),
        gain_one,
        bias_one,
        gain_two,
        bias_two,
    ]
    packed = jnp.concatenate([g.reshape(batch, -1) for g in small], 1)
    packed = spread(packed, 4)[0]
    vectors = []
    offset = 0
    for g in small:
        length = g.shape[0] // batch
        vectors.append(packed[offset : offset + length])
        offset += length
    grad_qkv = jnp.concatenate([grad_q, grad_k, grad_v], 1)
    return (
        output.reshape(docs, 1, L, width),
        input_grad.reshape(docs, 1, L, width),
        start_share,
        grad_qkv,
        grad_out,
        grad_in,
        grad_back,
    ) + tuple(vectors)


def solution(mesh):
    rows = P("batch", "seg", None, None)
    in_specs = (rows, P("batch", None, "seg"), P("batch"), P("batch", "seg", None)) + (P(),) * 13 + (rows,)
    out_specs = (rows, rows, P("batch", None, "seg")) + (P("batch", None),) * 4 + (P("batch"),) * 9
    return jax.shard_map(shards, mesh=mesh, in_specs=in_specs, out_specs=out_specs, check_vma=False)
```

```python
import functools

import jax
import jax.numpy as jnp
from jax import lax
from jax.experimental import pallas as pl
from jax.experimental.pallas import tpu as pltpu
from jax.sharding import PartitionSpec as P

HEADS = 12
HD = 64
NB = 256
L = 512
STICKY = 512
GRID = 4096

EPSILON = 1e-05
RIDGE = 0.5
HI = lax.Precision.HIGHEST
F32 = jnp.float32
BF16 = jnp.bfloat16
EXP2_SCALE = HD**-0.5 * 1.4426950408889634
LEAF = 32
PIVOTS = 4


def dot_hi(a, b, ca, cb):
    return lax.dot_general(a, b, (((ca,), (cb,)), ((), ())), precision=HI, preferred_element_type=F32)

def bumps(times):
    centers = (lax.broadcasted_iota(jnp.int32, (NB, 1), 0).astype(F32) + 0.5) / NB
    scaled = (times - centers) * NB
    return jnp.exp(-0.5 * scaled * scaled)

def small_inverse(s):
    p = len(s)
    s = [list(r) for r in s]
    for k in range(p):
        inv = 1.0 / s[k][k]
        row = [inv if j == k else s[k][j] * inv for j in range(p)]
        for i in range(p):
            if i != k:
                f = s[i][k]
                s[i] = [-f * row[j] if j == k else s[i][j] - f * row[j] for j in range(p)]
        s[k] = row
    return s


def leaf_inverse(d):
    n = d.shape[0]
    rows = lax.broadcasted_iota(jnp.int32, (n, n), 0)
    lanes = lax.broadcasted_iota(jnp.int32, (1, n), 1)
    for k in range(0, n, PIVOTS):
        cols = [jnp.broadcast_to(d[:, k + j : k + j + 1], (n, n)) for j in range(PIVOTS)]
        inv = small_inverse([[cols[j][k + i : k + i + 1] for j in range(PIVOTS)] for i in range(PIVOTS)])
        old = [d[k + j : k + j + 1] for j in range(PIVOTS)]
        inside = (lanes >= k) & (lanes < k + PIVOTS)
        fresh = []
        for i in range(PIVOTS):
            r = inv[i][0] * old[0]
            for j in range(1, PIVOTS):
                r = r + inv[i][j] * old[j]
            for j in range(PIVOTS):
                r = jnp.where(lanes == k + j, inv[i][j], r)
            fresh.append(r)
        out = jnp.where(inside, 0.0, d)
        for i in range(PIVOTS):
            out = out - cols[i] * fresh[i]
        for i in range(PIVOTS):
            out = jnp.where(rows == k + i, fresh[i], out)
        d = out
    return d


def maps_kernel(docs, sticky_ref, carry_ref, data_ref, a_ref):
    new_times = 0.5 + 0.5 * (lax.broadcasted_iota(jnp.int32, (1, L), 1).astype(F32) + 0.5) / L
    fresh = bumps(new_times)
    eye = (lax.broadcasted_iota(jnp.int32, (NB, NB), 0) == lax.broadcasted_iota(jnp.int32, (NB, NB), 1)).astype(F32)
    base = dot_hi(fresh, fresh, 1, 1) + RIDGE * eye
    for d in range(docs):
        old = (sticky_ref[pl.ds(d, 1), :].astype(F32) + 0.5) / GRID
        f1 = bumps(0.5 * old)
        a_ref[d] = base + dot_hi(f1, f1, 1, 1)
        carry_ref[d] = dot_hi(f1, bumps(old), 1, 1)
    lanes = lax.broadcasted_iota(jnp.int32, (1, NB), 1) // LEAF
    for j in range(NB // LEAF):
        sl = pl.ds(j * LEAF, LEAF)
        leaves = [leaf_inverse(a_ref[d, sl, sl]) for d in range(docs)]
        for d in range(docs):
            p = leaves[d]
            mine = lanes == j
            row = dot_hi(p, a_ref[d, sl, :], 1, 0)
            wide = jnp.concatenate([p] * (NB // LEAF), 1)
            row = jnp.where(mine, wide, row)
            col = a_ref[d, :, sl]
            rest = jnp.where(mine, 0.0, a_ref[d])
            a_ref[d] = rest - dot_hi(col, row, 1, 0)
            a_ref[d, sl, :] = row
    for d in range(docs):
        x = a_ref[d]
        carry_ref[d] = dot_hi(x, carry_ref[d], 1, 0)
        data_ref[d] = dot_hi(x, fresh, 1, 0)

def memory_maps(sticky):
    docs = sticky.shape[0]
    return pl.pallas_call(functools.partial(maps_kernel, docs),
        out_shape=[jax.ShapeDtypeStruct((docs, NB, NB), F32), jax.ShapeDtypeStruct((docs, NB, L), F32)],
        scratch_shapes=[pltpu.VMEM((docs, NB, NB), F32)],
        compiler_params=pltpu.CompilerParams(vmem_limit_bytes=32 << 20),
        cost_estimate=pl.CostEstimate(flops=docs * 10**10, bytes_accessed=docs * 10**6, transcendentals=0),
    )(sticky)


def nt(a, b):
    return lax.dot_general(a, b, (((1,), (1,)), ((), ())), preferred_element_type=F32)

def tn(a, b):
    return lax.dot_general(a, b, (((0,), (0,)), ((), ())), preferred_element_type=F32)

def nn(a, b):
    return jnp.dot(a, b, preferred_element_type=F32)

def head_lanes(h):
    return lax.broadcasted_iota(jnp.int32, (1, 2 * HD), 1) // HD == h

def causal():
    half = L // 2
    return lax.broadcasted_iota(jnp.int32, (half, half), 0) <= lax.broadcasted_iota(jnp.int32, (half, half), 1)

def attend_kernel(q_ref, k_ref, v_ref, mk_ref, mv_ref, out_ref, peak_ref):
    half = L // 2
    q = q_ref[0]; k = k_ref[0]; v = v_ref[0]; mk = mk_ref[0]; mv = mv_ref[0]
    seen = causal()
    outs = []
    for h in range(2):
        qh = jnp.where(head_lanes(h), q, jnp.zeros_like(q))
        s00 = jnp.where(seen, nt(k[:half], qh[:half]), -1e30)
        s01 = nt(k[:half], qh[half:])
        s11 = jnp.where(seen, nt(k[half:], qh[half:]), -1e30)
        sm = nt(mk, qh)
        sides = []
        for side, parts in enumerate(([s00, sm[:, :half]], [s01, s11, sm[:, half:]])):
            peak = functools.reduce(jnp.maximum, [jnp.max(p, 0, keepdims=True) for p in parts])
            ps = [jnp.exp2((p - peak) * EXP2_SCALE) for p in parts]
            total = functools.reduce(jnp.add, [jnp.sum(p, 0, keepdims=True) for p in ps])
            vs = [v[:half], mv] if side == 0 else [v[:half], v[half:], mv]
            o = functools.reduce(jnp.add, [tn(a, p.astype(BF16)) for a, p in zip(vs, ps)])
            sides.append(o * (1.0 / total))
            peak_ref[0, 0, h, pl.ds(side * half, half)] = (peak * EXP2_SCALE + jnp.log2(total))[0]
        outs.append(jnp.concatenate(sides, 1))
    lanes = lax.broadcasted_iota(jnp.int32, (2 * HD, 1), 0) // HD == 0
    out_ref[0] = jnp.where(lanes, outs[0], outs[1]).T.astype(BF16)

def attend(qkv, mem):
    docs, _, w3 = qkv.shape
    w = w3 // 3
    pairs = w // 128
    tok = lambda o: pl.BlockSpec((1, L, 128), lambda d, i: (d, 0, o * pairs + i))
    me = lambda o: pl.BlockSpec((1, NB, 128), lambda d, i: (d, 0, o * pairs + i))
    return pl.pallas_call(attend_kernel, grid=(docs, pairs),
        in_specs=[tok(0), tok(1), tok(2), me(0), me(1)],
        out_specs=[tok(0), pl.BlockSpec((1, 1, 2, L), lambda d, i: (d, i, 0, 0))],
        out_shape=[jax.ShapeDtypeStruct((docs, L, w), BF16), jax.ShapeDtypeStruct((docs, pairs, 2, L), F32)],
        compiler_params=pltpu.CompilerParams(vmem_limit_bytes=48 << 20),
        cost_estimate=pl.CostEstimate(flops=docs * pairs * 8 * 768 * 512 * 128, bytes_accessed=docs * L * w * 10, transcendentals=docs * 12 * 768 * 512),
    )(qkv, qkv, qkv, mem, mem)

def grads_core(q_ref, k_ref, v_ref, mk_ref, mv_ref, g_ref, o_ref, peak_ref, dtok_ref, dmem_ref):
    half = L // 2
    q = q_ref[0]; k = k_ref[0]; v = v_ref[0]; mk = mk_ref[0]; mv = mv_ref[0]; g = g_ref[0]
    scale = HD ** -0.5
    seen = causal()
    go = g.astype(F32) * o_ref[0].astype(F32)
    pick = (lax.broadcasted_iota(jnp.int32, (8, 2 * HD), 1) // HD == lax.broadcasted_iota(jnp.int32, (8, 2 * HD), 0)).astype(F32)
    delta = lax.dot_general(pick, go, (((1,), (1,)), ((), ())), precision=lax.Precision.HIGHEST, preferred_element_type=F32)
    first = head_lanes(0)
    res = []
    for h in range(2):
        mine = head_lanes(h)
        qh = jnp.where(mine, q, jnp.zeros_like(q))
        gh = jnp.where(mine, g, jnp.zeros_like(g))
        lse = peak_ref[0, 0, pl.ds(h, 1), :]
        dh = delta[h:h + 1]
        def tile(kk, vv, lo, hi, mask):
            s = nt(kk, qh[lo:hi])
            p = jnp.exp2(s * EXP2_SCALE - lse[:, lo:hi])
            if mask:
                p = jnp.where(seen, p, 0.0)
            dp = nt(vv, gh[lo:hi])
            return p.astype(BF16), (p * (dp - dh[:, lo:hi])).astype(BF16)
        p00, t00 = tile(k[:half], v[:half], 0, half, True)
        p01, t01 = tile(k[:half], v[:half], half, L, False)
        p11, t11 = tile(k[half:], v[half:], half, L, True)
        pm, tm = tile(mk, mv, 0, L, False)
        dv0 = nn(p00, g[:half]) + nn(p01, g[half:])
        dv1 = nn(p11, g[half:])
        dvm = nn(pm, g)
        dk0 = nn(t00, q[:half]) + nn(t01, q[half:])
        dk1 = nn(t11, q[half:])
        dkm = nn(tm, q)
        dq0 = tn(k[:half], t00) + tn(mk, tm[:, :half])
        dq1 = tn(k[:half], t01) + tn(k[half:], t11) + tn(mk, tm[:, half:])
        res.append((jnp.concatenate([dq0, dq1], 1), jnp.concatenate([dk0, dk1], 0), jnp.concatenate([dv0, dv1], 0), dkm, dvm))
    rows = lax.broadcasted_iota(jnp.int32, (2 * HD, 1), 0) // HD == 0
    dq = (jnp.where(rows, res[0][0], res[1][0]).T * scale).astype(BF16)
    dk, dv, dkm, dvm = [jnp.where(first, a, b) for a, b in zip(res[0][1:], res[1][1:])]
    dk = (dk * scale).astype(BF16); dkm = (dkm * scale).astype(BF16)
    dv = dv.astype(BF16); dvm = dvm.astype(BF16)
    dtok_ref[0, 0] = dq; dtok_ref[1, 0] = dk; dtok_ref[2, 0] = dv
    dmem_ref[0, 0] = dkm; dmem_ref[1, 0] = dvm
    qs = jnp.sum(dq.astype(F32), 0, keepdims=True)
    vs = jnp.sum(dv.astype(F32), 0, keepdims=True) + jnp.sum(dvm.astype(F32), 0, keepdims=True)
    return qs, vs


def grads_kernel(*refs):
    qs, vs = grads_core(*refs[:-1])
    r = lax.broadcasted_iota(jnp.int32, (8, 128), 0)
    refs[-1][0] = jnp.where(r == 0, qs, jnp.where(r == 1, vs, 0.0))

def attend_grads(qkv, mem, g, mixed, lse):
    docs, _, w3 = qkv.shape
    w = w3 // 3
    pairs = w // 128
    tok = lambda o: pl.BlockSpec((1, L, 128), lambda d, i: (d, 0, o * pairs + i))
    me = lambda o: pl.BlockSpec((1, NB, 128), lambda d, i: (d, 0, o * pairs + i))
    return pl.pallas_call(grads_kernel, grid=(docs, pairs),
        in_specs=[tok(0), tok(1), tok(2), me(0), me(1), tok(0), tok(0), pl.BlockSpec((1, 1, 2, L), lambda d, i: (d, i, 0, 0))],
        out_specs=[pl.BlockSpec((3, 1, L, 128), lambda d, i: (0, d, 0, i)), pl.BlockSpec((2, 1, NB, 128), lambda d, i: (0, d, 0, i)), pl.BlockSpec((1, 8, 128), lambda d, i: (d, 0, i))],
        out_shape=[jax.ShapeDtypeStruct((3, docs, L, w), BF16), jax.ShapeDtypeStruct((2, docs, NB, w), BF16), jax.ShapeDtypeStruct((docs, 8, w), F32)],
        compiler_params=pltpu.CompilerParams(vmem_limit_bytes=48 << 20),
        cost_estimate=pl.CostEstimate(flops=docs * pairs * 20 * 768 * 512 * 128, bytes_accessed=docs * L * w * 16, transcendentals=docs * 12 * 768 * 512),
    )(qkv, qkv, qkv, mem, mem, g, mixed, lse)


def mm(a, b):
    return jnp.dot(a, b, preferred_element_type=F32)


def normalised(values):
    center = jnp.mean(values, -1, keepdims=True)
    shifted = values - center
    rate = lax.rsqrt(jnp.mean(shifted * shifted, -1, keepdims=True) + EPSILON)
    return shifted * rate, rate


def norm_back(unit, rate, scaled_grad):
    inner = jnp.mean(scaled_grad * unit, -1, keepdims=True)
    return rate * (scaled_grad - jnp.mean(scaled_grad, -1, keepdims=True) - unit * inner)


def whole(shape):
    return pl.BlockSpec(shape, lambda *_: (0,) * len(shape), pipeline_mode=pl.Buffered(1))


def col_sums(values):
    return jnp.sum(values, 0, keepdims=True)


def project_kernel(x_ref, w_ref, bias_ref, gain_ref, offset_ref, hidden_ref, qkv_ref):
    unit, _ = normalised(x_ref[0].astype(F32))
    hidden = (unit * gain_ref[...] + offset_ref[...]).astype(BF16)
    hidden_ref[0] = hidden
    qkv_ref[0] = (mm(hidden, w_ref[...]) + bias_ref[...]).astype(BF16)


def project(x, w_qkv, bias, gain, offset):
    docs, _, w = x.shape
    tile = 256
    rows = lambda c: pl.BlockSpec((1, tile, c), lambda d, i: (d, i, 0))
    return pl.pallas_call(
        project_kernel,
        grid=(docs, L // tile),
        in_specs=[rows(w), whole(w_qkv.shape), whole((1, 3 * w)), whole((1, w)), whole((1, w))],
        out_specs=[rows(w), rows(3 * w)],
        out_shape=[jax.ShapeDtypeStruct((docs, L, w), BF16), jax.ShapeDtypeStruct((docs, L, 3 * w), BF16)],
        compiler_params=pltpu.CompilerParams(vmem_limit_bytes=40 << 20),
        cost_estimate=pl.CostEstimate(flops=docs * L * w * w * 6, bytes_accessed=docs * L * w * 10, transcendentals=0),
    )(x, w_qkv, bias[None], gain[None], offset[None])


def renew_kernel(carry_ref, data_ref, memory_ref, hidden_ref, out_ref):
    out_ref[0] = dot_hi(carry_ref[0], memory_ref[0], 1, 0) + dot_hi(data_ref[0], hidden_ref[0].astype(F32), 1, 0)


def renew(carry_map, data_map, memory, hidden):
    docs, _, w = hidden.shape
    one = lambda r, c: pl.BlockSpec((1, r, c), lambda d: (d, 0, 0))
    return pl.pallas_call(
        renew_kernel,
        grid=(docs,),
        in_specs=[one(NB, NB), one(NB, L), one(NB, w), one(L, w)],
        out_specs=one(NB, w),
        out_shape=jax.ShapeDtypeStruct((docs, NB, w), F32),
        compiler_params=pltpu.CompilerParams(vmem_limit_bytes=40 << 20),
        cost_estimate=pl.CostEstimate(flops=docs * 6 * NB * 768 * w * 2, bytes_accessed=docs * NB * w * 8, transcendentals=0),
    )(carry_map, data_map, memory, hidden)


def recall_kernel(memory_ref, w_ref, bias_ref, low_ref, out_ref):
    low = memory_ref[...].astype(BF16)
    low_ref[...] = low
    out_ref[...] = (mm(low, w_ref[...]) + bias_ref[...]).astype(BF16)


def recall(memory, w_qkv, bias):
    rows, w = memory.shape
    tile = w
    return pl.pallas_call(
        recall_kernel,
        grid=(2,),
        in_specs=[whole((rows, w)), pl.BlockSpec((w, tile), lambda i: (0, 1 + i)), pl.BlockSpec((1, tile), lambda i: (0, 1 + i))],
        out_specs=[pl.BlockSpec((rows, w), lambda i: (0, 0)), pl.BlockSpec((rows, tile), lambda i: (0, i))],
        out_shape=[jax.ShapeDtypeStruct((rows, w), BF16), jax.ShapeDtypeStruct((rows, 2 * w), BF16)],
        compiler_params=pltpu.CompilerParams(vmem_limit_bytes=40 << 20),
        cost_estimate=pl.CostEstimate(flops=rows * w * w * 4, bytes_accessed=rows * w * 10, transcendentals=0),
    )(memory, w_qkv, bias[None])


GELU_RATE = 0.7978845608028654
GELU_CUBE = 0.044715


def feed_kernel(x_ref, mixed_ref, cot_ref, w_out_ref, w_in_ref, w_back_ref, rows_ref, in_bias_ref,
                result_ref, normed_ref, act_ref, pre_ref, rgrad_ref, branch_ref, mgrad_ref, wide_ref, sums_ref):
    w = x_ref.shape[1]
    out_bias, back_bias, gain, offset = (rows_ref[i : i + 1] for i in range(4))
    cot = cot_ref[...]
    residual = x_ref[...].astype(F32) + (mm(mixed_ref[...], w_out_ref[...]) + out_bias)
    unit, rate = normalised(residual)
    normed = (unit * gain + offset).astype(BF16)
    normed_ref[...] = normed
    result = residual + back_bias
    ngrad = None
    chunk = 768
    wide = []
    for c in range(0, w_in_ref.shape[1], chunk):
        sl = pl.ds(c, chunk)
        v = mm(normed, w_in_ref[:, sl]) + in_bias_ref[:, sl]
        square = v * v
        t = jnp.tanh(GELU_RATE * v * (1.0 + GELU_CUBE * square))
        half = 0.5 * (1.0 + t)
        act = (v * half).astype(BF16)
        slope = half + (0.5 * GELU_RATE) * v * (1.0 - t * t) * (1.0 + 3.0 * GELU_CUBE * square)
        act_ref[:, sl] = act
        result = result + mm(act, w_back_ref[sl, :])
        pre = (nt(cot, w_back_ref[sl, :]) * slope).astype(BF16)
        pre_ref[:, sl] = pre
        wide.append(col_sums(pre.astype(F32)))
        part = nt(pre, w_in_ref[:, sl])
        ngrad = part if ngrad is None else ngrad + part
    result_ref[...] = result.astype(BF16)
    rgrad = cot.astype(F32) + norm_back(unit, rate, ngrad * gain)
    rgrad_ref[...] = rgrad
    branch = rgrad.astype(BF16)
    branch_ref[...] = branch
    mgrad_ref[...] = nt(branch, w_out_ref[...]).astype(BF16)
    sums = [col_sums(cot.astype(F32)), col_sums(branch.astype(F32)), col_sums(ngrad * unit), col_sums(ngrad)]
    sums = jnp.concatenate(sums + [jnp.zeros((4, w), F32)], 0)
    wide = jnp.concatenate(wide, 1)

    @pl.when(pl.program_id(0) == 0)
    def _():
        sums_ref[...] = sums
        wide_ref[...] = wide

    @pl.when(pl.program_id(0) > 0)
    def _():
        sums_ref[...] += sums
        wide_ref[...] += wide


def feed(x, mixed, cot, w_out, w_in, w_back, rows4, in_bias):
    n, w = x.shape
    ff = w_in.shape[1]
    tile = 256
    rows = lambda c: pl.BlockSpec((tile, c), lambda i: (i, 0))
    arr = lambda c, t: jax.ShapeDtypeStruct((n, c), t)
    return pl.pallas_call(
        feed_kernel,
        grid=(n // tile,),
        in_specs=[rows(w), rows(w), rows(w), whole(w_out.shape), whole(w_in.shape), whole(w_back.shape), whole((4, w)), whole((1, ff))],
        out_specs=[rows(w), rows(w), rows(ff), rows(ff), rows(w), rows(w), rows(w),
                   pl.BlockSpec((1, ff), lambda i: (0, 0)), pl.BlockSpec((8, w), lambda i: (0, 0))],
        out_shape=[arr(w, BF16), arr(w, BF16), arr(ff, BF16), arr(ff, BF16), arr(w, F32), arr(w, BF16), arr(w, BF16),
                   jax.ShapeDtypeStruct((1, ff), F32), jax.ShapeDtypeStruct((8, w), F32)],
        compiler_params=pltpu.CompilerParams(vmem_limit_bytes=56 << 20),
        cost_estimate=pl.CostEstimate(flops=n * (4 * w * ff + 2 * w * w) * 2, bytes_accessed=n * ff * 4 + 2 * w * ff * 4, transcendentals=n * ff),
    )(x, mixed, cot, w_out, w_in, w_back, rows4, in_bias[None])


def local_kernel(g_ref, w_ref, out_ref):
    part = nt(g_ref[0], w_ref[...])

    @pl.when(pl.program_id(0) == 0)
    def _():
        out_ref[...] = part

    @pl.when(pl.program_id(0) == 1)
    def _():
        out_ref[...] += part


def local_memory_grad(memory_proj, w_qkv):
    _, rows, w = memory_proj.shape
    return pl.pallas_call(
        local_kernel,
        grid=(2,),
        in_specs=[pl.BlockSpec((1, rows, w), lambda i: (i, 0, 0)), pl.BlockSpec((w, w), lambda i: (0, 1 + i))],
        out_specs=pl.BlockSpec((rows, w), lambda i: (0, 0)),
        out_shape=jax.ShapeDtypeStruct((rows, w), F32),
        compiler_params=pltpu.CompilerParams(vmem_limit_bytes=40 << 20),
        cost_estimate=pl.CostEstimate(flops=rows * w * w * 4, bytes_accessed=rows * w * 10, transcendentals=0),
    )(memory_proj, w_qkv)


def entry_kernel(x_ref, rgrad_ref, proj_ref, data_ref, inc_ref, w_ref, gain_ref, out_ref, sums_ref):
    w = x_ref.shape[2]
    hgrad = dot_hi(data_ref[0], inc_ref[0], 0, 0)
    for p in range(3):
        hgrad = hgrad + nt(proj_ref[p, 0], w_ref[:, pl.ds(p * w, w)])
    unit, rate = normalised(x_ref[0].astype(F32))
    out_ref[0] = (rgrad_ref[0] + norm_back(unit, rate, hgrad * gain_ref[...])).astype(BF16)
    sums = jnp.concatenate([col_sums(hgrad * unit), col_sums(hgrad), jnp.zeros((6, w), F32)], 0)
    start = (pl.program_id(0) == 0) & (pl.program_id(1) == 0)

    @pl.when(start)
    def _():
        sums_ref[...] = sums

    @pl.when(jnp.logical_not(start))
    def _():
        sums_ref[...] += sums


def entry_grads(x, rgrad, token_proj, data_map, incoming, w_qkv, gain):
    docs, _, w = x.shape
    tile = 256
    rows = pl.BlockSpec((1, tile, w), lambda d, i: (d, i, 0))
    return pl.pallas_call(
        entry_kernel,
        grid=(docs, L // tile),
        in_specs=[rows, rows, pl.BlockSpec((3, 1, tile, w), lambda d, i: (0, d, i, 0)),
                  pl.BlockSpec((1, NB, tile), lambda d, i: (d, 0, i)), pl.BlockSpec((1, NB, w), lambda d, i: (d, 0, 0)),
                  whole(w_qkv.shape), whole((1, w))],
        out_specs=[rows, pl.BlockSpec((8, w), lambda d, i: (0, 0))],
        out_shape=[jax.ShapeDtypeStruct((docs, L, w), BF16), jax.ShapeDtypeStruct((8, w), F32)],
        compiler_params=pltpu.CompilerParams(vmem_limit_bytes=40 << 20),
        cost_estimate=pl.CostEstimate(flops=docs * L * w * w * 6 + docs * L * NB * w * 12, bytes_accessed=docs * L * w * 14, transcendentals=0),
    )(x, rgrad, token_proj, data_map, incoming, w_qkv, gain[None])


MESH = pl.DeviceIdType.MESH
GROUPS = 3
STAGES = 5


class Part:
    def __init__(self, me, held, out, rows, cols, seg_first, got, sems):
        self.me, self.held, self.out, self.got, self.sems = me, held, out, got, sems
        self.rows, self.cols, self.seg_first = rows, cols, seg_first
        self.stage = 0
        self.copy = None

    def span(self, which):
        first, count = self.rows
        return pl.ds(pl.multiple_of(first + which * (count // 2), 8), count // 2)

    def view(self):
        me, held, cols = self.me, self.held, pl.ds(*self.cols)
        own = self.span(me["seg"])
        if self.stage == 0 and self.seg_first:
            return held.at[:, :, :, self.span(1 - me["seg"]), cols], lambda i: held.at[i // 4, i // 2 % 2, i % 2, own, cols], 8, "seg"
        if self.stage == 0:
            every = pl.ds(*self.rows)
            return held.at[:, :, 1 - me["x"], every, cols], lambda i: held.at[i // 2, i % 2, me["x"], every, cols], 4, "x"
        if self.stage == 1 and self.seg_first:
            return held.at[:, :, 1 - me["x"], own, cols], lambda i: held.at[i // 2, i % 2, me["x"], own, cols], 4, "x"
        if self.stage == 1:
            return held.at[:, :, me["x"], self.span(1 - me["seg"]), cols], lambda i: held.at[i // 2, i % 2, me["x"], own, cols], 4, "seg"
        if self.stage == 2:
            return held.at[:, 1 - me["z0"], me["x"], own, cols], lambda i: held.at[i, me["z0"], me["x"], own, cols], 2, "z0"
        if self.stage == 3:
            return held.at[1 - me["z1"], me["z0"], me["x"], own, cols], lambda i: held.at[me["z1"], me["z0"], me["x"], own, cols], 1, "z1"
        return held.at[me["z1"], me["z0"], me["x"], own, cols], None, 0, "seg"

    def send(self):
        source, _, _, to = self.view()
        target = self.out.at[self.span(self.me["seg"]), pl.ds(*self.cols)] if self.stage == 4 else self.got[self.stage]
        send, recv, local = self.sems
        self.copy = pltpu.make_async_remote_copy(
            src_ref=source, dst_ref=target, send_sem=send.at[self.stage], recv_sem=recv.at[self.stage],
            device_id=self.me["ids"][to], device_id_type=MESH)
        self.copy.start()
        if self.stage == 4:
            self.own = pltpu.make_async_copy(source, target, local)
            self.own.start()

    def advance(self):
        self.copy.wait()
        if self.stage == 4:
            self.own.wait()
            return
        _, into, count, _ = self.view()
        got = self.got[self.stage]
        lead = got.shape[:-2]

        def add(i, _):
            ref = into(i)
            where = {0: (), 1: (i,), 2: (i // 2, i % 2), 3: (i // 4, i // 2 % 2, i % 2)}[len(lead)]
            ref[...] += got[where]
            return 0

        lax.fori_loop(0, count, add, 0)
        self.stage += 1
        self.send()


def tail_kernel(docs, bits, *refs):
    (act, cot, normed, pre, qkv, mem, mgrad, mixed, lse, hidden, mem_rows, mixed_rows, branch, w_qkv, x, rgrad,
     data_map, carry_map, flags, gain, small_in) = refs[:21]
    o_back, o_in, o_three, o_input, o_start, small, tok, memp, s1, s2, s3 = refs[21:32]
    h1, h2, h3, rc1, rc2, acc1, acc2, acc3, lg, inc, rsmall = refs[32:43]
    gots = refs[43:43 + GROUPS * 2 * 4]
    send, recv, local, csend, crecv, misc_send, misc_recv, ssend, srecv, credit = refs[43 + GROUPS * 2 * 4:]
    b, s = lax.axis_index("batch"), lax.axis_index("seg")
    n, w = cot.shape
    ff = act.shape[1]

    def flip(distance):
        return b + distance * (1 - 2 * ((b // distance) % 2))

    ids = {"core": (flip(1), s), "x": (flip(2), s), "z0": (flip(4), s), "z1": (flip(8), s), "seg": (b, 1 - s)}
    me = {"core": b % 2, "x": (b // 2) % 2, "z0": (b // 4) % 2, "z1": (b // 8) % 2, "seg": s, "ids": ids}
    mine = me["core"]

    @pl.when(s == 1)
    def _():
        inc[...] = jnp.zeros_like(inc)

    small[...] = small_in[...]
    barrier = pltpu.get_barrier_semaphore()
    for who in ids.values():
        pl.semaphore_signal(barrier, inc=1, device_id=who, device_id_type=MESH)
    pl.semaphore_wait(barrier, len(ids))

    def between_cores(g, source, target):
        copy = pltpu.make_async_remote_copy(
            src_ref=source, dst_ref=target, send_sem=csend.at[g], recv_sem=crecv.at[g], device_id=ids["core"], device_id_type=MESH)
        copy.start()
        return copy

    def add_core(copy, held, got):
        copy.wait()

        def add(i, _):
            held[i // 4, i // 2 % 2, i % 2] += got[i]
            return 0

        lax.fori_loop(0, 8, add, 0)

    def parts(g, held, out):
        _, _, _, rows, cols = held.shape
        if g == 0:
            where = [((0, rows // 2), (0, cols)), ((rows // 2, rows // 2), (0, cols))]
        else:
            where = [((0, rows), (0, cols // 2)), ((0, rows), (cols // 2, cols // 2))]
        both = []
        for h in range(2):
            sems = (send.at[g, h], recv.at[g, h], local.at[g, h])
            both.append(Part(me, held, out, *where[h], h == 1, gots[(g * 2 + h) * 4 : (g * 2 + h) * 4 + 4], sems))
        return both

    p1, p2, p3 = parts(0, h1, o_back), parts(1, h2, o_in), parts(2, h3, o_three)

    own1 = ff // 16

    def back_body(act_ref, cot_ref, send_ref):
        i = pl.program_id(0)
        acc1[...] = tn(act_ref[...], cot_ref[...])
        h1[i // 4, i // 2 % 2, i % 2] = acc1[pl.ds(pl.multiple_of(mine * own1, 8), own1)]
        send_ref[0] = acc1[pl.ds(pl.multiple_of((1 - mine) * own1, 8), own1)]

    pltpu.emit_pipeline(
        back_body, grid=(8,),
        in_specs=[pl.BlockSpec((n, 2 * own1), lambda i: (0, i)), pl.BlockSpec((n, w), lambda i: (0, 0))],
        out_specs=[pl.BlockSpec((1, own1, w), lambda i: (i, 0, 0))],
    )(act, cot, s1)
    core1 = between_cores(0, s1, rc1)

    own2 = w // 16
    tile2 = acc2.shape[1]

    def scatter_rows(acc, held, cols, send_ref):
        for i in range(8):
            held[i // 4, i // 2 % 2, i % 2, :, cols] = acc[pl.ds(pl.multiple_of((2 * i + mine) * own2, 8), own2)]
            send_ref[i] = acc[pl.ds(pl.multiple_of((2 * i + 1 - mine) * own2, 8), own2)]

    def in_body(normed_ref, pre_ref, send_ref):
        acc2[...] = tn(normed_ref[...], pre_ref[...])
        scatter_rows(acc2, h2, pl.ds(pl.multiple_of(pl.program_id(0) * tile2, 128), tile2), send_ref)

    pltpu.emit_pipeline(
        in_body, grid=(ff // tile2,),
        in_specs=[pl.BlockSpec((n, w), lambda i: (0, 0)), pl.BlockSpec((n, tile2), lambda i: (0, i))],
        out_specs=[pl.BlockSpec((8, own2, tile2), lambda i: (0, 0, i))],
    )(normed, pre, s2)
    core2 = between_cores(1, s2, rc2)
    add_core(core1, h1, rc1)
    for p in p1:
        p.send()

    pairs = w // 128

    def attention(doc):
        def body(*r):
            cols = pl.ds(pl.multiple_of(pl.program_id(0) * 128, 128), 128)
            qs, vs = grads_core(*r)
            small[0:1, cols] += qs
            small[1:2, cols] += vs

        t = lambda o: pl.BlockSpec((1, L, 128), lambda i: (doc, 0, o * pairs + i))
        m = lambda o: pl.BlockSpec((1, NB, 128), lambda i: (doc, 0, o * pairs + i))
        pltpu.emit_pipeline(
            body, grid=(pairs,),
            in_specs=[t(0), t(1), t(2), m(0), m(1), t(0), t(0), pl.BlockSpec((1, 1, 2, L), lambda i: (doc, i, 0, 0))],
            out_specs=[pl.BlockSpec((3, 1, L, 128), lambda i: (0, doc, 0, i)), pl.BlockSpec((2, 1, NB, 128), lambda i: (0, doc, 0, i))],
        )(qkv, qkv, qkv, mem, mem, mgrad, mixed, lse, tok, memp)

    attention(0)
    add_core(core2, h2, rc2)
    pl.semaphore_signal(credit, inc=1, device_id=ids["core"], device_id_type=MESH)
    for p in p2:
        p.send()
    for doc in range(1, docs):
        attention(doc)

    def local_body(g_ref, w_ref):
        total = None
        for d in range(docs):
            part = nt(g_ref[0, d], w_ref[...])
            rows = pl.ds(d * NB, NB)

            @pl.when(pl.program_id(0) == 0)
            def _():
                lg[rows] = part

            @pl.when(pl.program_id(0) == 1)
            def _():
                lg[rows] += part

    pltpu.emit_pipeline(
        local_body, grid=(2,),
        in_specs=[pl.BlockSpec((1, docs, NB, w), lambda i: (i, 0, 0, 0)), pl.BlockSpec((w, w), lambda i: (0, 1 + i))],
        out_specs=[],
    )(memp, w_qkv)
    upward = pltpu.make_async_remote_copy(
        src_ref=lg, dst_ref=inc, send_sem=misc_send.at[0], recv_sem=misc_recv.at[0], device_id=ids["seg"], device_id_type=MESH)

    @pl.when(s == 1)
    def _():
        upward.start()

    for p in p1:
        p.advance()

    tile3 = acc3.shape[1]
    per = w // tile3
    m = mem_rows.shape[0]

    def three_body(hidden_ref, mem_ref, mixed_ref, tok_ref, memg_ref, branch_ref, send_ref):
        part = pl.program_id(0)

        @pl.when(part == 0)
        def _():
            acc3[...] = sum(tn(hidden_ref[d], tok_ref[0, d]) for d in range(docs))

        @pl.when((part == 1) | (part == 2))
        def _():
            acc3[...] = sum(tn(hidden_ref[d], tok_ref[0, d]) + tn(mem_ref[d], memg_ref[0, d]) for d in range(docs))

        @pl.when(part == 3)
        def _():
            acc3[...] = tn(mixed_ref[...], branch_ref[...])

        cols = pl.ds(pl.multiple_of((part * per + pl.program_id(1)) * tile3, 128), tile3)
        scatter_rows(acc3, h3, cols, send_ref)

    pltpu.emit_pipeline(
        three_body, grid=(4, per),
        in_specs=[pl.BlockSpec((docs, L, w), lambda p, i: (0, 0, 0)), pl.BlockSpec((docs, NB, w), lambda p, i: (0, 0, 0)),
                  pl.BlockSpec((n, w), lambda p, i: (0, 0)),
                  pl.BlockSpec((1, docs, L, tile3), lambda p, i: (jnp.minimum(p, 2), 0, 0, jnp.where(p < 3, i, per - 1))),
                  pl.BlockSpec((1, docs, NB, tile3), lambda p, i: (jnp.clip(p - 1, 0, 1), 0, 0, jnp.where(p < 1, 0, jnp.where(p < 3, i, per - 1)))),
                  pl.BlockSpec((n, tile3), lambda p, i: (0, jnp.where(p < 3, 0, i)))],
        out_specs=[pl.BlockSpec((8, own2, tile3), lambda p, i: (0, 0, p * per + i))],
    )(hidden, mem_rows, mixed_rows, tok, memp, branch, s3)
    pl.semaphore_wait(credit, 1)
    core3 = between_cores(2, s3, rc2)
    for p in p2 + p1:
        p.advance()
    add_core(core3, h3, rc2)
    for p in p3:
        p.send()

    @pl.when(s == 0)
    def _():
        upward.wait_recv()

    tile4 = 256

    def entry_body(x_ref, rgrad_ref, proj_ref, data_ref, w_ref, gain_ref, out_ref):
        d = pl.program_id(0)
        hgrad = dot_hi(data_ref[0], inc[pl.ds(pl.multiple_of(d * NB, NB), NB)], 0, 0)
        for p in range(3):
            hgrad = hgrad + nt(proj_ref[p, 0], w_ref[:, pl.ds(p * w, w)])
        unit, rate = normalised(x_ref[0].astype(F32))
        out_ref[0] = (rgrad_ref[0] + norm_back(unit, rate, hgrad * gain_ref[...])).astype(BF16)
        small[4:5] += col_sums(hgrad * unit)
        small[5:6] += col_sums(hgrad)

    rows4 = pl.BlockSpec((1, tile4, w), lambda d, i: (d, i, 0))
    pltpu.emit_pipeline(
        entry_body, grid=(docs, L // tile4),
        in_specs=[rows4, rows4, pl.BlockSpec((3, 1, tile4, w), lambda d, i: (0, d, i, 0)),
                  pl.BlockSpec((1, NB, tile4), lambda d, i: (d, 0, i)), pl.BlockSpec((w, 3 * w), lambda d, i: (0, 0)),
                  pl.BlockSpec((1, w), lambda d, i: (0, 0))],
        out_specs=[rows4],
    )(x, rgrad, tok, data_map, w_qkv, gain, o_input)

    def add_small(k, to):
        copy = pltpu.make_async_remote_copy(
            src_ref=small, dst_ref=rsmall.at[k], send_sem=ssend.at[k], recv_sem=srecv.at[k], device_id=ids[to], device_id_type=MESH)
        copy.start()
        return copy

    def took_small(k, copy):
        copy.wait()
        small[...] += rsmall[k]

    tiny = add_small(0, "core")

    @pl.when(s == 1)
    def _():
        upward.wait_send()

    def start_body(carry_ref, flag_ref):
        rows = pl.ds(pl.multiple_of(pl.program_id(0) * NB, NB), NB)
        lg[rows] = flag_ref[0] * (lg[rows] + dot_hi(carry_ref[0], inc[rows], 0, 0))

    pltpu.emit_pipeline(
        start_body, grid=(docs,),
        in_specs=[pl.BlockSpec((1, NB, NB), lambda d: (d, 0, 0)), pl.BlockSpec((1, 1, w), lambda d: (d, 0, 0))],
        out_specs=[],
    )(carry_map, flags)
    half = w // 2
    stay = pltpu.make_async_copy(lg.at[:, pl.ds(0, half)], o_start, misc_send.at[1])
    leave = pltpu.make_async_remote_copy(
        src_ref=lg.at[:, pl.ds(half, half)], dst_ref=o_start, send_sem=misc_send.at[2], recv_sem=misc_recv.at[1],
        device_id=ids["seg"], device_id_type=MESH)

    @pl.when(s == 0)
    def _():
        stay.start()
        leave.start()

    took_small(0, tiny)
    tiny = add_small(1, "x")
    for p in p1 + p2:
        p.advance()
    took_small(1, tiny)
    tiny = add_small(2, "seg")
    for p in p1 + p2:
        p.advance()
    took_small(2, tiny)
    tiny = add_small(3, "z0")
    for p in p3:
        p.advance()
    for p in p2:
        p.advance()
    took_small(3, tiny)
    tiny = add_small(4, "z1")
    for p in p3:
        p.advance()
    for p in p3:
        p.advance()
    took_small(4, tiny)
    for p in p3:
        p.advance()
    for p in p1 + p2 + p3:
        p.advance()

    @pl.when(s == 0)
    def _():
        stay.wait()
        leave.wait_send()

    @pl.when(s == 1)
    def _():
        leave.wait_recv()


def tail(docs, batch, act, cot, normed, pre, qkv, mem, mgrad, mixed, lse, hidden, mem_rows, branch, w_qkv, x, rgrad,
         data_map, carry_map, flags, gain, small):
    n, w = cot.shape
    ff = act.shape[1]
    own1, own2 = ff // batch, w // batch
    ops = [act, cot, normed, pre, qkv, mem, mgrad, mixed, lse, hidden, mem_rows, mixed.reshape(n, w), branch, w_qkv, x, rgrad,
           data_map, carry_map, flags, gain, small]
    anywhere = pl.BlockSpec(memory_space=pl.ANY)
    vmem = pl.BlockSpec(memory_space=pltpu.VMEM)
    f = lambda *shape: jax.ShapeDtypeStruct(shape, F32)
    outs = [f(own1, w), f(own2, ff), f(own2, 4 * w), jax.ShapeDtypeStruct((docs, L, w), BF16), f(docs * NB, w // 2), f(16, w),
            jax.ShapeDtypeStruct((3, docs, L, w), BF16), jax.ShapeDtypeStruct((2, docs, NB, w), BF16),
            f(8, own1, w), f(8, own2, ff), f(8, own2, 4 * w)]
    held = [pltpu.VMEM((2, 2, 2, own1, w), F32), pltpu.VMEM((2, 2, 2, own2, ff), F32), pltpu.VMEM((2, 2, 2, own2, 4 * w), F32)]
    rcs = [pltpu.VMEM((8, own1, w), F32), pltpu.VMEM((8, own2, ff), F32)]
    accs = [pltpu.VMEM((2 * own1, w), F32), pltpu.VMEM((w, 512), F32), pltpu.VMEM((w, 384), F32)]
    rest = [pltpu.VMEM((docs * NB, w), F32), pltpu.VMEM((docs * NB, w), F32), pltpu.VMEM((5, 16, w), F32)]
    gots = []
    for g in range(GROUPS):
        rows, cols = (own1 // 2, w) if g == 0 else (own2, ff // 2)
        for h in range(2):
            gots.append(pltpu.VMEM((2, 2, rows, cols) if h == 0 else (2, 2, 2, rows // 2, cols), F32))
            gots.append(pltpu.VMEM((2, 2, rows // 2, cols), F32))
            gots.append(pltpu.VMEM((2, rows // 2, cols), F32))
            gots.append(pltpu.VMEM((rows // 2, cols), F32))
    dma = pltpu.SemaphoreType.DMA
    sems = [dma((GROUPS, 2, STAGES)), dma((GROUPS, 2, STAGES)), dma((GROUPS, 2)), dma((GROUPS,)), dma((GROUPS,)),
            dma((3,)), dma((2,)), dma((5,)), dma((5,)), pltpu.SemaphoreType.REGULAR]
    return pl.pallas_call(
        functools.partial(tail_kernel, docs, 4),
        in_specs=[anywhere] * 20 + [vmem],
        out_specs=[anywhere] * 5 + [vmem] + [anywhere] * 5,
        out_shape=outs,
        scratch_shapes=held + rcs + accs + rest + gots + sems,
        compiler_params=pltpu.CompilerParams(vmem_limit_bytes=60 << 20, collective_id=0, has_side_effects=True),
        cost_estimate=pl.CostEstimate(flops=10**11, bytes_accessed=10**8, transcendentals=10**7),
    )(*ops)[:6]


def outer(a, b):
    return lax.dot_general(a, b, (((0,), (0,)), ((), ())), preferred_element_type=F32)


def passed(block, distance):
    n = lax.axis_size("seg")
    return lax.ppermute(block, "seg", [(i - distance, i) for i in range(n) if 0 <= i - distance < n])


def swap(block, axis, distance):
    n = lax.axis_size(axis)
    return lax.ppermute(block, axis, [(i, i ^ distance) for i in range(n)])


def halve(block, axis, distance, dim):
    bit = (lax.axis_index(axis) // distance) % 2
    send = lax.dynamic_index_in_dim(block, 1 - bit, dim, keepdims=False)
    keep = lax.dynamic_index_in_dim(block, bit, dim, keepdims=False)
    return keep + swap(send, axis, distance)


def spread(work, seg_place, first):
    n, s = lax.axis_size("batch"), lax.axis_size("seg")
    bits = n.bit_length() - 1
    _, own, cols = work.shape
    split = s if seg_place < bits and own % s == 0 else 1
    work = work.reshape((2,) * (bits - first) + (split, own // split, cols))
    for k in range(first, bits + 1):
        if k == seg_place:
            if split == 1:
                d = 1
                while d < s:
                    work = work + swap(work, "seg", d)
                    d *= 2
            else:
                left = bits - k
                work = work.reshape((2,) * left + (2,) * (s.bit_length() - 1) + (own // split, cols))
                d = 1
                while d < s:
                    work = halve(work, "seg", d, work.ndim - 3)
                    d *= 2
        if k < bits:
            work = halve(work, "batch", 1 << k, bits - 1 - k)
    if split > 1:
        d = s // 2
        while d >= 1:
            bit = (lax.axis_index("seg") // d) % 2
            other = swap(work, "seg", d)
            work = jnp.where(bit == 0, jnp.concatenate([work, other], 0), jnp.concatenate([other, work], 0))
            d //= 2
    return work.reshape(own, cols)


def spread_out(x, act, cot, normed, pre, qkv, mem, mgrad, mixed, lse, hidden, mem_rows, branch, w_qkv, rgrad, data_map, carry_map, has_memory, gain, small):
    docs, _, width = x.shape
    n = docs * L
    batch, chain = lax.axis_size("batch"), lax.axis_size("seg")
    is_first = lax.axis_index("seg") == 0
    flags = has_memory.astype(F32)[:, None, None]
    grad_back = spread(outer(act, cot).reshape(batch, -1, width), 2, 0)
    grad_in = spread(outer(normed, pre).reshape(batch, width // batch, -1), 1, 0)
    token_proj, memory_proj, attn_sums = attend_grads(qkv, mem, mgrad, mixed, lse)
    memory_proj = memory_proj.reshape(2, docs * NB, width)
    local_grad = local_memory_grad(memory_proj, w_qkv).reshape(docs, NB, width)
    carry_back = carry_map.swapaxes(1, 2)
    incoming = jnp.zeros_like(local_grad)
    for i in range(chain - 1):
        sent = local_grad if i == 0 else jnp.matmul(carry_back, incoming, precision=HI) + local_grad
        incoming = passed(sent, -1)
    hidden_rows = hidden.reshape(n, width)
    three = [outer(hidden_rows, token_proj[i].reshape(n, width)) for i in range(3)]
    three = [three[0]] + [three[i + 1] + outer(mem_rows, memory_proj[i]) for i in range(2)]
    three = jnp.concatenate(three + [outer(mixed.reshape(n, width), branch)], 1)
    grad_three = spread(three.reshape(batch, width // batch, -1), 2, 0)
    input_grad, entry_sums = entry_grads(
        x, rgrad, token_proj, data_map, incoming, w_qkv, gain
    )
    start_grad = jnp.where(is_first, flags * (local_grad + jnp.matmul(carry_back, incoming, precision=HI)), 0.0)
    own = width // chain
    start_share = start_grad[:, :, :own]
    for i in range(1, chain):
        start_share = start_share + lax.ppermute(start_grad[:, :, i * own : (i + 1) * own], "seg", [(0, i)])

    wide = small[8:12].reshape(-1)
    packed = jnp.concatenate(
        [g.reshape(batch, 1, -1)
         for g in (jnp.sum(attn_sums[:, 0], 0), jnp.sum(attn_sums[:, 1], 0), small[2], small[3], entry_sums[0], entry_sums[1],
                   small[6], small[7], wide)], 2)
    packed = spread(packed, batch.bit_length() - 1, 0)[0]
    own = width // batch
    vectors = [packed[i * own : (i + 1) * own] for i in range(8)] + [packed[8 * own :]]
    return input_grad, start_share, grad_back, grad_in, grad_three, vectors


def reduced(x, act, cot, normed, pre, qkv, mem, mgrad, mixed, lse, hidden, mem_rows, branch, w_qkv, rgrad, data_map, carry_map, has_memory, gain, small):
    docs, _, width = x.shape
    batch = lax.axis_size("batch")
    flags = jnp.broadcast_to(has_memory.astype(F32)[:, None, None], (docs, 1, width))
    grad_back, grad_in, grad_three, input_grad, start_share, small = tail(
        docs, batch, act, cot, normed, pre, qkv, mem, mgrad, mixed, lse, hidden, mem_rows.reshape(docs, NB, width), branch,
        w_qkv, x, rgrad, data_map, carry_map, flags, gain[None], small
    )
    own = width // batch
    b = lax.axis_index("batch")
    mine = lax.dynamic_slice_in_dim(small[:8], b * own, own, 1)
    wide = lax.dynamic_slice_in_dim(small[8:12].reshape(-1), b * 4 * own, 4 * own, 0)
    vectors = [mine[i] for i in range(8)] + [wide]
    return input_grad, start_share.reshape(docs, NB, width // 2), grad_back, grad_in, grad_three, vectors


def shards(
    tokens,
    start_memory,
    has_memory,
    sticky,
    w_qkv,
    w_out,
    w_in,
    w_back,
    q_bias,
    v_bias,
    out_bias,
    in_bias,
    back_bias,
    ln1_gain,
    ln1_bias,
    ln2_gain,
    ln2_bias,
    cotangent,
):
    width = w_qkv.shape[0]
    docs = tokens.shape[0]
    n = docs * L
    chain = lax.axis_size("seg")
    batch = lax.axis_size("batch")
    is_first = lax.axis_index("seg") == 0
    flags = has_memory.astype(F32)[:, None, None]

    parts = [start_memory] + [lax.ppermute(start_memory, "seg", [(i, 0)]) for i in range(1, chain)]
    own_start = jnp.where(is_first, flags * jnp.concatenate(parts, 2), 0.0)

    x = tokens[:, 0]
    cot = cotangent[:, 0].reshape(n, width)
    carry_map, data_map = memory_maps(sticky[:, 0])
    bias = jnp.concatenate([q_bias, jnp.zeros_like(q_bias), v_bias])
    hidden, qkv = project(x, w_qkv, bias, ln1_gain, ln1_bias)

    memory = own_start
    for i in range(chain - 1):
        memory = passed(renew(carry_map, data_map, memory, hidden), 1) + own_start

    mem_rows, mem = recall(memory.reshape(docs * NB, width), w_qkv, bias)
    mem = mem.reshape(docs, NB, 2 * width)
    mixed, log_total = attend(qkv, mem)
    rows4 = jnp.stack([out_bias, back_bias, ln2_gain, ln2_bias])
    result, normed, act, pre, residual_grad, branch, mixed_grad, wide, sums = feed(
        x.reshape(n, width), mixed.reshape(n, width), cot, w_out, w_in, w_back, rows4, in_bias
    )
    small = [sums[1:2], sums[0:1], jnp.zeros((2, width), F32), sums[2:4], wide.reshape(4, width)]
    small = jnp.concatenate([jnp.zeros((2, width), F32)] + small + [jnp.zeros((4, width), F32)], 0)
    grads = reduced if (batch, chain) == (16, 2) else spread_out
    input_grad, start_share, grad_back, grad_in, grad_three, vectors = grads(
        x, act, cot, normed, pre, qkv, mem, mixed_grad.reshape(docs, L, width), mixed, log_total, hidden, mem_rows,
        branch, w_qkv, residual_grad.reshape(docs, L, width), data_map, carry_map, has_memory, ln1_gain, small
    )
    return (
        result.reshape(docs, 1, L, width),
        input_grad.reshape(docs, 1, L, width),
        start_share,
        grad_three[:, : 3 * width],
        grad_three[:, 3 * width :],
        grad_in,
        grad_back,
    ) + tuple(vectors[i] for i in (0, 1, 2, 8, 3, 4, 5, 6, 7))


def solution(mesh):
    rows = P("batch", "seg", None, None)
    in_specs = (rows, P("batch", None, "seg"), P("batch"), P("batch", "seg", None)) + (P(),) * 13 + (rows,)
    out_specs = (rows, rows, P("batch", None, "seg")) + (P("batch", None),) * 4 + (P("batch"),) * 9
    return jax.shard_map(shards, mesh=mesh, in_specs=in_specs, out_specs=out_specs, check_vma=False)
```

```python
import functools

import jax
import jax.numpy as jnp
from jax import lax
from jax.experimental import pallas as pl
from jax.experimental.pallas import tpu as pltpu
from jax.sharding import PartitionSpec as P

HEADS = 12
HD = 64
NB = 256
L = 512
STICKY = 512
GRID = 4096

EPSILON = 1e-05
RIDGE = 0.5
HI = lax.Precision.HIGHEST
F32 = jnp.float32
BF16 = jnp.bfloat16
EXP2_SCALE = HD**-0.5 * 1.4426950408889634
LEAF = 32
PIVOTS = 4


def dot_hi(a, b, ca, cb):
    return lax.dot_general(a, b, (((ca,), (cb,)), ((), ())), precision=HI, preferred_element_type=F32)

def bumps(times):
    centers = (lax.broadcasted_iota(jnp.int32, (NB, 1), 0).astype(F32) + 0.5) / NB
    scaled = (times - centers) * NB
    return jnp.exp(-0.5 * scaled * scaled)

def small_inverse(s):
    p = len(s)
    s = [list(r) for r in s]
    for k in range(p):
        inv = 1.0 / s[k][k]
        row = [inv if j == k else s[k][j] * inv for j in range(p)]
        for i in range(p):
            if i != k:
                f = s[i][k]
                s[i] = [-f * row[j] if j == k else s[i][j] - f * row[j] for j in range(p)]
        s[k] = row
    return s


def leaf_inverse(d):
    n = d.shape[0]
    rows = lax.broadcasted_iota(jnp.int32, (n, n), 0)
    lanes = lax.broadcasted_iota(jnp.int32, (1, n), 1)
    for k in range(0, n, PIVOTS):
        cols = [jnp.broadcast_to(d[:, k + j : k + j + 1], (n, n)) for j in range(PIVOTS)]
        inv = small_inverse([[cols[j][k + i : k + i + 1] for j in range(PIVOTS)] for i in range(PIVOTS)])
        old = [d[k + j : k + j + 1] for j in range(PIVOTS)]
        inside = (lanes >= k) & (lanes < k + PIVOTS)
        fresh = []
        for i in range(PIVOTS):
            r = inv[i][0] * old[0]
            for j in range(1, PIVOTS):
                r = r + inv[i][j] * old[j]
            for j in range(PIVOTS):
                r = jnp.where(lanes == k + j, inv[i][j], r)
            fresh.append(r)
        out = jnp.where(inside, 0.0, d)
        for i in range(PIVOTS):
            out = out - cols[i] * fresh[i]
        for i in range(PIVOTS):
            out = jnp.where(rows == k + i, fresh[i], out)
        d = out
    return d


def maps_kernel(docs, sticky_ref, carry_ref, data_ref, a_ref):
    new_times = 0.5 + 0.5 * (lax.broadcasted_iota(jnp.int32, (1, L), 1).astype(F32) + 0.5) / L
    fresh = bumps(new_times)
    eye = (lax.broadcasted_iota(jnp.int32, (NB, NB), 0) == lax.broadcasted_iota(jnp.int32, (NB, NB), 1)).astype(F32)
    base = dot_hi(fresh, fresh, 1, 1) + RIDGE * eye
    for d in range(docs):
        old = (sticky_ref[pl.ds(d, 1), :].astype(F32) + 0.5) / GRID
        f1 = bumps(0.5 * old)
        a_ref[d] = base + dot_hi(f1, f1, 1, 1)
        carry_ref[d] = dot_hi(f1, bumps(old), 1, 1)
    lanes = lax.broadcasted_iota(jnp.int32, (1, NB), 1) // LEAF
    for j in range(NB // LEAF):
        sl = pl.ds(j * LEAF, LEAF)
        leaves = [leaf_inverse(a_ref[d, sl, sl]) for d in range(docs)]
        for d in range(docs):
            p = leaves[d]
            mine = lanes == j
            row = dot_hi(p, a_ref[d, sl, :], 1, 0)
            wide = jnp.concatenate([p] * (NB // LEAF), 1)
            row = jnp.where(mine, wide, row)
            col = a_ref[d, :, sl]
            rest = jnp.where(mine, 0.0, a_ref[d])
            a_ref[d] = rest - dot_hi(col, row, 1, 0)
            a_ref[d, sl, :] = row
    for d in range(docs):
        x = a_ref[d]
        carry_ref[d] = dot_hi(x, carry_ref[d], 1, 0)
        data_ref[d] = dot_hi(x, fresh, 1, 0)

def memory_maps(sticky):
    docs = sticky.shape[0]
    return pl.pallas_call(functools.partial(maps_kernel, docs),
        out_shape=[jax.ShapeDtypeStruct((docs, NB, NB), F32), jax.ShapeDtypeStruct((docs, NB, L), F32)],
        scratch_shapes=[pltpu.VMEM((docs, NB, NB), F32)],
        compiler_params=pltpu.CompilerParams(vmem_limit_bytes=32 << 20),
        cost_estimate=pl.CostEstimate(flops=docs * 10**10, bytes_accessed=docs * 10**6, transcendentals=0),
    )(sticky)


def nt(a, b):
    return lax.dot_general(a, b, (((1,), (1,)), ((), ())), preferred_element_type=F32)

def tn(a, b):
    return lax.dot_general(a, b, (((0,), (0,)), ((), ())), preferred_element_type=F32)

def nn(a, b):
    return jnp.dot(a, b, preferred_element_type=F32)

def head_lanes(h):
    return lax.broadcasted_iota(jnp.int32, (1, 2 * HD), 1) // HD == h

def causal():
    half = L // 2
    return lax.broadcasted_iota(jnp.int32, (half, half), 0) <= lax.broadcasted_iota(jnp.int32, (half, half), 1)

def attend_core(q_ref, k_ref, v_ref, mk_ref, mv_ref, out_ref, peak_ref):
    half = L // 2
    q = q_ref[...]; k = k_ref[...]; v = v_ref[...]; mk = mk_ref[...]; mv = mv_ref[...]
    seen = causal()
    outs = []
    for h in range(2):
        qh = jnp.where(head_lanes(h), q, jnp.zeros_like(q))
        s00 = jnp.where(seen, nt(k[:half], qh[:half]), -1e30)
        s01 = nt(k[:half], qh[half:])
        s11 = jnp.where(seen, nt(k[half:], qh[half:]), -1e30)
        sm = nt(mk, qh)
        sides = []
        for side, parts in enumerate(([s00, sm[:, :half]], [s01, s11, sm[:, half:]])):
            peak = functools.reduce(jnp.maximum, [jnp.max(p, 0, keepdims=True) for p in parts])
            ps = [jnp.exp2((p - peak) * EXP2_SCALE) for p in parts]
            total = functools.reduce(jnp.add, [jnp.sum(p, 0, keepdims=True) for p in ps])
            vs = [v[:half], mv] if side == 0 else [v[:half], v[half:], mv]
            o = functools.reduce(jnp.add, [tn(a, p.astype(BF16)) for a, p in zip(vs, ps)])
            sides.append(o * (1.0 / total))
            peak_ref[h, pl.ds(side * half, half)] = (peak * EXP2_SCALE + jnp.log2(total))[0]
        outs.append(jnp.concatenate(sides, 1))
    lanes = lax.broadcasted_iota(jnp.int32, (2 * HD, 1), 0) // HD == 0
    out_ref[...] = jnp.where(lanes, outs[0], outs[1]).T.astype(BF16)


def attend_tokens(q_ref, k_ref, v_ref, out_ref, peak_ref, total_ref):
    half = L // 2
    q = q_ref[...]
    k = k_ref[...]
    v = v_ref[...]
    seen = causal()
    outs = []
    for h in range(2):
        qh = jnp.where(head_lanes(h), q, jnp.zeros_like(q))
        s00 = jnp.where(seen, nt(k[:half], qh[:half]), -1e30)
        s01 = nt(k[:half], qh[half:])
        s11 = jnp.where(seen, nt(k[half:], qh[half:]), -1e30)
        sides = []
        for side, parts in enumerate(([s00], [s01, s11])):
            peak = functools.reduce(jnp.maximum, [jnp.max(p, 0, keepdims=True) for p in parts])
            ps = [jnp.exp2((p - peak) * EXP2_SCALE) for p in parts]
            total = functools.reduce(jnp.add, [jnp.sum(p, 0, keepdims=True) for p in ps])
            vs = [v[:half], v[half:]]
            sides.append(functools.reduce(jnp.add, [tn(a, p.astype(BF16)) for a, p in zip(vs, ps)]))
            cols = pl.ds(side * half, half)
            peak_ref[h : h + 1, cols] = peak
            total_ref[h : h + 1, cols] = total
        outs.append(jnp.concatenate(sides, 1))
    lanes = lax.broadcasted_iota(jnp.int32, (2 * HD, 1), 0) // HD == 0
    out_ref[...] = jnp.where(lanes, outs[0], outs[1])


def attend_memory(q_ref, mk_ref, mv_ref, tokens_ref, peak_ref, total_ref, out_ref, lse_ref):
    q = q_ref[...]
    mk = mk_ref[...]
    mv = mv_ref[...]
    lanes = lax.broadcasted_iota(jnp.int32, (2 * HD, 1), 0) // HD == 0
    found = []
    for h in range(2):
        s = nt(mk, jnp.where(head_lanes(h), q, jnp.zeros_like(q)))
        old = peak_ref[h : h + 1]
        peak = jnp.maximum(old, jnp.max(s, 0, keepdims=True))
        p = jnp.exp2((s - peak) * EXP2_SCALE)
        shrink = jnp.exp2((old - peak) * EXP2_SCALE)
        total = total_ref[h : h + 1] * shrink + jnp.sum(p, 0, keepdims=True)
        lse_ref[h : h + 1] = peak * EXP2_SCALE + jnp.log2(total)
        rate = 1.0 / total
        found.append((tn(mv, p.astype(BF16)) * rate, shrink * rate))
    (o0, r0), (o1, r1) = found
    out_ref[...] = (jnp.where(lanes, o0, o1) + tokens_ref[...] * jnp.where(lanes, r0, r1)).T.astype(BF16)


def attend_kernel(q_ref, k_ref, v_ref, mk_ref, mv_ref, out_ref, peak_ref):
    attend_core(*(r.at[0] for r in (q_ref, k_ref, v_ref, mk_ref, mv_ref, out_ref)), peak_ref.at[0, 0])

def attend(qkv, mem):
    docs, _, w3 = qkv.shape
    w = w3 // 3
    pairs = w // 128
    tok = lambda o: pl.BlockSpec((1, L, 128), lambda d, i: (d, 0, o * pairs + i))
    me = lambda o: pl.BlockSpec((1, NB, 128), lambda d, i: (d, 0, o * pairs + i))
    return pl.pallas_call(attend_kernel, grid=(docs, pairs),
        in_specs=[tok(0), tok(1), tok(2), me(0), me(1)],
        out_specs=[tok(0), pl.BlockSpec((1, 1, 2, L), lambda d, i: (d, i, 0, 0))],
        out_shape=[jax.ShapeDtypeStruct((docs, L, w), BF16), jax.ShapeDtypeStruct((docs, pairs, 2, L), F32)],
        compiler_params=pltpu.CompilerParams(vmem_limit_bytes=48 << 20),
        cost_estimate=pl.CostEstimate(flops=docs * pairs * 8 * 768 * 512 * 128, bytes_accessed=docs * L * w * 10, transcendentals=docs * 12 * 768 * 512),
    )(qkv, qkv, qkv, mem, mem)

def grads_core(q_ref, k_ref, v_ref, mk_ref, mv_ref, g_ref, o_ref, peak_ref, dtok_ref, dmem_ref):
    half = L // 2
    q = q_ref[0]; k = k_ref[0]; v = v_ref[0]; mk = mk_ref[0]; mv = mv_ref[0]; g = g_ref[0]
    scale = HD ** -0.5
    seen = causal()
    go = g.astype(F32) * o_ref[0].astype(F32)
    pick = (lax.broadcasted_iota(jnp.int32, (8, 2 * HD), 1) // HD == lax.broadcasted_iota(jnp.int32, (8, 2 * HD), 0)).astype(F32)
    delta = lax.dot_general(pick, go, (((1,), (1,)), ((), ())), precision=lax.Precision.HIGHEST, preferred_element_type=F32)
    first = head_lanes(0)
    res = []
    for h in range(2):
        mine = head_lanes(h)
        qh = jnp.where(mine, q, jnp.zeros_like(q))
        gh = jnp.where(mine, g, jnp.zeros_like(g))
        lse = peak_ref[0, 0, pl.ds(h, 1), :]
        dh = delta[h:h + 1]
        def tile(kk, vv, lo, hi, mask):
            s = nt(kk, qh[lo:hi])
            p = jnp.exp2(s * EXP2_SCALE - lse[:, lo:hi])
            if mask:
                p = jnp.where(seen, p, 0.0)
            dp = nt(vv, gh[lo:hi])
            return p.astype(BF16), (p * (dp - dh[:, lo:hi])).astype(BF16)
        p00, t00 = tile(k[:half], v[:half], 0, half, True)
        p01, t01 = tile(k[:half], v[:half], half, L, False)
        p11, t11 = tile(k[half:], v[half:], half, L, True)
        pm, tm = tile(mk, mv, 0, L, False)
        dv0 = nn(p00, g[:half]) + nn(p01, g[half:])
        dv1 = nn(p11, g[half:])
        dvm = nn(pm, g)
        dk0 = nn(t00, q[:half]) + nn(t01, q[half:])
        dk1 = nn(t11, q[half:])
        dkm = nn(tm, q)
        dq0 = tn(k[:half], t00) + tn(mk, tm[:, :half])
        dq1 = tn(k[:half], t01) + tn(k[half:], t11) + tn(mk, tm[:, half:])
        res.append((jnp.concatenate([dq0, dq1], 1), jnp.concatenate([dk0, dk1], 0), jnp.concatenate([dv0, dv1], 0), dkm, dvm))
    rows = lax.broadcasted_iota(jnp.int32, (2 * HD, 1), 0) // HD == 0
    dq = (jnp.where(rows, res[0][0], res[1][0]).T * scale).astype(BF16)
    dk, dv, dkm, dvm = [jnp.where(first, a, b) for a, b in zip(res[0][1:], res[1][1:])]
    dk = (dk * scale).astype(BF16); dkm = (dkm * scale).astype(BF16)
    dv = dv.astype(BF16); dvm = dvm.astype(BF16)
    dtok_ref[0, 0] = dq; dtok_ref[1, 0] = dk; dtok_ref[2, 0] = dv
    dmem_ref[0, 0] = dkm; dmem_ref[1, 0] = dvm
    qs = jnp.sum(dq.astype(F32), 0, keepdims=True)
    vs = jnp.sum(dv.astype(F32), 0, keepdims=True) + jnp.sum(dvm.astype(F32), 0, keepdims=True)
    return qs, vs


def grads_kernel(*refs):
    qs, vs = grads_core(*refs[:-1])
    r = lax.broadcasted_iota(jnp.int32, (8, 128), 0)
    refs[-1][0] = jnp.where(r == 0, qs, jnp.where(r == 1, vs, 0.0))

def attend_grads(qkv, mem, g, mixed, lse):
    docs, _, w3 = qkv.shape
    w = w3 // 3
    pairs = w // 128
    tok = lambda o: pl.BlockSpec((1, L, 128), lambda d, i: (d, 0, o * pairs + i))
    me = lambda o: pl.BlockSpec((1, NB, 128), lambda d, i: (d, 0, o * pairs + i))
    return pl.pallas_call(grads_kernel, grid=(docs, pairs),
        in_specs=[tok(0), tok(1), tok(2), me(0), me(1), tok(0), tok(0), pl.BlockSpec((1, 1, 2, L), lambda d, i: (d, i, 0, 0))],
        out_specs=[pl.BlockSpec((3, 1, L, 128), lambda d, i: (0, d, 0, i)), pl.BlockSpec((2, 1, NB, 128), lambda d, i: (0, d, 0, i)), pl.BlockSpec((1, 8, 128), lambda d, i: (d, 0, i))],
        out_shape=[jax.ShapeDtypeStruct((3, docs, L, w), BF16), jax.ShapeDtypeStruct((2, docs, NB, w), BF16), jax.ShapeDtypeStruct((docs, 8, w), F32)],
        compiler_params=pltpu.CompilerParams(vmem_limit_bytes=48 << 20),
        cost_estimate=pl.CostEstimate(flops=docs * pairs * 20 * 768 * 512 * 128, bytes_accessed=docs * L * w * 16, transcendentals=docs * 12 * 768 * 512),
    )(qkv, qkv, qkv, mem, mem, g, mixed, lse)


def mm(a, b):
    return jnp.dot(a, b, preferred_element_type=F32)


def normalised(values):
    center = jnp.mean(values, -1, keepdims=True)
    shifted = values - center
    rate = lax.rsqrt(jnp.mean(shifted * shifted, -1, keepdims=True) + EPSILON)
    return shifted * rate, rate


def norm_back(unit, rate, scaled_grad):
    inner = jnp.mean(scaled_grad * unit, -1, keepdims=True)
    return rate * (scaled_grad - jnp.mean(scaled_grad, -1, keepdims=True) - unit * inner)


def whole(shape):
    return pl.BlockSpec(shape, lambda *_: (0,) * len(shape), pipeline_mode=pl.Buffered(1))


def col_sums(values):
    return jnp.sum(values, 0, keepdims=True)


def project_kernel(x_ref, w_ref, bias_ref, gain_ref, offset_ref, hidden_ref, qkv_ref):
    unit, _ = normalised(x_ref[0].astype(F32))
    hidden = (unit * gain_ref[...] + offset_ref[...]).astype(BF16)
    hidden_ref[0] = hidden
    qkv_ref[0] = (mm(hidden, w_ref[...]) + bias_ref[...]).astype(BF16)


def project(x, w_qkv, bias, gain, offset):
    docs, _, w = x.shape
    tile = 256
    rows = lambda c: pl.BlockSpec((1, tile, c), lambda d, i: (d, i, 0))
    return pl.pallas_call(
        project_kernel,
        grid=(docs, L // tile),
        in_specs=[rows(w), whole(w_qkv.shape), whole((1, 3 * w)), whole((1, w)), whole((1, w))],
        out_specs=[rows(w), rows(3 * w)],
        out_shape=[jax.ShapeDtypeStruct((docs, L, w), BF16), jax.ShapeDtypeStruct((docs, L, 3 * w), BF16)],
        compiler_params=pltpu.CompilerParams(vmem_limit_bytes=40 << 20),
        cost_estimate=pl.CostEstimate(flops=docs * L * w * w * 6, bytes_accessed=docs * L * w * 10, transcendentals=0),
    )(x, w_qkv, bias[None], gain[None], offset[None])


def renew_kernel(carry_ref, data_ref, memory_ref, hidden_ref, out_ref):
    out_ref[0] = dot_hi(carry_ref[0], memory_ref[0], 1, 0) + dot_hi(data_ref[0], hidden_ref[0].astype(F32), 1, 0)


def renew(carry_map, data_map, memory, hidden):
    docs, _, w = hidden.shape
    one = lambda r, c: pl.BlockSpec((1, r, c), lambda d: (d, 0, 0))
    return pl.pallas_call(
        renew_kernel,
        grid=(docs,),
        in_specs=[one(NB, NB), one(NB, L), one(NB, w), one(L, w)],
        out_specs=one(NB, w),
        out_shape=jax.ShapeDtypeStruct((docs, NB, w), F32),
        compiler_params=pltpu.CompilerParams(vmem_limit_bytes=40 << 20),
        cost_estimate=pl.CostEstimate(flops=docs * 6 * NB * 768 * w * 2, bytes_accessed=docs * NB * w * 8, transcendentals=0),
    )(carry_map, data_map, memory, hidden)


def recall_kernel(memory_ref, w_ref, bias_ref, low_ref, out_ref):
    low = memory_ref[...].astype(BF16)
    low_ref[...] = low
    out_ref[...] = (mm(low, w_ref[...]) + bias_ref[...]).astype(BF16)


def recall(memory, w_qkv, bias):
    rows, w = memory.shape
    tile = w
    return pl.pallas_call(
        recall_kernel,
        grid=(2,),
        in_specs=[whole((rows, w)), pl.BlockSpec((w, tile), lambda i: (0, 1 + i)), pl.BlockSpec((1, tile), lambda i: (0, 1 + i))],
        out_specs=[pl.BlockSpec((rows, w), lambda i: (0, 0)), pl.BlockSpec((rows, tile), lambda i: (0, i))],
        out_shape=[jax.ShapeDtypeStruct((rows, w), BF16), jax.ShapeDtypeStruct((rows, 2 * w), BF16)],
        compiler_params=pltpu.CompilerParams(vmem_limit_bytes=40 << 20),
        cost_estimate=pl.CostEstimate(flops=rows * w * w * 4, bytes_accessed=rows * w * 10, transcendentals=0),
    )(memory, w_qkv, bias[None])


GELU_RATE = 0.7978845608028654
GELU_CUBE = 0.044715


def feed_core(x_ref, mixed_ref, cot_ref, w_out_ref, w_in_ref, w_back_ref, vectors, in_bias,
              result_ref, normed_ref, act_ref, pre_ref, rgrad_ref, branch_ref, mgrad_ref):
    out_bias, back_bias, gain, offset = (ref[...] for ref in vectors)
    cot = cot_ref[...]
    residual = x_ref[...].astype(F32) + (mm(mixed_ref[...], w_out_ref[...]) + out_bias)
    unit, rate = normalised(residual)
    normed = (unit * gain + offset).astype(BF16)
    normed_ref[...] = normed
    result = residual + back_bias
    ngrad = None
    chunk = 768
    wide = []
    for c in range(0, w_in_ref.shape[1], chunk):
        sl = pl.ds(c, chunk)
        v = mm(normed, w_in_ref[:, sl]) + in_bias(c // chunk)
        square = v * v
        t = jnp.tanh(GELU_RATE * v * (1.0 + GELU_CUBE * square))
        half = 0.5 * (1.0 + t)
        act = (v * half).astype(BF16)
        slope = half + (0.5 * GELU_RATE) * v * (1.0 - t * t) * (1.0 + 3.0 * GELU_CUBE * square)
        act_ref[:, sl] = act
        result = result + mm(act, w_back_ref[sl, :])
        pre = (nt(cot, w_back_ref[sl, :]) * slope).astype(BF16)
        pre_ref[:, sl] = pre
        wide.append(col_sums(pre.astype(F32)))
        part = nt(pre, w_in_ref[:, sl])
        ngrad = part if ngrad is None else ngrad + part
    result_ref[...] = result.astype(BF16)
    rgrad = cot.astype(F32) + norm_back(unit, rate, ngrad * gain)
    rgrad_ref[...] = rgrad
    branch = rgrad.astype(BF16)
    branch_ref[...] = branch
    mgrad_ref[...] = nt(branch, w_out_ref[...]).astype(BF16)
    sums = [col_sums(cot.astype(F32)), col_sums(branch.astype(F32)), col_sums(ngrad * unit), col_sums(ngrad)]
    return wide, sums


def feed_kernel(x_ref, mixed_ref, cot_ref, w_out_ref, w_in_ref, w_back_ref, rows_ref, in_bias_ref, *out_refs):
    vectors = [rows_ref.at[pl.ds(i, 1)] for i in range(4)]
    in_bias = lambda k: in_bias_ref[:, pl.ds(k * 768, 768)]
    wide, sums = feed_core(x_ref, mixed_ref, cot_ref, w_out_ref, w_in_ref, w_back_ref, vectors, in_bias, *out_refs[:7])
    wide_ref, sums_ref = out_refs[7:]
    w = x_ref.shape[1]
    sums = jnp.concatenate(sums + [jnp.zeros((4, w), F32)], 0)
    wide = jnp.concatenate(wide, 1)

    @pl.when(pl.program_id(0) == 0)
    def _():
        sums_ref[...] = sums
        wide_ref[...] = wide

    @pl.when(pl.program_id(0) > 0)
    def _():
        sums_ref[...] += sums
        wide_ref[...] += wide


def feed(x, mixed, cot, w_out, w_in, w_back, rows4, in_bias):
    n, w = x.shape
    ff = w_in.shape[1]
    tile = 256
    rows = lambda c: pl.BlockSpec((tile, c), lambda i: (i, 0))
    arr = lambda c, t: jax.ShapeDtypeStruct((n, c), t)
    return pl.pallas_call(
        feed_kernel,
        grid=(n // tile,),
        in_specs=[rows(w), rows(w), rows(w), whole(w_out.shape), whole(w_in.shape), whole(w_back.shape), whole((4, w)), whole((1, ff))],
        out_specs=[rows(w), rows(w), rows(ff), rows(ff), rows(w), rows(w), rows(w),
                   pl.BlockSpec((1, ff), lambda i: (0, 0)), pl.BlockSpec((8, w), lambda i: (0, 0))],
        out_shape=[arr(w, BF16), arr(w, BF16), arr(ff, BF16), arr(ff, BF16), arr(w, F32), arr(w, BF16), arr(w, BF16),
                   jax.ShapeDtypeStruct((1, ff), F32), jax.ShapeDtypeStruct((8, w), F32)],
        compiler_params=pltpu.CompilerParams(vmem_limit_bytes=56 << 20),
        cost_estimate=pl.CostEstimate(flops=n * (4 * w * ff + 2 * w * w) * 2, bytes_accessed=n * ff * 4 + 2 * w * ff * 4, transcendentals=n * ff),
    )(x, mixed, cot, w_out, w_in, w_back, rows4, in_bias[None])


def local_kernel(g_ref, w_ref, out_ref):
    part = nt(g_ref[0], w_ref[...])

    @pl.when(pl.program_id(0) == 0)
    def _():
        out_ref[...] = part

    @pl.when(pl.program_id(0) == 1)
    def _():
        out_ref[...] += part


def local_memory_grad(memory_proj, w_qkv):
    _, rows, w = memory_proj.shape
    return pl.pallas_call(
        local_kernel,
        grid=(2,),
        in_specs=[pl.BlockSpec((1, rows, w), lambda i: (i, 0, 0)), pl.BlockSpec((w, w), lambda i: (0, 1 + i))],
        out_specs=pl.BlockSpec((rows, w), lambda i: (0, 0)),
        out_shape=jax.ShapeDtypeStruct((rows, w), F32),
        compiler_params=pltpu.CompilerParams(vmem_limit_bytes=40 << 20),
        cost_estimate=pl.CostEstimate(flops=rows * w * w * 4, bytes_accessed=rows * w * 10, transcendentals=0),
    )(memory_proj, w_qkv)


def entry_kernel(x_ref, rgrad_ref, proj_ref, data_ref, inc_ref, w_ref, gain_ref, out_ref, sums_ref):
    w = x_ref.shape[2]
    hgrad = dot_hi(data_ref[0], inc_ref[0], 0, 0)
    for p in range(3):
        hgrad = hgrad + nt(proj_ref[p, 0], w_ref[:, pl.ds(p * w, w)])
    unit, rate = normalised(x_ref[0].astype(F32))
    out_ref[0] = (rgrad_ref[0] + norm_back(unit, rate, hgrad * gain_ref[...])).astype(BF16)
    sums = jnp.concatenate([col_sums(hgrad * unit), col_sums(hgrad), jnp.zeros((6, w), F32)], 0)
    start = (pl.program_id(0) == 0) & (pl.program_id(1) == 0)

    @pl.when(start)
    def _():
        sums_ref[...] = sums

    @pl.when(jnp.logical_not(start))
    def _():
        sums_ref[...] += sums


def entry_grads(x, rgrad, token_proj, data_map, incoming, w_qkv, gain):
    docs, _, w = x.shape
    tile = 256
    rows = pl.BlockSpec((1, tile, w), lambda d, i: (d, i, 0))
    return pl.pallas_call(
        entry_kernel,
        grid=(docs, L // tile),
        in_specs=[rows, rows, pl.BlockSpec((3, 1, tile, w), lambda d, i: (0, d, i, 0)),
                  pl.BlockSpec((1, NB, tile), lambda d, i: (d, 0, i)), pl.BlockSpec((1, NB, w), lambda d, i: (d, 0, 0)),
                  whole(w_qkv.shape), whole((1, w))],
        out_specs=[rows, pl.BlockSpec((8, w), lambda d, i: (0, 0))],
        out_shape=[jax.ShapeDtypeStruct((docs, L, w), BF16), jax.ShapeDtypeStruct((8, w), F32)],
        compiler_params=pltpu.CompilerParams(vmem_limit_bytes=40 << 20),
        cost_estimate=pl.CostEstimate(flops=docs * L * w * w * 6 + docs * L * NB * w * 12, bytes_accessed=docs * L * w * 14, transcendentals=0),
    )(x, rgrad, token_proj, data_map, incoming, w_qkv, gain[None])


MESH = pl.DeviceIdType.MESH
GROUPS = 3
STAGES = 5


AXES = ("z1", "z0", "x")


class Part:
    def __init__(self, me, held, out, cols, order, got, sems):
        self.me, self.held, self.out, self.got, self.sems = me, held, out, got, sems
        self.cols, self.order = cols, order
        self.stage = 0

    def span(self, which):
        count = self.held.shape[3] // 2
        return pl.ds(pl.multiple_of(which * count, 8), count)

    def at(self, axis, flip, index):
        done = self.order[: self.stage]
        where, free = [], 0
        for name in AXES:
            if name in done or name == axis:
                which = self.me[name]
                where.append(1 - which if flip and name == axis else which)
            elif index is None:
                where.append(slice(None))
            else:
                where.append(index[free])
                free += 1
        rows = slice(None)
        if "seg" in done or axis == "seg":
            which = self.me["seg"]
            rows = self.span(1 - which if flip and axis == "seg" else which)
        return self.held.at[(*where, rows, pl.ds(*self.cols))]

    def send(self):
        last = self.stage == 4
        to = "seg" if last else self.order[self.stage]
        source = self.at(None if last else to, not last, None)
        target = self.out.at[self.span(self.me["seg"]), pl.ds(*self.cols)] if last else self.got[self.stage]
        send, recv, local = self.sems
        self.copy = pltpu.make_async_remote_copy(
            src_ref=source, dst_ref=target, send_sem=send.at[self.stage], recv_sem=recv.at[self.stage],
            device_id=self.me["ids"][to], device_id_type=MESH)
        self.copy.start()
        if last:
            self.own = pltpu.make_async_copy(source, target, local)
            self.own.start()

    def advance(self):
        self.copy.wait()
        if self.stage == 4:
            self.own.wait()
            return
        got = self.got[self.stage]
        axis = self.order[self.stage]
        lead = len(got.shape) - 2

        def add(i, _):
            index = tuple((i >> (lead - 1 - k)) & 1 for k in range(lead))
            ref = self.at(axis, False, index)
            ref[...] += got[index]
            return 0

        lax.fori_loop(0, 1 << lead, add, 0)
        self.stage += 1
        self.send()


ORDERS = {
    "A": ("x", "seg", "z0", "z1"),
    "B": ("seg", "x", "z0", "z1"),
    "C": ("z0", "x", "seg", "z1"),
    "D": ("x", "z0", "seg", "z1"),
    "E": ("z0", "seg", "x", "z1"),
    "F": ("x", "z0", "z1", "seg"),
    "H": ("z0", "x", "z1", "seg"),
    "I": ("seg", "z0", "x", "z1"),
}
UNIT = 384
PLAN = ((("D", 4), ("I", 4)), (("H", 4), ("A", 4)), (("C", 4), ("A", 4)))
SCRIPT = (
    "back", "in", "att0", "att1", "local", "1D", "1I", "three", "1D", "1I",
    "2H", "2A", "entry", "1D", "1I", "3A", "3C", "2A", "s1", "2H",
    "1D", "1I", "3C", "1D", "s2", "3A", "2A", "1I", "2H", "3C",
    "s3", "2A", "2H", "3A", "3C", "s4", "2A", "2H", "3C", "3A",
    "3A", "s5",
)


def landing(rows, cols, order):
    shapes = []
    for stage, axis in enumerate(order):
        done = order[: stage + 1]
        lead = sum(name not in done for name in AXES)
        shapes.append((2,) * lead + (rows // 2 if "seg" in done else rows, cols))
    return [pltpu.VMEM(shape, F32) for shape in shapes]


def tail_kernel(docs, bits, *refs):
    (act, cot, normed, pre, qkv, mem, mgrad, mixed, lse, hidden, mem_rows, mixed_rows, branch, w_qkv, x, rgrad,
     data_map, carry_map, has, vec, small_in) = refs[:21]
    o_back, o_in, o_three, o_input, o_start, small, tok, memp = refs[21:29]
    h1, h2, h3, rc, slots, slot1, acc1, acc2, lg, inc, rsmall = refs[29:40]
    count = sum(len(p) for p in PLAN)
    gots = refs[40 : 40 + count * 4]
    send, recv, local, csend, crecv, misc_send, misc_recv, ssend, srecv, credit = refs[40 + count * 4 :]
    b, s = lax.axis_index("batch"), lax.axis_index("seg")
    n, w = cot.shape
    ff = act.shape[1]

    def flip(distance):
        return b + distance * (1 - 2 * ((b // distance) % 2))

    ids = {"core": (flip(1), s), "x": (flip(2), s), "z0": (flip(4), s), "z1": (flip(8), s), "seg": (b, 1 - s)}
    me = {"core": b % 2, "x": (b // 2) % 2, "z0": (b // 4) % 2, "z1": (b // 8) % 2, "seg": s, "ids": ids}
    mine = me["core"]

    @pl.when(s == 1)
    def _():
        inc[...] = jnp.zeros_like(inc)

    small[...] = small_in[...]
    barrier = pltpu.get_barrier_semaphore()
    for who in ids.values():
        pl.semaphore_signal(barrier, inc=1, device_id=who, device_id_type=MESH)
    pl.semaphore_wait(barrier, len(ids))

    def core_copy(g, i, slot, target):
        return pltpu.make_async_remote_copy(
            src_ref=slot, dst_ref=target, send_sem=csend.at[g, i], recv_sem=crecv.at[g, i], device_id=ids["core"], device_id_type=MESH)

    parts = {}
    for g, held in enumerate((h1, h2, h3)):
        first = 0
        for kind, units in PLAN[g]:
            i = len(parts)
            sems = (send.at[i], recv.at[i], local.at[i])
            out = (o_back, o_in, o_three)[g]
            parts[str(g + 1) + kind] = Part(me, held, out, (first, units * UNIT), ORDERS[kind], gots[4 * i : 4 * i + 4], sems)
            first += units * UNIT

    def send_group(g):
        for name, part in parts.items():
            if name[0] == str(g + 1):
                part.send()

    own2 = w // 16

    def core_slice(g, i, tile):
        cols = pl.ds(pl.multiple_of(i * tile, 128), tile)
        return core_copy(g, i, slots.at[i % 2, :, :, pl.ds(0, tile)], rc.at[:, :, cols])

    def pass_rows(g, i, held, tile):
        cols = pl.ds(pl.multiple_of(i * tile, 128), tile)

        @pl.when(i >= 2)
        def _():
            core_slice(g, i - 2, tile).wait_send()

        for k in range(8):
            slots[i % 2, k, :, 0:tile] = acc2[pl.ds(pl.multiple_of((2 * k + 1 - mine) * own2, 8), own2), 0:tile]
        core_slice(g, i, tile).start()
        for k in range(8):
            held[k // 4, k // 2 % 2, k % 2, :, cols] = acc2[pl.ds(pl.multiple_of((2 * k + mine) * own2, 8), own2), 0:tile]

    def took_core(g, copy, steps, held):
        copy(steps - 2).wait_send()
        copy(steps - 1).wait_send()

        def took(i, _):
            copy(i).wait_recv()
            return 0

        def add(k, _):
            held[k // 4, k // 2 % 2, k % 2] += rc[k]
            return 0

        lax.fori_loop(0, steps, took, 0)
        lax.fori_loop(0, 8, add, 0)
        if g < 2:
            pl.semaphore_signal(credit, inc=1, device_id=ids["core"], device_id_type=MESH)
        send_group(g)

    own1 = ff // 16

    def copy1(i):
        return core_copy(0, i, slot1.at[i % 2], rc.at[i])

    def back_body(act_ref, cot_ref):
        i = pl.program_id(0)
        acc1[...] = tn(act_ref[...], cot_ref[...])

        @pl.when(i >= 2)
        def _():
            copy1(i - 2).wait_send()

        for q in range(own1 // own2):
            cols = pl.ds(q * w, w)
            slot1[i % 2, :, cols] = acc1[pl.ds(pl.multiple_of((1 - mine) * own1 + q * own2, 8), own2)]
        copy1(i).start()
        for q in range(own1 // own2):
            cols = pl.ds(q * w, w)
            h1[i // 4, i // 2 % 2, i % 2, :, cols] = acc1[pl.ds(pl.multiple_of(mine * own1 + q * own2, 8), own2)]

    def do_back():
        pltpu.emit_pipeline(
            back_body, grid=(8,),
            in_specs=[pl.BlockSpec((n, 2 * own1), lambda i: (0, i)), pl.BlockSpec((n, w), lambda i: (0, 0))],
            out_specs=[],
        )(act, cot)
        took_core(0, copy1, 8, h1)

    tile2 = acc2.shape[1]

    def in_body(normed_ref, pre_ref):
        acc2[...] = tn(normed_ref[...], pre_ref[...])
        pass_rows(1, pl.program_id(0), h2, tile2)

    def do_in():
        pl.semaphore_wait(credit, 1)
        pltpu.emit_pipeline(
            in_body, grid=(ff // tile2,),
            in_specs=[pl.BlockSpec((n, w), lambda i: (0, 0)), pl.BlockSpec((n, tile2), lambda i: (0, i))],
            out_specs=[],
        )(normed, pre)
        took_core(1, lambda i: core_slice(1, i, tile2), ff // tile2, h2)

    pairs = w // 128

    def attention(doc):
        def body(*r):
            cols = pl.ds(pl.multiple_of(pl.program_id(0) * 128, 128), 128)
            qs, vs = grads_core(*r)
            small[0:1, cols] += qs
            small[1:2, cols] += vs

        t = lambda o: pl.BlockSpec((1, L, 128), lambda i: (doc, 0, o * pairs + i))
        m = lambda o: pl.BlockSpec((1, NB, 128), lambda i: (doc, 0, o * pairs + i))
        pltpu.emit_pipeline(
            body, grid=(pairs,),
            in_specs=[t(0), t(1), t(2), m(0), m(1), t(0), t(0), pl.BlockSpec((1, 1, 2, L), lambda i: (doc, i, 0, 0))],
            out_specs=[pl.BlockSpec((3, 1, L, 128), lambda i: (0, doc, 0, i)), pl.BlockSpec((2, 1, NB, 128), lambda i: (0, doc, 0, i))],
        )(qkv, qkv, qkv, mem, mem, mgrad, mixed, lse, tok, memp)

    def local_body(g_ref, w_ref):
        total = None
        for d in range(docs):
            part = nt(g_ref[0, d], w_ref[...])
            rows = pl.ds(d * NB, NB)

            @pl.when(pl.program_id(0) == 0)
            def _():
                lg[rows] = part

            @pl.when(pl.program_id(0) == 1)
            def _():
                lg[rows] += part

    def do_local():
        pltpu.emit_pipeline(
            local_body, grid=(2,),
            in_specs=[pl.BlockSpec((1, docs, NB, w), lambda i: (i, 0, 0, 0)), pl.BlockSpec((w, w), lambda i: (0, 1 + i))],
            out_specs=[],
        )(memp, w_qkv)

    upward = pltpu.make_async_remote_copy(
        src_ref=lg, dst_ref=inc, send_sem=misc_send.at[0], recv_sem=misc_recv.at[0], device_id=ids["seg"], device_id_type=MESH)

    def begin_upward():
        @pl.when(s == 1)
        def _():
            upward.start()

    tile3 = w
    per = w // tile3
    m = mem_rows.shape[0]

    def three_body(hidden_ref, mem_ref, mixed_ref, tok_ref, memg_ref, branch_ref):
        part = pl.program_id(0)

        @pl.when(part == 0)
        def _():
            acc2[:, 0:tile3] = sum(tn(hidden_ref[d], tok_ref[0, d]) for d in range(docs))

        @pl.when((part == 1) | (part == 2))
        def _():
            acc2[:, 0:tile3] = sum(tn(hidden_ref[d], tok_ref[0, d]) + tn(mem_ref[d], memg_ref[0, d]) for d in range(docs))

        @pl.when(part == 3)
        def _():
            acc2[:, 0:tile3] = tn(mixed_ref[...], branch_ref[...])

        pass_rows(2, part * per + pl.program_id(1), h3, tile3)

    def do_three():
        pl.semaphore_wait(credit, 1)
        pltpu.emit_pipeline(
            three_body, grid=(4, per),
            in_specs=[pl.BlockSpec((docs, L, w), lambda p, i: (0, 0, 0)), pl.BlockSpec((docs, NB, w), lambda p, i: (0, 0, 0)),
                      pl.BlockSpec((n, w), lambda p, i: (0, 0)),
                      pl.BlockSpec((1, docs, L, tile3), lambda p, i: (jnp.minimum(p, 2), 0, 0, jnp.where(p < 3, i, per - 1))),
                      pl.BlockSpec((1, docs, NB, tile3), lambda p, i: (jnp.clip(p - 1, 0, 1), 0, 0, jnp.where(p < 1, 0, jnp.where(p < 3, i, per - 1)))),
                      pl.BlockSpec((n, tile3), lambda p, i: (0, jnp.where(p < 3, 0, i)))],
            out_specs=[],
        )(hidden, mem_rows, mixed_rows, tok, memp, branch)
        took_core(2, lambda i: core_slice(2, i, tile3), 4 * per, h3)

    tile4 = 256

    def entry_body(x_ref, rgrad_ref, proj_ref, data_ref, w_ref, out_ref):
        d = pl.program_id(0)
        hgrad = dot_hi(data_ref[0], inc[pl.ds(pl.multiple_of(d * NB, NB), NB)], 0, 0)
        for p in range(3):
            hgrad = hgrad + nt(proj_ref[p, 0], w_ref[:, pl.ds(p * w, w)])
        unit, rate = normalised(x_ref[0].astype(F32))
        out_ref[0] = (rgrad_ref[0] + norm_back(unit, rate, hgrad * vec[4:5])).astype(BF16)
        small[4:5] += col_sums(hgrad * unit)
        small[5:6] += col_sums(hgrad)

    rows4 = pl.BlockSpec((1, tile4, w), lambda d, i: (d, i, 0))
    def do_entry():
        @pl.when(s == 0)
        def _():
            upward.wait_recv()

        pltpu.emit_pipeline(
            entry_body, grid=(docs, L // tile4),
            in_specs=[rows4, rows4, pl.BlockSpec((3, 1, tile4, w), lambda d, i: (0, d, i, 0)),
                      pl.BlockSpec((1, NB, tile4), lambda d, i: (d, 0, i)), pl.BlockSpec((w, 3 * w), lambda d, i: (0, 0))],
            out_specs=[rows4],
        )(x, rgrad, tok, data_map, w_qkv, o_input)

    def add_small(k, to):
        copy = pltpu.make_async_remote_copy(
            src_ref=small, dst_ref=rsmall.at[k], send_sem=ssend.at[k], recv_sem=srecv.at[k], device_id=ids[to], device_id_type=MESH)
        copy.start()
        return copy

    def took_small(k, copy):
        copy.wait()
        small[...] += rsmall[k]

    def start_body(carry_ref):
        d = pl.program_id(0)
        rows = pl.ds(pl.multiple_of(d * NB, NB), NB)
        lg[rows] = has[d].astype(F32) * (lg[rows] + dot_hi(carry_ref[0], inc[rows], 0, 0))

    half = w // 2
    stay = pltpu.make_async_copy(lg.at[:, pl.ds(0, half)], o_start, misc_send.at[1])
    leave = pltpu.make_async_remote_copy(
        src_ref=lg.at[:, pl.ds(half, half)], dst_ref=o_start, send_sem=misc_send.at[2], recv_sem=misc_recv.at[1],
        device_id=ids["seg"], device_id_type=MESH)

    def do_start():
        @pl.when(s == 1)
        def _():
            upward.wait_send()

        pltpu.emit_pipeline(
            start_body, grid=(docs,),
            in_specs=[pl.BlockSpec((1, NB, NB), lambda d: (d, 0, 0))],
            out_specs=[],
        )(carry_map)

        @pl.when(s == 0)
        def _():
            stay.start()
            leave.start()

    links = ("core", "x", "seg", "z0", "z1")
    for step in SCRIPT:
        if step == "back":
            do_back()
        elif step == "in":
            do_in()
        elif step[:3] == "att":
            attention(int(step[3:]))
        elif step == "local":
            do_local()
            begin_upward()
        elif step == "three":
            do_three()
        elif step == "entry":
            do_entry()
            tiny = add_small(0, "core")
            do_start()
        elif step[0] == "s":
            k = int(step[1])
            took_small(k - 1, tiny)
            if k < 5:
                tiny = add_small(k, links[k])
        else:
            parts[step].advance()

    @pl.when(s == 0)
    def _():
        stay.wait()
        leave.wait_send()

    @pl.when(s == 1)
    def _():
        leave.wait_recv()


def tail(docs, batch, act, cot, normed, pre, qkv, mem, mgrad, mixed, lse, hidden, mem_rows, branch, w_qkv, x, rgrad,
         data_map, carry_map, has, vec, small):
    n, w = cot.shape
    ff = act.shape[1]
    own1, own2 = ff // batch, w // batch
    ops = [act, cot, normed, pre, qkv, mem, mgrad, mixed, lse, hidden, mem_rows, mixed.reshape(n, w), branch, w_qkv, x, rgrad,
           data_map, carry_map, has, vec, small]
    anywhere = pl.BlockSpec(memory_space=pl.ANY)
    vmem = pl.BlockSpec(memory_space=pltpu.VMEM)
    f = lambda *shape: jax.ShapeDtypeStruct(shape, F32)
    outs = [f(own2, ff), f(own2, ff), f(own2, 4 * w), jax.ShapeDtypeStruct((docs, L, w), BF16), f(docs * NB, w // 2), f(16, w),
            jax.ShapeDtypeStruct((3, docs, L, w), BF16), jax.ShapeDtypeStruct((2, docs, NB, w), BF16)]
    held = [pltpu.VMEM((2, 2, 2, own2, ff), F32)] * GROUPS
    slots = [pltpu.VMEM((8, own2, ff), F32), pltpu.VMEM((2, 8, own2, w), F32), pltpu.VMEM((2, own2, ff), F32)]
    accs = [pltpu.VMEM((2 * own1, w), F32), pltpu.VMEM((w, w), F32)]
    rest = [pltpu.VMEM((docs * NB, w), F32), pltpu.VMEM((docs * NB, w), F32), pltpu.VMEM((5, 16, w), F32)]
    gots = [buffer for plan in PLAN for kind, units in plan for buffer in landing(own2, units * UNIT, ORDERS[kind])]
    count = len(gots) // 4
    dma = pltpu.SemaphoreType.DMA
    sems = [dma((count, STAGES)), dma((count, STAGES)), dma((count,)), dma((GROUPS, 8)), dma((GROUPS, 8)),
            dma((3,)), dma((2,)), dma((5,)), dma((5,)), pltpu.SemaphoreType.REGULAR]
    return pl.pallas_call(
        functools.partial(tail_kernel, docs, 4),
        in_specs=[anywhere] * 18 + [pl.BlockSpec(memory_space=pltpu.SMEM), vmem, vmem],
        out_specs=[anywhere] * 5 + [vmem] + [anywhere] * 2,
        out_shape=outs,
        scratch_shapes=held + slots + accs + rest + gots + sems,
        compiler_params=pltpu.CompilerParams(vmem_limit_bytes=60 << 20, collective_id=0, has_side_effects=True),
        cost_estimate=pl.CostEstimate(flops=10**11, bytes_accessed=10**8, transcendentals=10**7),
    )(*ops)[:6]


def front_kernel(docs, *refs):
    (x, cot, w_qkv_hbm, w_out_hbm, w_in_hbm, w_back_hbm, start, has, sticky, *singles) = refs[:18]
    (result, normed, act, pre, rgrad, branch, mgrad, qkv_out, mem_out, mem_low_out, hidden_out, mixed_out, lse_out,
     carry_out, data_out, small, vec) = refs[18:35]
    (w_qkv, w_out, w_in, w_back, xs, hidden, qkv, memory, fresh, begin, mem, mem_low, mixed, lse, carry, data, a,
     partial, peaks, totals, wsem, osem, bsem, ssem, rsem) = refs[35:]
    b, s = lax.axis_index("batch"), lax.axis_index("seg")
    w = x.shape[2]
    half = w // 2
    q_bias, v_bias, out_bias, back_bias, gain1, offset1, gain2, offset2 = (vec.at[pl.ds(i, 1)] for i in range(8))
    in_bias = lambda k: vec[8 + k : 9 + k]
    for i in range(8):
        vec[i : i + 1] = singles[i][...][None]
    for i in range(w_in_hbm.shape[1] // w):
        vec[8 + i : 9 + i] = singles[8][pl.ds(i * w, w)][None]
    loads = [pltpu.make_async_copy(src, dst, wsem.at[i]) for i, (src, dst) in enumerate(
        [(x, xs), (w_qkv_hbm, w_qkv), (w_out_hbm, w_out), (w_in_hbm, w_in), (w_back_hbm, w_back)])]
    for load in loads:
        load.start()
    own_begin = pltpu.make_async_copy(start, begin.at[0], bsem)
    own_begin.start()
    peer = (b, 1 - s)
    barrier = pltpu.get_barrier_semaphore()
    pl.semaphore_signal(barrier, inc=1, device_id=peer, device_id_type=MESH)
    pl.semaphore_wait(barrier, 1)

    given = pltpu.make_async_remote_copy(
        src_ref=start, dst_ref=begin.at[1], send_sem=ssem.at[docs], recv_sem=rsem.at[docs], device_id=peer, device_id_type=MESH)

    @pl.when(s == 1)
    def _():
        given.start()

    maps_kernel(docs, sticky.at[:, 0], carry, data, a)
    outs = [pltpu.make_async_copy(carry, carry_out, osem.at[0]), pltpu.make_async_copy(data, data_out, osem.at[1])]
    for out in outs:
        out.start()

    loads[0].wait()
    for d in range(docs):
        unit, _ = normalised(xs[d].astype(F32))
        hidden[d] = (unit * gain1[...] + offset1[...]).astype(BF16)
    outs.append(pltpu.make_async_copy(hidden, hidden_out, osem.at[2]))
    outs[-1].start()
    own_begin.wait()

    @pl.when(s == 0)
    def _():
        given.wait_recv()
        for d in range(docs):
            flag = has[d].astype(F32)
            memory[d, :, 0:half] = flag * begin[0, d]
            memory[d, :, half:w] = flag * begin[1, d]

    def carried(d):
        return pltpu.make_async_remote_copy(
            src_ref=fresh.at[d], dst_ref=memory.at[d], send_sem=ssem.at[d], recv_sem=rsem.at[d], device_id=peer, device_id_type=MESH)

    @pl.when(s == 0)
    def _():
        for d in range(docs):
            fresh[d] = dot_hi(carry[d], memory[d], 1, 0) + dot_hi(data[d], hidden[d].astype(F32), 1, 0)
            carried(d).start()

    loads[1].wait()
    zero = jnp.zeros((1, w), F32)
    for d in range(docs):
        for p, bias in enumerate((q_bias[...], zero, v_bias[...])):
            cols = pl.ds(p * w, w)
            qkv[d, :, cols] = (mm(hidden[d], w_qkv[:, cols]) + bias).astype(BF16)
    outs.append(pltpu.make_async_copy(qkv, qkv_out, osem.at[3]))
    outs[-1].start()
    small[...] = jnp.zeros_like(small)
    vectors = (out_bias, back_bias, gain2, offset2)
    tile = 256
    pairs = w // 128

    def columns(p, i):
        return pl.ds(pl.multiple_of(p * w + i * 128, 128), 128)

    def early(k, _):
        d, i = k // pairs, k % pairs
        attend_tokens(qkv.at[d, :, columns(0, i)], qkv.at[d, :, columns(1, i)], qkv.at[d, :, columns(2, i)],
                      partial.at[d, i], peaks.at[d, i], totals.at[d, i])
        return 0

    lax.fori_loop(0, docs * pairs, early, 0)
    for load in loads[2:]:
        load.wait()
    for d in range(docs):
        @pl.when(s == 1)
        def _():
            carried(d).wait_recv()

        low = memory[d].astype(BF16)
        mem_low[d] = low
        for p, bias in enumerate((zero, v_bias[...])):
            mem[d, :, pl.ds(p * w, w)] = (mm(low, w_qkv[:, pl.ds((p + 1) * w, w)]) + bias).astype(BF16)

        def late(i, _):
            attend_memory(qkv.at[d, :, columns(0, i)], mem.at[d, :, columns(0, i)], mem.at[d, :, columns(1, i)],
                          partial.at[d, i], peaks.at[d, i], totals.at[d, i], mixed.at[d, :, columns(0, i)], lse.at[d, i])
            return 0

        lax.fori_loop(0, pairs, late, 0)

        def feed_body(x_ref, cot_ref, *out_refs):
            rows = pl.ds(pl.multiple_of(pl.program_id(0) * tile, tile), tile)
            wide, sums = feed_core(x_ref, mixed.at[d, rows], cot_ref, w_out, w_in, w_back, vectors, in_bias, *out_refs)
            small[2:3] += sums[1]
            small[3:4] += sums[0]
            small[6:7] += sums[2]
            small[7:8] += sums[3]
            for k, part in enumerate(wide):
                small[8 + k : 9 + k] += part

        first = d * (L // tile)
        rows = lambda c: pl.BlockSpec((tile, c), lambda i: (first + i, 0))
        ff = w_in.shape[1]
        pltpu.emit_pipeline(
            feed_body, grid=(L // tile,),
            in_specs=[pl.BlockSpec((tile, w), lambda i: (i, 0)), rows(w)],
            out_specs=[rows(w), rows(w), rows(ff), rows(ff), rows(w), rows(w), rows(w)],
        )(x.at[d], cot, result, normed, act, pre, rgrad, branch, mgrad)
    for i, (src, dst) in enumerate([(mem, mem_out), (mem_low, mem_low_out), (mixed, mixed_out), (lse, lse_out)]):
        outs.append(pltpu.make_async_copy(src, dst, osem.at[4 + i]))
        outs[-1].start()
    for out in outs:
        out.wait()

    @pl.when(s == 0)
    def _():
        for d in range(docs):
            carried(d).wait_send()

    @pl.when(s == 1)
    def _():
        given.wait_send()


def front(x, cot, w_qkv, w_out, w_in, w_back, start, has, sticky, *singles):
    docs, _, w = x.shape
    n = docs * L
    ff = w_in.shape[1]
    anywhere = pl.BlockSpec(memory_space=pl.ANY)
    vmem = pl.BlockSpec(memory_space=pltpu.VMEM)
    arr = jax.ShapeDtypeStruct
    lse_shape = (docs, w // 128, 2, L)
    kept = [(docs, L, 3 * w), (docs, NB, 2 * w), (docs, NB, w), (docs, L, w), (docs, L, w)]
    outs = [arr((n, c), t) for c, t in ((w, BF16), (w, BF16), (ff, BF16), (ff, BF16), (w, F32), (w, BF16), (w, BF16))]
    outs += [arr(shape, BF16) for shape in kept]
    outs += [arr(lse_shape, F32), arr((docs, NB, NB), F32), arr((docs, NB, L), F32), arr((16, w), F32), arr((16, w), F32)]
    v = pltpu.VMEM
    scratch = [v(w_qkv.shape, BF16), v(w_out.shape, BF16), v(w_in.shape, BF16), v(w_back.shape, BF16), v((docs, L, w), BF16),
               v((docs, L, w), BF16), v(kept[0], BF16), v((docs, NB, w), F32), v((docs, NB, w), F32), v((2, docs, NB, w // 2), F32),
               v(kept[1], BF16), v(kept[2], BF16), v((docs, L, w), BF16), v(lse_shape, F32), v((docs, NB, NB), F32),
               v((docs, NB, L), F32), v((docs, NB, NB), F32), v((docs, w // 128, 128, L), F32), v(lse_shape, F32), v(lse_shape, F32)]
    dma = pltpu.SemaphoreType.DMA
    scratch += [dma((5,)), dma((8,)), dma, dma((docs + 1,)), dma((docs + 1,))]
    return pl.pallas_call(
        functools.partial(front_kernel, docs),
        in_specs=[anywhere] * 7 + [pl.BlockSpec(memory_space=pltpu.SMEM)] + [vmem] * 10,
        out_specs=[anywhere] * 15 + [vmem] * 2,
        out_shape=outs,
        scratch_shapes=scratch,
        compiler_params=pltpu.CompilerParams(vmem_limit_bytes=60 << 20, collective_id=1, has_side_effects=True),
        cost_estimate=pl.CostEstimate(flops=10**11, bytes_accessed=10**8, transcendentals=10**7),
    )(x, cot, w_qkv, w_out, w_in, w_back, start, has, sticky, *singles)


def hand_over_kernel(back, wide, three, entry, start, result, small, *refs):
    outs, stages, sem = refs[:16], refs[16:23], refs[23]
    w = three.shape[1] // 4
    b = lax.axis_index("batch")
    pairs = [(back, outs[5]), (wide, outs[4]), (three.at[:, pl.ds(0, 3 * w)], outs[2]), (three.at[:, pl.ds(3 * w, w)], outs[3]),
             (entry, outs[1]), (result, outs[0]), (start, outs[6])]
    copies = [pltpu.make_async_copy(src, stage, sem.at[0, i]) for i, ((src, _), stage) in enumerate(zip(pairs, stages))]
    for copy in copies:
        copy.start()
    away = [pltpu.make_async_copy(stages[i], pairs[i][1], sem.at[1, i]) for i in range(1, len(pairs))]
    copies[0].wait()
    short = back.shape[0]
    for q in range(4):
        out = pltpu.make_async_copy(stages[0].at[:, pl.ds(q * w, w)], outs[5].at[pl.ds(q * short, short)], sem.at[1, 7 + q])
        out.start()
        away.append(out)
    for copy, out in zip(copies[1:], away):
        copy.wait()
        out.start()
    own = w // 16
    rows = lax.broadcasted_iota(jnp.int32, (w, 256), 0)
    cols = lax.broadcasted_iota(jnp.int32, (w, 256), 1)
    pick = (rows == cols + b * own) & (cols < own)
    mine = dot_hi(small[...], jnp.where(pick, 1.0, 0.0), 1, 0)
    pick = (rows == cols + (b % 4) * (4 * own)) & (cols < 4 * own)
    row = lax.broadcasted_iota(jnp.int32, (16, 1), 0) == 8 + b // 4
    long = dot_hi(jnp.where(row, small[...], 0.0), jnp.where(pick, 1.0, 0.0), 1, 0)
    long = jnp.sum(long, 0, keepdims=True)
    for i in range(8):
        outs[7 + i][...] = mine[i, :own]
    outs[15][...] = long[0, : 4 * own]
    for out in away:
        out.wait()


def hand_over(back, wide, three, entry, start, result, small):
    w = three.shape[1] // 4
    anywhere = pl.BlockSpec(memory_space=pl.ANY)
    vmem = pl.BlockSpec(memory_space=pltpu.VMEM)
    arr = lambda a: jax.ShapeDtypeStruct(a.shape, a.dtype)
    rows = three.shape[0]
    stages = [(back.shape, F32), (wide.shape, F32), ((rows, 3 * w), F32), ((rows, w), F32), (entry.shape, BF16), (result.shape, BF16),
              (start.shape, F32)]
    return pl.pallas_call(
        hand_over_kernel,
        in_specs=[anywhere] * 6 + [vmem],
        out_specs=[anywhere] * 7 + [vmem] * 9,
        out_shape=[arr(result), arr(entry), jax.ShapeDtypeStruct((rows, 3 * w), F32), jax.ShapeDtypeStruct((rows, w), F32), arr(wide),
                   jax.ShapeDtypeStruct((4 * rows, w), F32), arr(start)] + [jax.ShapeDtypeStruct((w // 16,), F32)] * 8 + [jax.ShapeDtypeStruct((w // 4,), F32)],
        scratch_shapes=[pltpu.VMEM(a, t) for a, t in stages] + [pltpu.SemaphoreType.DMA((2, 11))],
        compiler_params=pltpu.CompilerParams(vmem_limit_bytes=60 << 20),
        cost_estimate=pl.CostEstimate(flops=10**7, bytes_accessed=10**7, transcendentals=0),
    )(back, wide, three, entry, start, result, small)


def outer(a, b):
    return lax.dot_general(a, b, (((0,), (0,)), ((), ())), preferred_element_type=F32)


def passed(block, distance):
    n = lax.axis_size("seg")
    return lax.ppermute(block, "seg", [(i - distance, i) for i in range(n) if 0 <= i - distance < n])


def swap(block, axis, distance):
    n = lax.axis_size(axis)
    return lax.ppermute(block, axis, [(i, i ^ distance) for i in range(n)])


def halve(block, axis, distance, dim):
    bit = (lax.axis_index(axis) // distance) % 2
    send = lax.dynamic_index_in_dim(block, 1 - bit, dim, keepdims=False)
    keep = lax.dynamic_index_in_dim(block, bit, dim, keepdims=False)
    return keep + swap(send, axis, distance)


def spread(work, seg_place, first):
    n, s = lax.axis_size("batch"), lax.axis_size("seg")
    bits = n.bit_length() - 1
    _, own, cols = work.shape
    split = s if seg_place < bits and own % s == 0 else 1
    work = work.reshape((2,) * (bits - first) + (split, own // split, cols))
    for k in range(first, bits + 1):
        if k == seg_place:
            if split == 1:
                d = 1
                while d < s:
                    work = work + swap(work, "seg", d)
                    d *= 2
            else:
                left = bits - k
                work = work.reshape((2,) * left + (2,) * (s.bit_length() - 1) + (own // split, cols))
                d = 1
                while d < s:
                    work = halve(work, "seg", d, work.ndim - 3)
                    d *= 2
        if k < bits:
            work = halve(work, "batch", 1 << k, bits - 1 - k)
    if split > 1:
        d = s // 2
        while d >= 1:
            bit = (lax.axis_index("seg") // d) % 2
            other = swap(work, "seg", d)
            work = jnp.where(bit == 0, jnp.concatenate([work, other], 0), jnp.concatenate([other, work], 0))
            d //= 2
    return work.reshape(own, cols)


def forward(x, cot, w_qkv, w_out, w_in, w_back, start_memory, has_memory, sticky,
            q_bias, v_bias, out_bias, in_bias, back_bias, ln1_gain, ln1_bias, ln2_gain, ln2_bias):
    docs, _, width = x.shape
    n = docs * L
    chain = lax.axis_size("seg")
    is_first = lax.axis_index("seg") == 0
    flags = has_memory.astype(F32)[:, None, None]

    parts = [start_memory] + [lax.ppermute(start_memory, "seg", [(i, 0)]) for i in range(1, chain)]
    own_start = jnp.where(is_first, flags * jnp.concatenate(parts, 2), 0.0)

    carry_map, data_map = memory_maps(sticky)
    bias = jnp.concatenate([q_bias, jnp.zeros_like(q_bias), v_bias])
    hidden, qkv = project(x, w_qkv, bias, ln1_gain, ln1_bias)

    memory = own_start
    for i in range(chain - 1):
        memory = passed(renew(carry_map, data_map, memory, hidden), 1) + own_start

    mem_rows, mem = recall(memory.reshape(docs * NB, width), w_qkv, bias)
    mem = mem.reshape(docs, NB, 2 * width)
    mixed, log_total = attend(qkv, mem)
    rows4 = jnp.stack([out_bias, back_bias, ln2_gain, ln2_bias])
    result, normed, act, pre, residual_grad, branch, mixed_grad, wide, sums = feed(
        x.reshape(n, width), mixed.reshape(n, width), cot, w_out, w_in, w_back, rows4, in_bias
    )
    small = [sums[1:2], sums[0:1], jnp.zeros((2, width), F32), sums[2:4], wide.reshape(4, width)]
    small = jnp.concatenate([jnp.zeros((2, width), F32)] + small + [jnp.zeros((4, width), F32)], 0)
    return (result, normed, act, pre, residual_grad, branch, mixed_grad, qkv, mem, mem_rows, hidden, mixed, log_total,
            carry_map, data_map, small)


def spread_out(x, act, cot, normed, pre, qkv, mem, mgrad, mixed, lse, hidden, mem_rows, branch, w_qkv, rgrad, data_map, carry_map, has_memory, gain, small):
    docs, _, width = x.shape
    n = docs * L
    batch, chain = lax.axis_size("batch"), lax.axis_size("seg")
    is_first = lax.axis_index("seg") == 0
    flags = has_memory.astype(F32)[:, None, None]
    grad_back = spread(outer(act, cot).reshape(batch, -1, width), 2, 0)
    grad_in = spread(outer(normed, pre).reshape(batch, width // batch, -1), 1, 0)
    token_proj, memory_proj, attn_sums = attend_grads(qkv, mem, mgrad, mixed, lse)
    memory_proj = memory_proj.reshape(2, docs * NB, width)
    local_grad = local_memory_grad(memory_proj, w_qkv).reshape(docs, NB, width)
    carry_back = carry_map.swapaxes(1, 2)
    incoming = jnp.zeros_like(local_grad)
    for i in range(chain - 1):
        sent = local_grad if i == 0 else jnp.matmul(carry_back, incoming, precision=HI) + local_grad
        incoming = passed(sent, -1)
    hidden_rows = hidden.reshape(n, width)
    three = [outer(hidden_rows, token_proj[i].reshape(n, width)) for i in range(3)]
    three = [three[0]] + [three[i + 1] + outer(mem_rows, memory_proj[i]) for i in range(2)]
    three = jnp.concatenate(three + [outer(mixed.reshape(n, width), branch)], 1)
    grad_three = spread(three.reshape(batch, width // batch, -1), 2, 0)
    input_grad, entry_sums = entry_grads(
        x, rgrad, token_proj, data_map, incoming, w_qkv, gain
    )
    start_grad = jnp.where(is_first, flags * (local_grad + jnp.matmul(carry_back, incoming, precision=HI)), 0.0)
    own = width // chain
    start_share = start_grad[:, :, :own]
    for i in range(1, chain):
        start_share = start_share + lax.ppermute(start_grad[:, :, i * own : (i + 1) * own], "seg", [(0, i)])

    wide = small[8:12].reshape(-1)
    packed = jnp.concatenate(
        [g.reshape(batch, 1, -1)
         for g in (jnp.sum(attn_sums[:, 0], 0), jnp.sum(attn_sums[:, 1], 0), small[2], small[3], entry_sums[0], entry_sums[1],
                   small[6], small[7], wide)], 2)
    packed = spread(packed, batch.bit_length() - 1, 0)[0]
    own = width // batch
    vectors = [packed[i * own : (i + 1) * own] for i in range(8)] + [packed[8 * own :]]
    return input_grad, start_share, grad_back, grad_in, grad_three, vectors


def shards(
    tokens,
    start_memory,
    has_memory,
    sticky,
    w_qkv,
    w_out,
    w_in,
    w_back,
    q_bias,
    v_bias,
    out_bias,
    in_bias,
    back_bias,
    ln1_gain,
    ln1_bias,
    ln2_gain,
    ln2_bias,
    cotangent,
):
    width = w_qkv.shape[0]
    docs = tokens.shape[0]
    n = docs * L
    chain = lax.axis_size("seg")
    batch = lax.axis_size("batch")
    x = tokens[:, 0]
    cot = cotangent[:, 0].reshape(n, width)
    if (batch, chain) == (16, 2):
        (result, normed, act, pre, residual_grad, branch, mixed_grad, qkv, mem, mem_rows, hidden, mixed, log_total,
         carry_map, data_map, small, vec) = front(
            x, cot, w_qkv, w_out, w_in, w_back, start_memory, has_memory, sticky,
            q_bias, v_bias, out_bias, back_bias, ln1_gain, ln1_bias, ln2_gain, ln2_bias, in_bias)
        sums = tail(
            docs, batch, act, cot, normed, pre, qkv, mem, mixed_grad.reshape(docs, L, width), mixed, log_total, hidden,
            mem_rows, branch, w_qkv, x, residual_grad.reshape(docs, L, width), data_map, carry_map, has_memory, vec, small)
        back, wide, three, entry, start, vectors = sums
        result, input_grad, grad_qkv, grad_out, grad_in, grad_back, start_share, *vectors = hand_over(
            back, wide, three, entry, start, result, vectors)
        start_share = start_share.reshape(docs, NB, width // chain)
    else:
        (result, normed, act, pre, residual_grad, branch, mixed_grad, qkv, mem, mem_rows, hidden, mixed, log_total,
         carry_map, data_map, small) = forward(
            x, cot, w_qkv, w_out, w_in, w_back, start_memory, has_memory, sticky[:, 0],
            q_bias, v_bias, out_bias, in_bias, back_bias, ln1_gain, ln1_bias, ln2_gain, ln2_bias)
        input_grad, start_share, grad_back, grad_in, grad_three, vectors = spread_out(
            x, act, cot, normed, pre, qkv, mem, mixed_grad.reshape(docs, L, width), mixed, log_total, hidden, mem_rows,
            branch, w_qkv, residual_grad.reshape(docs, L, width), data_map, carry_map, has_memory, ln1_gain, small
        )
        grad_qkv, grad_out = grad_three[:, : 3 * width], grad_three[:, 3 * width :]
    return (
        result.reshape(docs, 1, L, width),
        input_grad.reshape(docs, 1, L, width),
        start_share,
        grad_qkv,
        grad_out,
        grad_in,
        grad_back,
    ) + tuple(vectors[i] for i in (0, 1, 2, 8, 3, 4, 5, 6, 7))


def solution(mesh):
    rows = P("batch", "seg", None, None)
    in_specs = (rows, P("batch", None, "seg"), P("batch"), P("batch", "seg", None)) + (P(),) * 13 + (rows,)
    out_specs = (rows, rows, P("batch", None, "seg")) + (P("batch", None),) * 4 + (P("batch"),) * 9
    return jax.shard_map(shards, mesh=mesh, in_specs=in_specs, out_specs=out_specs, check_vma=False)
```

```python
import functools

import jax
import jax.numpy as jnp
from jax import lax
from jax.experimental import pallas as pl
from jax.experimental.pallas import tpu as pltpu
from jax.sharding import PartitionSpec as P

HEADS = 12
HD = 64
NB = 256
L = 512
STICKY = 512
GRID = 4096

EPSILON = 1e-05
RIDGE = 0.5
HI = lax.Precision.HIGHEST
F32 = jnp.float32
BF16 = jnp.bfloat16
EXP2_SCALE = HD**-0.5 * 1.4426950408889634
LEAF = 32
PIVOTS = 4


def dot_hi(a, b, ca, cb):
    return lax.dot_general(a, b, (((ca,), (cb,)), ((), ())), precision=HI, preferred_element_type=F32)

def bumps(times):
    centers = (lax.broadcasted_iota(jnp.int32, (NB, 1), 0).astype(F32) + 0.5) / NB
    scaled = (times - centers) * NB
    return jnp.exp(-0.5 * scaled * scaled)

def small_inverse(s):
    p = len(s)
    s = [list(r) for r in s]
    for k in range(p):
        inv = 1.0 / s[k][k]
        row = [inv if j == k else s[k][j] * inv for j in range(p)]
        for i in range(p):
            if i != k:
                f = s[i][k]
                s[i] = [-f * row[j] if j == k else s[i][j] - f * row[j] for j in range(p)]
        s[k] = row
    return s


def leaf_inverse(d):
    n = d.shape[0]
    rows = lax.broadcasted_iota(jnp.int32, (n, n), 0)
    lanes = lax.broadcasted_iota(jnp.int32, (1, n), 1)
    for k in range(0, n, PIVOTS):
        cols = [jnp.broadcast_to(d[:, k + j : k + j + 1], (n, n)) for j in range(PIVOTS)]
        inv = small_inverse([[cols[j][k + i : k + i + 1] for j in range(PIVOTS)] for i in range(PIVOTS)])
        old = [d[k + j : k + j + 1] for j in range(PIVOTS)]
        inside = (lanes >= k) & (lanes < k + PIVOTS)
        fresh = []
        for i in range(PIVOTS):
            r = inv[i][0] * old[0]
            for j in range(1, PIVOTS):
                r = r + inv[i][j] * old[j]
            for j in range(PIVOTS):
                r = jnp.where(lanes == k + j, inv[i][j], r)
            fresh.append(r)
        out = jnp.where(inside, 0.0, d)
        for i in range(PIVOTS):
            out = out - cols[i] * fresh[i]
        for i in range(PIVOTS):
            out = jnp.where(rows == k + i, fresh[i], out)
        d = out
    return d


def maps_kernel(docs, sticky_ref, carry_ref, data_ref, a_ref):
    new_times = 0.5 + 0.5 * (lax.broadcasted_iota(jnp.int32, (1, L), 1).astype(F32) + 0.5) / L
    fresh = bumps(new_times)
    eye = (lax.broadcasted_iota(jnp.int32, (NB, NB), 0) == lax.broadcasted_iota(jnp.int32, (NB, NB), 1)).astype(F32)
    base = dot_hi(fresh, fresh, 1, 1) + RIDGE * eye
    for d in range(docs):
        old = (sticky_ref[pl.ds(d, 1), :].astype(F32) + 0.5) / GRID
        f1 = bumps(0.5 * old)
        a_ref[d] = base + dot_hi(f1, f1, 1, 1)
        carry_ref[d] = dot_hi(f1, bumps(old), 1, 1)
    lanes = lax.broadcasted_iota(jnp.int32, (1, NB), 1) // LEAF
    for j in range(NB // LEAF):
        sl = pl.ds(j * LEAF, LEAF)
        leaves = [leaf_inverse(a_ref[d, sl, sl]) for d in range(docs)]
        for d in range(docs):
            p = leaves[d]
            mine = lanes == j
            row = dot_hi(p, a_ref[d, sl, :], 1, 0)
            wide = jnp.concatenate([p] * (NB // LEAF), 1)
            row = jnp.where(mine, wide, row)
            col = a_ref[d, :, sl]
            rest = jnp.where(mine, 0.0, a_ref[d])
            a_ref[d] = rest - dot_hi(col, row, 1, 0)
            a_ref[d, sl, :] = row
    for d in range(docs):
        x = a_ref[d]
        carry_ref[d] = dot_hi(x, carry_ref[d], 1, 0)
        data_ref[d] = dot_hi(x, fresh, 1, 0)

def memory_maps(sticky):
    docs = sticky.shape[0]
    return pl.pallas_call(functools.partial(maps_kernel, docs),
        out_shape=[jax.ShapeDtypeStruct((docs, NB, NB), F32), jax.ShapeDtypeStruct((docs, NB, L), F32)],
        scratch_shapes=[pltpu.VMEM((docs, NB, NB), F32)],
        compiler_params=pltpu.CompilerParams(vmem_limit_bytes=32 << 20),
        cost_estimate=pl.CostEstimate(flops=docs * 10**10, bytes_accessed=docs * 10**6, transcendentals=0),
    )(sticky)


def nt(a, b):
    return lax.dot_general(a, b, (((1,), (1,)), ((), ())), preferred_element_type=F32)

def tn(a, b):
    return lax.dot_general(a, b, (((0,), (0,)), ((), ())), preferred_element_type=F32)

def nn(a, b):
    return jnp.dot(a, b, preferred_element_type=F32)

def head_lanes(h):
    return lax.broadcasted_iota(jnp.int32, (1, 2 * HD), 1) // HD == h

def causal():
    half = L // 2
    return lax.broadcasted_iota(jnp.int32, (half, half), 0) <= lax.broadcasted_iota(jnp.int32, (half, half), 1)

def attend_core(q_ref, k_ref, v_ref, mk_ref, mv_ref, out_ref, peak_ref):
    half = L // 2
    q = q_ref[...]; k = k_ref[...]; v = v_ref[...]; mk = mk_ref[...]; mv = mv_ref[...]
    seen = causal()
    outs = []
    for h in range(2):
        qh = jnp.where(head_lanes(h), q, jnp.zeros_like(q))
        s00 = jnp.where(seen, nt(k[:half], qh[:half]), -1e30)
        s01 = nt(k[:half], qh[half:])
        s11 = jnp.where(seen, nt(k[half:], qh[half:]), -1e30)
        sm = nt(mk, qh)
        sides = []
        for side, parts in enumerate(([s00, sm[:, :half]], [s01, s11, sm[:, half:]])):
            peak = functools.reduce(jnp.maximum, [jnp.max(p, 0, keepdims=True) for p in parts])
            ps = [jnp.exp2((p - peak) * EXP2_SCALE) for p in parts]
            total = functools.reduce(jnp.add, [jnp.sum(p, 0, keepdims=True) for p in ps])
            vs = [v[:half], mv] if side == 0 else [v[:half], v[half:], mv]
            o = functools.reduce(jnp.add, [tn(a, p.astype(BF16)) for a, p in zip(vs, ps)])
            sides.append(o * (1.0 / total))
            peak_ref[h, pl.ds(side * half, half)] = (peak * EXP2_SCALE + jnp.log2(total))[0]
        outs.append(jnp.concatenate(sides, 1))
    lanes = lax.broadcasted_iota(jnp.int32, (2 * HD, 1), 0) // HD == 0
    out_ref[...] = jnp.where(lanes, outs[0], outs[1]).T.astype(BF16)


def attend_tokens(q_ref, k_ref, v_ref, out_ref, peak_ref, total_ref):
    half = L // 2
    q = q_ref[...]
    k = k_ref[...]
    v = v_ref[...]
    seen = causal()
    outs = []
    for h in range(2):
        qh = jnp.where(head_lanes(h), q, jnp.zeros_like(q))
        s00 = jnp.where(seen, nt(k[:half], qh[:half]), -1e30)
        s01 = nt(k[:half], qh[half:])
        s11 = jnp.where(seen, nt(k[half:], qh[half:]), -1e30)
        sides = []
        for side, parts in enumerate(([s00], [s01, s11])):
            peak = functools.reduce(jnp.maximum, [jnp.max(p, 0, keepdims=True) for p in parts])
            ps = [jnp.exp2((p - peak) * EXP2_SCALE) for p in parts]
            total = functools.reduce(jnp.add, [jnp.sum(p, 0, keepdims=True) for p in ps])
            vs = [v[:half], v[half:]]
            sides.append(functools.reduce(jnp.add, [tn(a, p.astype(BF16)) for a, p in zip(vs, ps)]))
            cols = pl.ds(side * half, half)
            peak_ref[h : h + 1, cols] = peak
            total_ref[h : h + 1, cols] = total
        outs.append(jnp.concatenate(sides, 1))
    lanes = lax.broadcasted_iota(jnp.int32, (2 * HD, 1), 0) // HD == 0
    out_ref[...] = jnp.where(lanes, outs[0], outs[1])


def attend_memory(q_ref, mk_ref, mv_ref, tokens_ref, peak_ref, total_ref, out_ref, lse_ref):
    q = q_ref[...]
    mk = mk_ref[...]
    mv = mv_ref[...]
    lanes = lax.broadcasted_iota(jnp.int32, (2 * HD, 1), 0) // HD == 0
    found = []
    for h in range(2):
        s = nt(mk, jnp.where(head_lanes(h), q, jnp.zeros_like(q)))
        old = peak_ref[h : h + 1]
        peak = jnp.maximum(old, jnp.max(s, 0, keepdims=True))
        p = jnp.exp2((s - peak) * EXP2_SCALE)
        shrink = jnp.exp2((old - peak) * EXP2_SCALE)
        total = total_ref[h : h + 1] * shrink + jnp.sum(p, 0, keepdims=True)
        lse_ref[h : h + 1] = peak * EXP2_SCALE + jnp.log2(total)
        rate = 1.0 / total
        found.append((tn(mv, p.astype(BF16)) * rate, shrink * rate))
    (o0, r0), (o1, r1) = found
    out_ref[...] = (jnp.where(lanes, o0, o1) + tokens_ref[...] * jnp.where(lanes, r0, r1)).T.astype(BF16)


def attend_kernel(q_ref, k_ref, v_ref, mk_ref, mv_ref, out_ref, peak_ref):
    attend_core(*(r.at[0] for r in (q_ref, k_ref, v_ref, mk_ref, mv_ref, out_ref)), peak_ref.at[0, 0])

def attend(qkv, mem):
    docs, _, w3 = qkv.shape
    w = w3 // 3
    pairs = w // 128
    tok = lambda o: pl.BlockSpec((1, L, 128), lambda d, i: (d, 0, o * pairs + i))
    me = lambda o: pl.BlockSpec((1, NB, 128), lambda d, i: (d, 0, o * pairs + i))
    return pl.pallas_call(attend_kernel, grid=(docs, pairs),
        in_specs=[tok(0), tok(1), tok(2), me(0), me(1)],
        out_specs=[tok(0), pl.BlockSpec((1, 1, 2, L), lambda d, i: (d, i, 0, 0))],
        out_shape=[jax.ShapeDtypeStruct((docs, L, w), BF16), jax.ShapeDtypeStruct((docs, pairs, 2, L), F32)],
        compiler_params=pltpu.CompilerParams(vmem_limit_bytes=48 << 20),
        cost_estimate=pl.CostEstimate(flops=docs * pairs * 8 * 768 * 512 * 128, bytes_accessed=docs * L * w * 10, transcendentals=docs * 12 * 768 * 512),
    )(qkv, qkv, qkv, mem, mem)

def grads_core(q_ref, k_ref, v_ref, mk_ref, mv_ref, g_ref, o_ref, peak_ref, dtok_ref, dmem_ref):
    half = L // 2
    q = q_ref[0]; k = k_ref[0]; v = v_ref[0]; mk = mk_ref[0]; mv = mv_ref[0]; g = g_ref[0]
    scale = HD ** -0.5
    seen = causal()
    go = g.astype(F32) * o_ref[0].astype(F32)
    pick = (lax.broadcasted_iota(jnp.int32, (8, 2 * HD), 1) // HD == lax.broadcasted_iota(jnp.int32, (8, 2 * HD), 0)).astype(F32)
    delta = lax.dot_general(pick, go, (((1,), (1,)), ((), ())), precision=lax.Precision.HIGHEST, preferred_element_type=F32)
    first = head_lanes(0)
    res = []
    for h in range(2):
        mine = head_lanes(h)
        qh = jnp.where(mine, q, jnp.zeros_like(q))
        gh = jnp.where(mine, g, jnp.zeros_like(g))
        lse = peak_ref[0, 0, pl.ds(h, 1), :]
        dh = delta[h:h + 1]
        def tile(kk, vv, lo, hi, mask):
            s = nt(kk, qh[lo:hi])
            p = jnp.exp2(s * EXP2_SCALE - lse[:, lo:hi])
            if mask:
                p = jnp.where(seen, p, 0.0)
            dp = nt(vv, gh[lo:hi])
            return p.astype(BF16), (p * (dp - dh[:, lo:hi])).astype(BF16)
        p00, t00 = tile(k[:half], v[:half], 0, half, True)
        p01, t01 = tile(k[:half], v[:half], half, L, False)
        p11, t11 = tile(k[half:], v[half:], half, L, True)
        pm, tm = tile(mk, mv, 0, L, False)
        dv0 = nn(p00, g[:half]) + nn(p01, g[half:])
        dv1 = nn(p11, g[half:])
        dvm = nn(pm, g)
        dk0 = nn(t00, q[:half]) + nn(t01, q[half:])
        dk1 = nn(t11, q[half:])
        dkm = nn(tm, q)
        dq0 = tn(k[:half], t00) + tn(mk, tm[:, :half])
        dq1 = tn(k[:half], t01) + tn(k[half:], t11) + tn(mk, tm[:, half:])
        res.append((jnp.concatenate([dq0, dq1], 1), jnp.concatenate([dk0, dk1], 0), jnp.concatenate([dv0, dv1], 0), dkm, dvm))
    rows = lax.broadcasted_iota(jnp.int32, (2 * HD, 1), 0) // HD == 0
    dq = (jnp.where(rows, res[0][0], res[1][0]).T * scale).astype(BF16)
    dk, dv, dkm, dvm = [jnp.where(first, a, b) for a, b in zip(res[0][1:], res[1][1:])]
    dk = (dk * scale).astype(BF16); dkm = (dkm * scale).astype(BF16)
    dv = dv.astype(BF16); dvm = dvm.astype(BF16)
    dtok_ref[0, 0] = dq; dtok_ref[1, 0] = dk; dtok_ref[2, 0] = dv
    dmem_ref[0, 0] = dkm; dmem_ref[1, 0] = dvm
    qs = jnp.sum(dq.astype(F32), 0, keepdims=True)
    vs = jnp.sum(dv.astype(F32), 0, keepdims=True) + jnp.sum(dvm.astype(F32), 0, keepdims=True)
    return qs, vs


def grads_kernel(*refs):
    qs, vs = grads_core(*refs[:-1])
    r = lax.broadcasted_iota(jnp.int32, (8, 128), 0)
    refs[-1][0] = jnp.where(r == 0, qs, jnp.where(r == 1, vs, 0.0))

def attend_grads(qkv, mem, g, mixed, lse):
    docs, _, w3 = qkv.shape
    w = w3 // 3
    pairs = w // 128
    tok = lambda o: pl.BlockSpec((1, L, 128), lambda d, i: (d, 0, o * pairs + i))
    me = lambda o: pl.BlockSpec((1, NB, 128), lambda d, i: (d, 0, o * pairs + i))
    return pl.pallas_call(grads_kernel, grid=(docs, pairs),
        in_specs=[tok(0), tok(1), tok(2), me(0), me(1), tok(0), tok(0), pl.BlockSpec((1, 1, 2, L), lambda d, i: (d, i, 0, 0))],
        out_specs=[pl.BlockSpec((3, 1, L, 128), lambda d, i: (0, d, 0, i)), pl.BlockSpec((2, 1, NB, 128), lambda d, i: (0, d, 0, i)), pl.BlockSpec((1, 8, 128), lambda d, i: (d, 0, i))],
        out_shape=[jax.ShapeDtypeStruct((3, docs, L, w), BF16), jax.ShapeDtypeStruct((2, docs, NB, w), BF16), jax.ShapeDtypeStruct((docs, 8, w), F32)],
        compiler_params=pltpu.CompilerParams(vmem_limit_bytes=48 << 20),
        cost_estimate=pl.CostEstimate(flops=docs * pairs * 20 * 768 * 512 * 128, bytes_accessed=docs * L * w * 16, transcendentals=docs * 12 * 768 * 512),
    )(qkv, qkv, qkv, mem, mem, g, mixed, lse)


def mm(a, b):
    return jnp.dot(a, b, preferred_element_type=F32)


def normalised(values):
    center = jnp.mean(values, -1, keepdims=True)
    shifted = values - center
    rate = lax.rsqrt(jnp.mean(shifted * shifted, -1, keepdims=True) + EPSILON)
    return shifted * rate, rate


def norm_back(unit, rate, scaled_grad):
    inner = jnp.mean(scaled_grad * unit, -1, keepdims=True)
    return rate * (scaled_grad - jnp.mean(scaled_grad, -1, keepdims=True) - unit * inner)


def whole(shape):
    return pl.BlockSpec(shape, lambda *_: (0,) * len(shape), pipeline_mode=pl.Buffered(1))


def col_sums(values):
    return jnp.sum(values, 0, keepdims=True)


def project_kernel(x_ref, w_ref, bias_ref, gain_ref, offset_ref, hidden_ref, qkv_ref):
    unit, _ = normalised(x_ref[0].astype(F32))
    hidden = (unit * gain_ref[...] + offset_ref[...]).astype(BF16)
    hidden_ref[0] = hidden
    qkv_ref[0] = (mm(hidden, w_ref[...]) + bias_ref[...]).astype(BF16)


def project(x, w_qkv, bias, gain, offset):
    docs, _, w = x.shape
    tile = 256
    rows = lambda c: pl.BlockSpec((1, tile, c), lambda d, i: (d, i, 0))
    return pl.pallas_call(
        project_kernel,
        grid=(docs, L // tile),
        in_specs=[rows(w), whole(w_qkv.shape), whole((1, 3 * w)), whole((1, w)), whole((1, w))],
        out_specs=[rows(w), rows(3 * w)],
        out_shape=[jax.ShapeDtypeStruct((docs, L, w), BF16), jax.ShapeDtypeStruct((docs, L, 3 * w), BF16)],
        compiler_params=pltpu.CompilerParams(vmem_limit_bytes=40 << 20),
        cost_estimate=pl.CostEstimate(flops=docs * L * w * w * 6, bytes_accessed=docs * L * w * 10, transcendentals=0),
    )(x, w_qkv, bias[None], gain[None], offset[None])


def renew_kernel(carry_ref, data_ref, memory_ref, hidden_ref, out_ref):
    out_ref[0] = dot_hi(carry_ref[0], memory_ref[0], 1, 0) + dot_hi(data_ref[0], hidden_ref[0].astype(F32), 1, 0)


def renew(carry_map, data_map, memory, hidden):
    docs, _, w = hidden.shape
    one = lambda r, c: pl.BlockSpec((1, r, c), lambda d: (d, 0, 0))
    return pl.pallas_call(
        renew_kernel,
        grid=(docs,),
        in_specs=[one(NB, NB), one(NB, L), one(NB, w), one(L, w)],
        out_specs=one(NB, w),
        out_shape=jax.ShapeDtypeStruct((docs, NB, w), F32),
        compiler_params=pltpu.CompilerParams(vmem_limit_bytes=40 << 20),
        cost_estimate=pl.CostEstimate(flops=docs * 6 * NB * 768 * w * 2, bytes_accessed=docs * NB * w * 8, transcendentals=0),
    )(carry_map, data_map, memory, hidden)


def recall_kernel(memory_ref, w_ref, bias_ref, low_ref, out_ref):
    low = memory_ref[...].astype(BF16)
    low_ref[...] = low
    out_ref[...] = (mm(low, w_ref[...]) + bias_ref[...]).astype(BF16)


def recall(memory, w_qkv, bias):
    rows, w = memory.shape
    tile = w
    return pl.pallas_call(
        recall_kernel,
        grid=(2,),
        in_specs=[whole((rows, w)), pl.BlockSpec((w, tile), lambda i: (0, 1 + i)), pl.BlockSpec((1, tile), lambda i: (0, 1 + i))],
        out_specs=[pl.BlockSpec((rows, w), lambda i: (0, 0)), pl.BlockSpec((rows, tile), lambda i: (0, i))],
        out_shape=[jax.ShapeDtypeStruct((rows, w), BF16), jax.ShapeDtypeStruct((rows, 2 * w), BF16)],
        compiler_params=pltpu.CompilerParams(vmem_limit_bytes=40 << 20),
        cost_estimate=pl.CostEstimate(flops=rows * w * w * 4, bytes_accessed=rows * w * 10, transcendentals=0),
    )(memory, w_qkv, bias[None])


GELU_RATE = 0.7978845608028654
GELU_CUBE = 0.044715


def feed_core(x_ref, mixed_ref, cot_ref, w_out_ref, w_in_ref, w_back_ref, vectors, in_bias,
              result_ref, normed_ref, act_ref, pre_ref, rgrad_ref, branch_ref, mgrad_ref):
    out_bias, back_bias, gain, offset = (ref[...] for ref in vectors)
    cot = cot_ref[...]
    residual = x_ref[...].astype(F32) + (mm(mixed_ref[...], w_out_ref[...]) + out_bias)
    unit, rate = normalised(residual)
    normed = (unit * gain + offset).astype(BF16)
    normed_ref[...] = normed
    result = residual + back_bias
    ngrad = None
    chunk = 768
    wide = []
    for c in range(0, w_in_ref.shape[1], chunk):
        sl = pl.ds(c, chunk)
        v = mm(normed, w_in_ref[:, sl]) + in_bias(c // chunk)
        square = v * v
        t = jnp.tanh(GELU_RATE * v * (1.0 + GELU_CUBE * square))
        half = 0.5 * (1.0 + t)
        act = (v * half).astype(BF16)
        slope = half + (0.5 * GELU_RATE) * v * (1.0 - t * t) * (1.0 + 3.0 * GELU_CUBE * square)
        act_ref[:, sl] = act
        result = result + mm(act, w_back_ref[sl, :])
        pre = (nt(cot, w_back_ref[sl, :]) * slope).astype(BF16)
        pre_ref[:, sl] = pre
        wide.append(col_sums(pre.astype(F32)))
        part = nt(pre, w_in_ref[:, sl])
        ngrad = part if ngrad is None else ngrad + part
    result_ref[...] = result.astype(BF16)
    rgrad = cot.astype(F32) + norm_back(unit, rate, ngrad * gain)
    rgrad_ref[...] = rgrad
    branch = rgrad.astype(BF16)
    branch_ref[...] = branch
    mgrad_ref[...] = nt(branch, w_out_ref[...]).astype(BF16)
    sums = [col_sums(cot.astype(F32)), col_sums(branch.astype(F32)), col_sums(ngrad * unit), col_sums(ngrad)]
    return wide, sums


def feed_kernel(x_ref, mixed_ref, cot_ref, w_out_ref, w_in_ref, w_back_ref, rows_ref, in_bias_ref, *out_refs):
    vectors = [rows_ref.at[pl.ds(i, 1)] for i in range(4)]
    in_bias = lambda k: in_bias_ref[:, pl.ds(k * 768, 768)]
    wide, sums = feed_core(x_ref, mixed_ref, cot_ref, w_out_ref, w_in_ref, w_back_ref, vectors, in_bias, *out_refs[:7])
    wide_ref, sums_ref = out_refs[7:]
    w = x_ref.shape[1]
    sums = jnp.concatenate(sums + [jnp.zeros((4, w), F32)], 0)
    wide = jnp.concatenate(wide, 1)

    @pl.when(pl.program_id(0) == 0)
    def _():
        sums_ref[...] = sums
        wide_ref[...] = wide

    @pl.when(pl.program_id(0) > 0)
    def _():
        sums_ref[...] += sums
        wide_ref[...] += wide


def feed(x, mixed, cot, w_out, w_in, w_back, rows4, in_bias):
    n, w = x.shape
    ff = w_in.shape[1]
    tile = 256
    rows = lambda c: pl.BlockSpec((tile, c), lambda i: (i, 0))
    arr = lambda c, t: jax.ShapeDtypeStruct((n, c), t)
    return pl.pallas_call(
        feed_kernel,
        grid=(n // tile,),
        in_specs=[rows(w), rows(w), rows(w), whole(w_out.shape), whole(w_in.shape), whole(w_back.shape), whole((4, w)), whole((1, ff))],
        out_specs=[rows(w), rows(w), rows(ff), rows(ff), rows(w), rows(w), rows(w),
                   pl.BlockSpec((1, ff), lambda i: (0, 0)), pl.BlockSpec((8, w), lambda i: (0, 0))],
        out_shape=[arr(w, BF16), arr(w, BF16), arr(ff, BF16), arr(ff, BF16), arr(w, F32), arr(w, BF16), arr(w, BF16),
                   jax.ShapeDtypeStruct((1, ff), F32), jax.ShapeDtypeStruct((8, w), F32)],
        compiler_params=pltpu.CompilerParams(vmem_limit_bytes=56 << 20),
        cost_estimate=pl.CostEstimate(flops=n * (4 * w * ff + 2 * w * w) * 2, bytes_accessed=n * ff * 4 + 2 * w * ff * 4, transcendentals=n * ff),
    )(x, mixed, cot, w_out, w_in, w_back, rows4, in_bias[None])


def local_kernel(g_ref, w_ref, out_ref):
    part = nt(g_ref[0], w_ref[...])

    @pl.when(pl.program_id(0) == 0)
    def _():
        out_ref[...] = part

    @pl.when(pl.program_id(0) == 1)
    def _():
        out_ref[...] += part


def local_memory_grad(memory_proj, w_qkv):
    _, rows, w = memory_proj.shape
    return pl.pallas_call(
        local_kernel,
        grid=(2,),
        in_specs=[pl.BlockSpec((1, rows, w), lambda i: (i, 0, 0)), pl.BlockSpec((w, w), lambda i: (0, 1 + i))],
        out_specs=pl.BlockSpec((rows, w), lambda i: (0, 0)),
        out_shape=jax.ShapeDtypeStruct((rows, w), F32),
        compiler_params=pltpu.CompilerParams(vmem_limit_bytes=40 << 20),
        cost_estimate=pl.CostEstimate(flops=rows * w * w * 4, bytes_accessed=rows * w * 10, transcendentals=0),
    )(memory_proj, w_qkv)


def entry_kernel(x_ref, rgrad_ref, proj_ref, data_ref, inc_ref, w_ref, gain_ref, out_ref, sums_ref):
    w = x_ref.shape[2]
    hgrad = dot_hi(data_ref[0], inc_ref[0], 0, 0)
    for p in range(3):
        hgrad = hgrad + nt(proj_ref[p, 0], w_ref[:, pl.ds(p * w, w)])
    unit, rate = normalised(x_ref[0].astype(F32))
    out_ref[0] = (rgrad_ref[0] + norm_back(unit, rate, hgrad * gain_ref[...])).astype(BF16)
    sums = jnp.concatenate([col_sums(hgrad * unit), col_sums(hgrad), jnp.zeros((6, w), F32)], 0)
    start = (pl.program_id(0) == 0) & (pl.program_id(1) == 0)

    @pl.when(start)
    def _():
        sums_ref[...] = sums

    @pl.when(jnp.logical_not(start))
    def _():
        sums_ref[...] += sums


def entry_grads(x, rgrad, token_proj, data_map, incoming, w_qkv, gain):
    docs, _, w = x.shape
    tile = 256
    rows = pl.BlockSpec((1, tile, w), lambda d, i: (d, i, 0))
    return pl.pallas_call(
        entry_kernel,
        grid=(docs, L // tile),
        in_specs=[rows, rows, pl.BlockSpec((3, 1, tile, w), lambda d, i: (0, d, i, 0)),
                  pl.BlockSpec((1, NB, tile), lambda d, i: (d, 0, i)), pl.BlockSpec((1, NB, w), lambda d, i: (d, 0, 0)),
                  whole(w_qkv.shape), whole((1, w))],
        out_specs=[rows, pl.BlockSpec((8, w), lambda d, i: (0, 0))],
        out_shape=[jax.ShapeDtypeStruct((docs, L, w), BF16), jax.ShapeDtypeStruct((8, w), F32)],
        compiler_params=pltpu.CompilerParams(vmem_limit_bytes=40 << 20),
        cost_estimate=pl.CostEstimate(flops=docs * L * w * w * 6 + docs * L * NB * w * 12, bytes_accessed=docs * L * w * 14, transcendentals=0),
    )(x, rgrad, token_proj, data_map, incoming, w_qkv, gain[None])


MESH = pl.DeviceIdType.MESH
GROUPS = 3
STAGES = 5


AXES = ("z1", "z0", "x")


class Part:
    def __init__(self, me, held, out, cols, order, got, sems):
        self.me, self.held, self.out, self.got, self.sems = me, held, out, got, sems
        self.cols, self.order = cols, order
        self.stage = 0

    def span(self, which):
        count = self.held.shape[3] // 2
        return pl.ds(pl.multiple_of(which * count, 8), count)

    def at(self, axis, flip, index):
        done = self.order[: self.stage]
        where, free = [], 0
        for name in AXES:
            if name in done or name == axis:
                which = self.me[name]
                where.append(1 - which if flip and name == axis else which)
            elif index is None:
                where.append(slice(None))
            else:
                where.append(index[free])
                free += 1
        rows = slice(None)
        if "seg" in done or axis == "seg":
            which = self.me["seg"]
            rows = self.span(1 - which if flip and axis == "seg" else which)
        return self.held.at[(*where, rows, pl.ds(*self.cols))]

    def send(self):
        last = self.stage == 4
        to = "seg" if last else self.order[self.stage]
        source = self.at(None if last else to, not last, None)
        target = self.out.at[self.span(self.me["seg"]), pl.ds(*self.cols)] if last else self.got[self.stage]
        send, recv, local = self.sems
        self.copy = pltpu.make_async_remote_copy(
            src_ref=source, dst_ref=target, send_sem=send.at[self.stage], recv_sem=recv.at[self.stage],
            device_id=self.me["ids"][to], device_id_type=MESH)
        self.copy.start()
        if last:
            self.own = pltpu.make_async_copy(source, target, local)
            self.own.start()

    def advance(self):
        self.copy.wait()
        if self.stage == 4:
            self.own.wait()
            return
        got = self.got[self.stage]
        axis = self.order[self.stage]
        lead = len(got.shape) - 2

        def add(i, _):
            index = tuple((i >> (lead - 1 - k)) & 1 for k in range(lead))
            ref = self.at(axis, False, index)
            ref[...] += got[index]
            return 0

        lax.fori_loop(0, 1 << lead, add, 0)
        self.stage += 1
        self.send()


ORDERS = {
    "A": ("x", "seg", "z0", "z1"),
    "B": ("seg", "x", "z0", "z1"),
    "C": ("z0", "x", "seg", "z1"),
    "D": ("x", "z0", "seg", "z1"),
    "E": ("z0", "seg", "x", "z1"),
    "F": ("x", "z0", "z1", "seg"),
    "H": ("z0", "x", "z1", "seg"),
    "I": ("seg", "z0", "x", "z1"),
}
UNIT = 384
PLAN = ((("D", 4), ("I", 4)), (("H", 4), ("A", 4)), (("C", 4), ("A", 4)))
SCRIPT = (
    "back", "in", "att0", "1D", "1I", "att1", "local", "2H", "2A", "three",
    "1D", "1I", "entry", "1D", "1I", "2H", "2A", "3C", "s1",
    "3A", "3C", "3A", "1D", "1I", "s2", "2A", "3C", "1D", "1I",
    "2H", "s3", "2H", "3A", "2A", "2H", "3C", "s4", "2A", "3A",
    "3C", "3A", "s5",
)


def landing(rows, cols, order):
    shapes = []
    for stage, axis in enumerate(order):
        done = order[: stage + 1]
        lead = sum(name not in done for name in AXES)
        shapes.append((2,) * lead + (rows // 2 if "seg" in done else rows, cols))
    return [pltpu.VMEM(shape, F32) for shape in shapes]


def tail_kernel(docs, bits, *refs):
    (act, cot, normed, pre, qkv, mem, mgrad, mixed, lse, hidden, mem_rows, mixed_rows, branch, w_qkv, x, rgrad,
     data_map, carry_map, has, vec, small_in) = refs[:21]
    o_back, o_in, o_three, o_input, o_start, small, tok, memp = refs[21:29]
    h1, h2, h3, rc, slots, slot1, acc1, acc2, lg, inc, rsmall = refs[29:40]
    count = sum(len(p) for p in PLAN)
    gots = refs[40 : 40 + count * 4]
    send, recv, local, csend, crecv, misc_send, misc_recv, ssend, srecv, credit = refs[40 + count * 4 :]
    b, s = lax.axis_index("batch"), lax.axis_index("seg")
    n, w = cot.shape
    ff = act.shape[1]

    def flip(distance):
        return b + distance * (1 - 2 * ((b // distance) % 2))

    ids = {"core": (flip(1), s), "x": (flip(2), s), "z0": (flip(4), s), "z1": (flip(8), s), "seg": (b, 1 - s)}
    me = {"core": b % 2, "x": (b // 2) % 2, "z0": (b // 4) % 2, "z1": (b // 8) % 2, "seg": s, "ids": ids}
    mine = me["core"]

    @pl.when(s == 1)
    def _():
        inc[...] = jnp.zeros_like(inc)

    small[...] = small_in[...]
    barrier = pltpu.get_barrier_semaphore()
    for who in ids.values():
        pl.semaphore_signal(barrier, inc=1, device_id=who, device_id_type=MESH)
    pl.semaphore_wait(barrier, len(ids))

    def core_copy(g, i, slot, target):
        return pltpu.make_async_remote_copy(
            src_ref=slot, dst_ref=target, send_sem=csend.at[g, i], recv_sem=crecv.at[g, i], device_id=ids["core"], device_id_type=MESH)

    parts = {}
    for g, held in enumerate((h1, h2, h3)):
        first = 0
        for kind, units in PLAN[g]:
            i = len(parts)
            sems = (send.at[i], recv.at[i], local.at[i])
            out = (o_back, o_in, o_three)[g]
            parts[str(g + 1) + kind] = Part(me, held, out, (first, units * UNIT), ORDERS[kind], gots[4 * i : 4 * i + 4], sems)
            first += units * UNIT

    def send_group(g):
        for name, part in parts.items():
            if name[0] == str(g + 1):
                part.send()

    own2 = w // 16

    def core_slice(g, i, tile):
        cols = pl.ds(pl.multiple_of(i * tile, 128), tile)
        return core_copy(g, i, slots.at[i % 2, :, :, pl.ds(0, tile)], rc.at[:, :, cols])

    def pass_rows(g, i, held, tile):
        cols = pl.ds(pl.multiple_of(i * tile, 128), tile)

        @pl.when(i >= 2)
        def _():
            core_slice(g, i - 2, tile).wait_send()

        for k in range(8):
            slots[i % 2, k, :, 0:tile] = acc2[pl.ds(pl.multiple_of((2 * k + 1 - mine) * own2, 8), own2), 0:tile]
        core_slice(g, i, tile).start()
        for k in range(8):
            held[k // 4, k // 2 % 2, k % 2, :, cols] = acc2[pl.ds(pl.multiple_of((2 * k + mine) * own2, 8), own2), 0:tile]

    def took_core(g, copy, steps, held):
        copy(steps - 2).wait_send()
        copy(steps - 1).wait_send()

        def took(i, _):
            copy(i).wait_recv()
            return 0

        def add(k, _):
            held[k // 4, k // 2 % 2, k % 2] += rc[k]
            return 0

        lax.fori_loop(0, steps, took, 0)
        lax.fori_loop(0, 8, add, 0)
        if g < 2:
            pl.semaphore_signal(credit, inc=1, device_id=ids["core"], device_id_type=MESH)
        send_group(g)

    own1 = ff // 16

    def copy1(i):
        return core_copy(0, i, slot1.at[i % 2], rc.at[i])

    def back_body(act_ref, cot_ref):
        i = pl.program_id(0)
        acc1[...] = tn(act_ref[...], cot_ref[...])

        @pl.when(i >= 2)
        def _():
            copy1(i - 2).wait_send()

        for q in range(own1 // own2):
            cols = pl.ds(q * w, w)
            slot1[i % 2, :, cols] = acc1[pl.ds(pl.multiple_of((1 - mine) * own1 + q * own2, 8), own2)]
        copy1(i).start()
        for q in range(own1 // own2):
            cols = pl.ds(q * w, w)
            h1[i // 4, i // 2 % 2, i % 2, :, cols] = acc1[pl.ds(pl.multiple_of(mine * own1 + q * own2, 8), own2)]

    def do_back():
        pltpu.emit_pipeline(
            back_body, grid=(8,),
            in_specs=[pl.BlockSpec((n, 2 * own1), lambda i: (0, i)), pl.BlockSpec((n, w), lambda i: (0, 0))],
            out_specs=[],
        )(act, cot)
        took_core(0, copy1, 8, h1)

    tile2 = acc2.shape[1]

    def in_body(normed_ref, pre_ref):
        acc2[...] = tn(normed_ref[...], pre_ref[...])
        pass_rows(1, pl.program_id(0), h2, tile2)

    def do_in():
        pl.semaphore_wait(credit, 1)
        pltpu.emit_pipeline(
            in_body, grid=(ff // tile2,),
            in_specs=[pl.BlockSpec((n, w), lambda i: (0, 0)), pl.BlockSpec((n, tile2), lambda i: (0, i))],
            out_specs=[],
        )(normed, pre)
        took_core(1, lambda i: core_slice(1, i, tile2), ff // tile2, h2)

    pairs = w // 128

    def attention(doc):
        def body(*r):
            cols = pl.ds(pl.multiple_of(pl.program_id(0) * 128, 128), 128)
            qs, vs = grads_core(*r)
            small[0:1, cols] += qs
            small[1:2, cols] += vs

        t = lambda o: pl.BlockSpec((1, L, 128), lambda i: (doc, 0, o * pairs + i))
        m = lambda o: pl.BlockSpec((1, NB, 128), lambda i: (doc, 0, o * pairs + i))
        pltpu.emit_pipeline(
            body, grid=(pairs,),
            in_specs=[t(0), t(1), t(2), m(0), m(1), t(0), t(0), pl.BlockSpec((1, 1, 2, L), lambda i: (doc, i, 0, 0))],
            out_specs=[pl.BlockSpec((3, 1, L, 128), lambda i: (0, doc, 0, i)), pl.BlockSpec((2, 1, NB, 128), lambda i: (0, doc, 0, i))],
        )(qkv, qkv, qkv, mem, mem, mgrad, mixed, lse, tok, memp)

    def local_body(g_ref, w_ref):
        total = None
        for d in range(docs):
            part = nt(g_ref[0, d], w_ref[...])
            rows = pl.ds(d * NB, NB)

            @pl.when(pl.program_id(0) == 0)
            def _():
                lg[rows] = part

            @pl.when(pl.program_id(0) == 1)
            def _():
                lg[rows] += part

    def do_local():
        pltpu.emit_pipeline(
            local_body, grid=(2,),
            in_specs=[pl.BlockSpec((1, docs, NB, w), lambda i: (i, 0, 0, 0)), pl.BlockSpec((w, w), lambda i: (0, 1 + i))],
            out_specs=[],
        )(memp, w_qkv)

    upward = pltpu.make_async_remote_copy(
        src_ref=lg, dst_ref=inc, send_sem=misc_send.at[0], recv_sem=misc_recv.at[0], device_id=ids["seg"], device_id_type=MESH)

    def begin_upward():
        @pl.when(s == 1)
        def _():
            upward.start()

    tile3 = w
    per = w // tile3
    m = mem_rows.shape[0]

    def three_body(hidden_ref, mem_ref, mixed_ref, tok_ref, memg_ref, branch_ref):
        part = pl.program_id(0)

        @pl.when(part == 0)
        def _():
            acc2[:, 0:tile3] = sum(tn(hidden_ref[d], tok_ref[0, d]) for d in range(docs))

        @pl.when((part == 1) | (part == 2))
        def _():
            acc2[:, 0:tile3] = sum(tn(hidden_ref[d], tok_ref[0, d]) + tn(mem_ref[d], memg_ref[0, d]) for d in range(docs))

        @pl.when(part == 3)
        def _():
            acc2[:, 0:tile3] = tn(mixed_ref[...], branch_ref[...])

        pass_rows(2, part * per + pl.program_id(1), h3, tile3)

    def do_three():
        pl.semaphore_wait(credit, 1)
        pltpu.emit_pipeline(
            three_body, grid=(4, per),
            in_specs=[pl.BlockSpec((docs, L, w), lambda p, i: (0, 0, 0)), pl.BlockSpec((docs, NB, w), lambda p, i: (0, 0, 0)),
                      pl.BlockSpec((n, w), lambda p, i: (0, 0)),
                      pl.BlockSpec((1, docs, L, tile3), lambda p, i: (jnp.minimum(p, 2), 0, 0, jnp.where(p < 3, i, per - 1))),
                      pl.BlockSpec((1, docs, NB, tile3), lambda p, i: (jnp.clip(p - 1, 0, 1), 0, 0, jnp.where(p < 1, 0, jnp.where(p < 3, i, per - 1)))),
                      pl.BlockSpec((n, tile3), lambda p, i: (0, jnp.where(p < 3, 0, i)))],
            out_specs=[],
        )(hidden, mem_rows, mixed_rows, tok, memp, branch)
        took_core(2, lambda i: core_slice(2, i, tile3), 4 * per, h3)

    tile4 = 256

    def entry_body(x_ref, rgrad_ref, proj_ref, data_ref, w_ref, out_ref):
        d = pl.program_id(0)
        hgrad = dot_hi(data_ref[0], inc[pl.ds(pl.multiple_of(d * NB, NB), NB)], 0, 0)
        for p in range(3):
            hgrad = hgrad + nt(proj_ref[p, 0], w_ref[:, pl.ds(p * w, w)])
        unit, rate = normalised(x_ref[0].astype(F32))
        out_ref[0] = (rgrad_ref[0] + norm_back(unit, rate, hgrad * vec[4:5])).astype(BF16)
        small[4:5] += col_sums(hgrad * unit)
        small[5:6] += col_sums(hgrad)

    rows4 = pl.BlockSpec((1, tile4, w), lambda d, i: (d, i, 0))
    def do_entry():
        @pl.when(s == 0)
        def _():
            upward.wait_recv()

        pltpu.emit_pipeline(
            entry_body, grid=(docs, L // tile4),
            in_specs=[rows4, rows4, pl.BlockSpec((3, 1, tile4, w), lambda d, i: (0, d, i, 0)),
                      pl.BlockSpec((1, NB, tile4), lambda d, i: (d, 0, i)), pl.BlockSpec((w, 3 * w), lambda d, i: (0, 0))],
            out_specs=[rows4],
        )(x, rgrad, tok, data_map, w_qkv, o_input)

    def add_small(k, to):
        copy = pltpu.make_async_remote_copy(
            src_ref=small, dst_ref=rsmall.at[k], send_sem=ssend.at[k], recv_sem=srecv.at[k], device_id=ids[to], device_id_type=MESH)
        copy.start()
        return copy

    def took_small(k, copy):
        copy.wait()
        small[...] += rsmall[k]

    def start_body(carry_ref):
        d = pl.program_id(0)
        rows = pl.ds(pl.multiple_of(d * NB, NB), NB)
        lg[rows] = has[d].astype(F32) * (lg[rows] + dot_hi(carry_ref[0], inc[rows], 0, 0))

    half = w // 2
    stay = pltpu.make_async_copy(lg.at[:, pl.ds(0, half)], o_start, misc_send.at[1])
    leave = pltpu.make_async_remote_copy(
        src_ref=lg.at[:, pl.ds(half, half)], dst_ref=o_start, send_sem=misc_send.at[2], recv_sem=misc_recv.at[1],
        device_id=ids["seg"], device_id_type=MESH)

    def do_start():
        @pl.when(s == 1)
        def _():
            upward.wait_send()

        pltpu.emit_pipeline(
            start_body, grid=(docs,),
            in_specs=[pl.BlockSpec((1, NB, NB), lambda d: (d, 0, 0))],
            out_specs=[],
        )(carry_map)

        @pl.when(s == 0)
        def _():
            stay.start()
            leave.start()

    links = ("core", "x", "seg", "z0", "z1")
    for step in SCRIPT:
        if step == "back":
            do_back()
        elif step == "in":
            do_in()
        elif step[:3] == "att":
            attention(int(step[3:]))
        elif step == "local":
            do_local()
            begin_upward()
        elif step == "three":
            do_three()
        elif step == "entry":
            do_entry()
            tiny = add_small(0, "core")
            do_start()
        elif step[0] == "s":
            k = int(step[1])
            took_small(k - 1, tiny)
            if k < 5:
                tiny = add_small(k, links[k])
        else:
            parts[step].advance()

    @pl.when(s == 0)
    def _():
        stay.wait()
        leave.wait_send()

    @pl.when(s == 1)
    def _():
        leave.wait_recv()


def tail(docs, batch, act, cot, normed, pre, qkv, mem, mgrad, mixed, lse, hidden, mem_rows, branch, w_qkv, x, rgrad,
         data_map, carry_map, has, vec, small):
    n, w = cot.shape
    ff = act.shape[1]
    own1, own2 = ff // batch, w // batch
    ops = [act, cot, normed, pre, qkv, mem, mgrad, mixed, lse, hidden, mem_rows, mixed.reshape(n, w), branch, w_qkv, x, rgrad,
           data_map, carry_map, has, vec, small]
    anywhere = pl.BlockSpec(memory_space=pl.ANY)
    vmem = pl.BlockSpec(memory_space=pltpu.VMEM)
    f = lambda *shape: jax.ShapeDtypeStruct(shape, F32)
    outs = [f(own2, ff), f(own2, ff), f(own2, 4 * w), jax.ShapeDtypeStruct((docs, L, w), BF16), f(docs * NB, w // 2), f(16, w),
            jax.ShapeDtypeStruct((3, docs, L, w), BF16), jax.ShapeDtypeStruct((2, docs, NB, w), BF16)]
    held = [pltpu.VMEM((2, 2, 2, own2, ff), F32)] * GROUPS
    slots = [pltpu.VMEM((8, own2, ff), F32), pltpu.VMEM((2, 8, own2, w), F32), pltpu.VMEM((2, own2, ff), F32)]
    accs = [pltpu.VMEM((2 * own1, w), F32), pltpu.VMEM((w, w), F32)]
    rest = [pltpu.VMEM((docs * NB, w), F32), pltpu.VMEM((docs * NB, w), F32), pltpu.VMEM((5, 16, w), F32)]
    gots = [buffer for plan in PLAN for kind, units in plan for buffer in landing(own2, units * UNIT, ORDERS[kind])]
    count = len(gots) // 4
    dma = pltpu.SemaphoreType.DMA
    sems = [dma((count, STAGES)), dma((count, STAGES)), dma((count,)), dma((GROUPS, 8)), dma((GROUPS, 8)),
            dma((3,)), dma((2,)), dma((5,)), dma((5,)), pltpu.SemaphoreType.REGULAR]
    return pl.pallas_call(
        functools.partial(tail_kernel, docs, 4),
        in_specs=[anywhere] * 18 + [pl.BlockSpec(memory_space=pltpu.SMEM), vmem, vmem],
        out_specs=[anywhere] * 5 + [vmem] + [anywhere] * 2,
        out_shape=outs,
        scratch_shapes=held + slots + accs + rest + gots + sems,
        compiler_params=pltpu.CompilerParams(vmem_limit_bytes=60 << 20, collective_id=0, has_side_effects=True),
        cost_estimate=pl.CostEstimate(flops=10**11, bytes_accessed=10**8, transcendentals=10**7),
    )(*ops)[:6]


def front_kernel(docs, *refs):
    (x, cot, w_qkv_hbm, w_out_hbm, w_in_hbm, w_back_hbm, start, has, sticky, *singles) = refs[:18]
    (result, normed, act, pre, rgrad, branch, mgrad, qkv_out, mem_out, mem_low_out, hidden_out, mixed_out, lse_out,
     carry_out, data_out, small, vec) = refs[18:35]
    (w_qkv, w_out, w_in, w_back, xs, hidden, qkv, memory, fresh, begin, mem, mem_low, mixed, lse, carry, data, a,
     partial, peaks, totals, wsem, osem, bsem, ssem, rsem) = refs[35:]
    b, s = lax.axis_index("batch"), lax.axis_index("seg")
    w = x.shape[2]
    half = w // 2
    q_bias, v_bias, out_bias, back_bias, gain1, offset1, gain2, offset2 = (vec.at[pl.ds(i, 1)] for i in range(8))
    in_bias = lambda k: vec[8 + k : 9 + k]
    for i in range(8):
        vec[i : i + 1] = singles[i][...][None]
    for i in range(w_in_hbm.shape[1] // w):
        vec[8 + i : 9 + i] = singles[8][pl.ds(i * w, w)][None]
    loads = [pltpu.make_async_copy(src, dst, wsem.at[i]) for i, (src, dst) in enumerate(
        [(x, xs), (w_qkv_hbm, w_qkv), (w_out_hbm, w_out), (w_in_hbm, w_in), (w_back_hbm, w_back)])]
    for load in loads:
        load.start()
    own_begin = pltpu.make_async_copy(start, begin.at[0], bsem)
    own_begin.start()
    peer = (b, 1 - s)
    barrier = pltpu.get_barrier_semaphore()
    pl.semaphore_signal(barrier, inc=1, device_id=peer, device_id_type=MESH)
    pl.semaphore_wait(barrier, 1)

    given = pltpu.make_async_remote_copy(
        src_ref=start, dst_ref=begin.at[1], send_sem=ssem.at[docs], recv_sem=rsem.at[docs], device_id=peer, device_id_type=MESH)

    @pl.when(s == 1)
    def _():
        given.start()

    maps_kernel(docs, sticky.at[:, 0], carry, data, a)
    outs = [pltpu.make_async_copy(carry, carry_out, osem.at[0]), pltpu.make_async_copy(data, data_out, osem.at[1])]
    for out in outs:
        out.start()

    loads[0].wait()
    for d in range(docs):
        unit, _ = normalised(xs[d].astype(F32))
        hidden[d] = (unit * gain1[...] + offset1[...]).astype(BF16)
    outs.append(pltpu.make_async_copy(hidden, hidden_out, osem.at[2]))
    outs[-1].start()
    own_begin.wait()

    @pl.when(s == 0)
    def _():
        given.wait_recv()
        for d in range(docs):
            flag = has[d].astype(F32)
            memory[d, :, 0:half] = flag * begin[0, d]
            memory[d, :, half:w] = flag * begin[1, d]

    def carried(d):
        return pltpu.make_async_remote_copy(
            src_ref=fresh.at[d], dst_ref=memory.at[d], send_sem=ssem.at[d], recv_sem=rsem.at[d], device_id=peer, device_id_type=MESH)

    @pl.when(s == 0)
    def _():
        for d in range(docs):
            fresh[d] = dot_hi(carry[d], memory[d], 1, 0) + dot_hi(data[d], hidden[d].astype(F32), 1, 0)
            carried(d).start()

    loads[1].wait()
    zero = jnp.zeros((1, w), F32)
    for d in range(docs):
        for p, bias in enumerate((q_bias[...], zero, v_bias[...])):
            cols = pl.ds(p * w, w)
            qkv[d, :, cols] = (mm(hidden[d], w_qkv[:, cols]) + bias).astype(BF16)
    outs.append(pltpu.make_async_copy(qkv, qkv_out, osem.at[3]))
    outs[-1].start()
    small[...] = jnp.zeros_like(small)
    vectors = (out_bias, back_bias, gain2, offset2)
    tile = 256
    pairs = w // 128

    def columns(p, i):
        return pl.ds(pl.multiple_of(p * w + i * 128, 128), 128)

    def early(k, _):
        d, i = k // pairs, k % pairs
        attend_tokens(qkv.at[d, :, columns(0, i)], qkv.at[d, :, columns(1, i)], qkv.at[d, :, columns(2, i)],
                      partial.at[d, i], peaks.at[d, i], totals.at[d, i])
        return 0

    lax.fori_loop(0, docs * pairs, early, 0)
    for load in loads[2:]:
        load.wait()
    for d in range(docs):
        @pl.when(s == 1)
        def _():
            carried(d).wait_recv()

        low = memory[d].astype(BF16)
        mem_low[d] = low
        for p, bias in enumerate((zero, v_bias[...])):
            mem[d, :, pl.ds(p * w, w)] = (mm(low, w_qkv[:, pl.ds((p + 1) * w, w)]) + bias).astype(BF16)

        def late(i, _):
            attend_memory(qkv.at[d, :, columns(0, i)], mem.at[d, :, columns(0, i)], mem.at[d, :, columns(1, i)],
                          partial.at[d, i], peaks.at[d, i], totals.at[d, i], mixed.at[d, :, columns(0, i)], lse.at[d, i])
            return 0

        lax.fori_loop(0, pairs, late, 0)

        def feed_body(x_ref, cot_ref, *out_refs):
            rows = pl.ds(pl.multiple_of(pl.program_id(0) * tile, tile), tile)
            wide, sums = feed_core(x_ref, mixed.at[d, rows], cot_ref, w_out, w_in, w_back, vectors, in_bias, *out_refs)
            small[2:3] += sums[1]
            small[3:4] += sums[0]
            small[6:7] += sums[2]
            small[7:8] += sums[3]
            for k, part in enumerate(wide):
                small[8 + k : 9 + k] += part

        first = d * (L // tile)
        rows = lambda c: pl.BlockSpec((tile, c), lambda i: (first + i, 0))
        ff = w_in.shape[1]
        pltpu.emit_pipeline(
            feed_body, grid=(L // tile,),
            in_specs=[pl.BlockSpec((tile, w), lambda i: (i, 0)), rows(w)],
            out_specs=[rows(w), rows(w), rows(ff), rows(ff), rows(w), rows(w), rows(w)],
        )(x.at[d], cot, result, normed, act, pre, rgrad, branch, mgrad)
    for i, (src, dst) in enumerate([(mem, mem_out), (mem_low, mem_low_out), (mixed, mixed_out), (lse, lse_out)]):
        outs.append(pltpu.make_async_copy(src, dst, osem.at[4 + i]))
        outs[-1].start()
    for out in outs:
        out.wait()

    @pl.when(s == 0)
    def _():
        for d in range(docs):
            carried(d).wait_send()

    @pl.when(s == 1)
    def _():
        given.wait_send()


def front(x, cot, w_qkv, w_out, w_in, w_back, start, has, sticky, *singles):
    docs, _, w = x.shape
    n = docs * L
    ff = w_in.shape[1]
    anywhere = pl.BlockSpec(memory_space=pl.ANY)
    vmem = pl.BlockSpec(memory_space=pltpu.VMEM)
    arr = jax.ShapeDtypeStruct
    lse_shape = (docs, w // 128, 2, L)
    kept = [(docs, L, 3 * w), (docs, NB, 2 * w), (docs, NB, w), (docs, L, w), (docs, L, w)]
    outs = [arr((n, c), t) for c, t in ((w, BF16), (w, BF16), (ff, BF16), (ff, BF16), (w, F32), (w, BF16), (w, BF16))]
    outs += [arr(shape, BF16) for shape in kept]
    outs += [arr(lse_shape, F32), arr((docs, NB, NB), F32), arr((docs, NB, L), F32), arr((16, w), F32), arr((16, w), F32)]
    v = pltpu.VMEM
    scratch = [v(w_qkv.shape, BF16), v(w_out.shape, BF16), v(w_in.shape, BF16), v(w_back.shape, BF16), v((docs, L, w), BF16),
               v((docs, L, w), BF16), v(kept[0], BF16), v((docs, NB, w), F32), v((docs, NB, w), F32), v((2, docs, NB, w // 2), F32),
               v(kept[1], BF16), v(kept[2], BF16), v((docs, L, w), BF16), v(lse_shape, F32), v((docs, NB, NB), F32),
               v((docs, NB, L), F32), v((docs, NB, NB), F32), v((docs, w // 128, 128, L), F32), v(lse_shape, F32), v(lse_shape, F32)]
    dma = pltpu.SemaphoreType.DMA
    scratch += [dma((5,)), dma((8,)), dma, dma((docs + 1,)), dma((docs + 1,))]
    return pl.pallas_call(
        functools.partial(front_kernel, docs),
        in_specs=[anywhere] * 7 + [pl.BlockSpec(memory_space=pltpu.SMEM)] + [vmem] * 10,
        out_specs=[anywhere] * 15 + [vmem] * 2,
        out_shape=outs,
        scratch_shapes=scratch,
        compiler_params=pltpu.CompilerParams(vmem_limit_bytes=60 << 20, collective_id=1, has_side_effects=True),
        cost_estimate=pl.CostEstimate(flops=10**11, bytes_accessed=10**8, transcendentals=10**7),
    )(x, cot, w_qkv, w_out, w_in, w_back, start, has, sticky, *singles)


def hand_over_kernel(back, wide, three, entry, start, result, small, *refs):
    outs, stages, sem = refs[:16], refs[16:23], refs[23]
    w = three.shape[1] // 4
    b = lax.axis_index("batch")
    pairs = [(back, outs[5]), (wide, outs[4]), (three.at[:, pl.ds(0, 3 * w)], outs[2]), (three.at[:, pl.ds(3 * w, w)], outs[3]),
             (entry, outs[1]), (result, outs[0]), (start, outs[6])]
    copies = [pltpu.make_async_copy(src, stage, sem.at[0, i]) for i, ((src, _), stage) in enumerate(zip(pairs, stages))]
    for copy in copies:
        copy.start()
    away = [pltpu.make_async_copy(stages[i], pairs[i][1], sem.at[1, i]) for i in range(1, len(pairs))]
    copies[0].wait()
    short = back.shape[0]
    for q in range(4):
        out = pltpu.make_async_copy(stages[0].at[:, pl.ds(q * w, w)], outs[5].at[pl.ds(q * short, short)], sem.at[1, 7 + q])
        out.start()
        away.append(out)
    for copy, out in zip(copies[1:], away):
        copy.wait()
        out.start()
    own = w // 16
    rows = lax.broadcasted_iota(jnp.int32, (w, 256), 0)
    cols = lax.broadcasted_iota(jnp.int32, (w, 256), 1)
    pick = (rows == cols + b * own) & (cols < own)
    mine = dot_hi(small[...], jnp.where(pick, 1.0, 0.0), 1, 0)
    pick = (rows == cols + (b % 4) * (4 * own)) & (cols < 4 * own)
    row = lax.broadcasted_iota(jnp.int32, (16, 1), 0) == 8 + b // 4
    long = dot_hi(jnp.where(row, small[...], 0.0), jnp.where(pick, 1.0, 0.0), 1, 0)
    long = jnp.sum(long, 0, keepdims=True)
    for i in range(8):
        outs[7 + i][...] = mine[i, :own]
    outs[15][...] = long[0, : 4 * own]
    for out in away:
        out.wait()


def hand_over(back, wide, three, entry, start, result, small):
    w = three.shape[1] // 4
    anywhere = pl.BlockSpec(memory_space=pl.ANY)
    vmem = pl.BlockSpec(memory_space=pltpu.VMEM)
    arr = lambda a: jax.ShapeDtypeStruct(a.shape, a.dtype)
    rows = three.shape[0]
    stages = [(back.shape, F32), (wide.shape, F32), ((rows, 3 * w), F32), ((rows, w), F32), (entry.shape, BF16), (result.shape, BF16),
              (start.shape, F32)]
    return pl.pallas_call(
        hand_over_kernel,
        in_specs=[anywhere] * 6 + [vmem],
        out_specs=[anywhere] * 7 + [vmem] * 9,
        out_shape=[arr(result), arr(entry), jax.ShapeDtypeStruct((rows, 3 * w), F32), jax.ShapeDtypeStruct((rows, w), F32), arr(wide),
                   jax.ShapeDtypeStruct((4 * rows, w), F32), arr(start)] + [jax.ShapeDtypeStruct((w // 16,), F32)] * 8 + [jax.ShapeDtypeStruct((w // 4,), F32)],
        scratch_shapes=[pltpu.VMEM(a, t) for a, t in stages] + [pltpu.SemaphoreType.DMA((2, 11))],
        compiler_params=pltpu.CompilerParams(vmem_limit_bytes=60 << 20),
        cost_estimate=pl.CostEstimate(flops=10**7, bytes_accessed=10**7, transcendentals=0),
    )(back, wide, three, entry, start, result, small)


def outer(a, b):
    return lax.dot_general(a, b, (((0,), (0,)), ((), ())), preferred_element_type=F32)


def passed(block, distance):
    n = lax.axis_size("seg")
    return lax.ppermute(block, "seg", [(i - distance, i) for i in range(n) if 0 <= i - distance < n])


def swap(block, axis, distance):
    n = lax.axis_size(axis)
    return lax.ppermute(block, axis, [(i, i ^ distance) for i in range(n)])


def halve(block, axis, distance, dim):
    bit = (lax.axis_index(axis) // distance) % 2
    send = lax.dynamic_index_in_dim(block, 1 - bit, dim, keepdims=False)
    keep = lax.dynamic_index_in_dim(block, bit, dim, keepdims=False)
    return keep + swap(send, axis, distance)


def spread(work, seg_place, first):
    n, s = lax.axis_size("batch"), lax.axis_size("seg")
    bits = n.bit_length() - 1
    _, own, cols = work.shape
    split = s if seg_place < bits and own % s == 0 else 1
    work = work.reshape((2,) * (bits - first) + (split, own // split, cols))
    for k in range(first, bits + 1):
        if k == seg_place:
            if split == 1:
                d = 1
                while d < s:
                    work = work + swap(work, "seg", d)
                    d *= 2
            else:
                left = bits - k
                work = work.reshape((2,) * left + (2,) * (s.bit_length() - 1) + (own // split, cols))
                d = 1
                while d < s:
                    work = halve(work, "seg", d, work.ndim - 3)
                    d *= 2
        if k < bits:
            work = halve(work, "batch", 1 << k, bits - 1 - k)
    if split > 1:
        d = s // 2
        while d >= 1:
            bit = (lax.axis_index("seg") // d) % 2
            other = swap(work, "seg", d)
            work = jnp.where(bit == 0, jnp.concatenate([work, other], 0), jnp.concatenate([other, work], 0))
            d //= 2
    return work.reshape(own, cols)


def forward(x, cot, w_qkv, w_out, w_in, w_back, start_memory, has_memory, sticky,
            q_bias, v_bias, out_bias, in_bias, back_bias, ln1_gain, ln1_bias, ln2_gain, ln2_bias):
    docs, _, width = x.shape
    n = docs * L
    chain = lax.axis_size("seg")
    is_first = lax.axis_index("seg") == 0
    flags = has_memory.astype(F32)[:, None, None]

    parts = [start_memory] + [lax.ppermute(start_memory, "seg", [(i, 0)]) for i in range(1, chain)]
    own_start = jnp.where(is_first, flags * jnp.concatenate(parts, 2), 0.0)

    carry_map, data_map = memory_maps(sticky)
    bias = jnp.concatenate([q_bias, jnp.zeros_like(q_bias), v_bias])
    hidden, qkv = project(x, w_qkv, bias, ln1_gain, ln1_bias)

    memory = own_start
    for i in range(chain - 1):
        memory = passed(renew(carry_map, data_map, memory, hidden), 1) + own_start

    mem_rows, mem = recall(memory.reshape(docs * NB, width), w_qkv, bias)
    mem = mem.reshape(docs, NB, 2 * width)
    mixed, log_total = attend(qkv, mem)
    rows4 = jnp.stack([out_bias, back_bias, ln2_gain, ln2_bias])
    result, normed, act, pre, residual_grad, branch, mixed_grad, wide, sums = feed(
        x.reshape(n, width), mixed.reshape(n, width), cot, w_out, w_in, w_back, rows4, in_bias
    )
    small = [sums[1:2], sums[0:1], jnp.zeros((2, width), F32), sums[2:4], wide.reshape(4, width)]
    small = jnp.concatenate([jnp.zeros((2, width), F32)] + small + [jnp.zeros((4, width), F32)], 0)
    return (result, normed, act, pre, residual_grad, branch, mixed_grad, qkv, mem, mem_rows, hidden, mixed, log_total,
            carry_map, data_map, small)


def spread_out(x, act, cot, normed, pre, qkv, mem, mgrad, mixed, lse, hidden, mem_rows, branch, w_qkv, rgrad, data_map, carry_map, has_memory, gain, small):
    docs, _, width = x.shape
    n = docs * L
    batch, chain = lax.axis_size("batch"), lax.axis_size("seg")
    is_first = lax.axis_index("seg") == 0
    flags = has_memory.astype(F32)[:, None, None]
    grad_back = spread(outer(act, cot).reshape(batch, -1, width), 2, 0)
    grad_in = spread(outer(normed, pre).reshape(batch, width // batch, -1), 1, 0)
    token_proj, memory_proj, attn_sums = attend_grads(qkv, mem, mgrad, mixed, lse)
    memory_proj = memory_proj.reshape(2, docs * NB, width)
    local_grad = local_memory_grad(memory_proj, w_qkv).reshape(docs, NB, width)
    carry_back = carry_map.swapaxes(1, 2)
    incoming = jnp.zeros_like(local_grad)
    for i in range(chain - 1):
        sent = local_grad if i == 0 else jnp.matmul(carry_back, incoming, precision=HI) + local_grad
        incoming = passed(sent, -1)
    hidden_rows = hidden.reshape(n, width)
    three = [outer(hidden_rows, token_proj[i].reshape(n, width)) for i in range(3)]
    three = [three[0]] + [three[i + 1] + outer(mem_rows, memory_proj[i]) for i in range(2)]
    three = jnp.concatenate(three + [outer(mixed.reshape(n, width), branch)], 1)
    grad_three = spread(three.reshape(batch, width // batch, -1), 2, 0)
    input_grad, entry_sums = entry_grads(
        x, rgrad, token_proj, data_map, incoming, w_qkv, gain
    )
    start_grad = jnp.where(is_first, flags * (local_grad + jnp.matmul(carry_back, incoming, precision=HI)), 0.0)
    own = width // chain
    start_share = start_grad[:, :, :own]
    for i in range(1, chain):
        start_share = start_share + lax.ppermute(start_grad[:, :, i * own : (i + 1) * own], "seg", [(0, i)])

    wide = small[8:12].reshape(-1)
    packed = jnp.concatenate(
        [g.reshape(batch, 1, -1)
         for g in (jnp.sum(attn_sums[:, 0], 0), jnp.sum(attn_sums[:, 1], 0), small[2], small[3], entry_sums[0], entry_sums[1],
                   small[6], small[7], wide)], 2)
    packed = spread(packed, batch.bit_length() - 1, 0)[0]
    own = width // batch
    vectors = [packed[i * own : (i + 1) * own] for i in range(8)] + [packed[8 * own :]]
    return input_grad, start_share, grad_back, grad_in, grad_three, vectors


def shards(
    tokens,
    start_memory,
    has_memory,
    sticky,
    w_qkv,
    w_out,
    w_in,
    w_back,
    q_bias,
    v_bias,
    out_bias,
    in_bias,
    back_bias,
    ln1_gain,
    ln1_bias,
    ln2_gain,
    ln2_bias,
    cotangent,
):
    width = w_qkv.shape[0]
    docs = tokens.shape[0]
    n = docs * L
    chain = lax.axis_size("seg")
    batch = lax.axis_size("batch")
    x = tokens[:, 0]
    cot = cotangent[:, 0].reshape(n, width)
    if (batch, chain) == (16, 2):
        (result, normed, act, pre, residual_grad, branch, mixed_grad, qkv, mem, mem_rows, hidden, mixed, log_total,
         carry_map, data_map, small, vec) = front(
            x, cot, w_qkv, w_out, w_in, w_back, start_memory, has_memory, sticky,
            q_bias, v_bias, out_bias, back_bias, ln1_gain, ln1_bias, ln2_gain, ln2_bias, in_bias)
        sums = tail(
            docs, batch, act, cot, normed, pre, qkv, mem, mixed_grad.reshape(docs, L, width), mixed, log_total, hidden,
            mem_rows, branch, w_qkv, x, residual_grad.reshape(docs, L, width), data_map, carry_map, has_memory, vec, small)
        back, wide, three, entry, start, vectors = sums
        result, input_grad, grad_qkv, grad_out, grad_in, grad_back, start_share, *vectors = hand_over(
            back, wide, three, entry, start, result, vectors)
        start_share = start_share.reshape(docs, NB, width // chain)
    else:
        (result, normed, act, pre, residual_grad, branch, mixed_grad, qkv, mem, mem_rows, hidden, mixed, log_total,
         carry_map, data_map, small) = forward(
            x, cot, w_qkv, w_out, w_in, w_back, start_memory, has_memory, sticky[:, 0],
            q_bias, v_bias, out_bias, in_bias, back_bias, ln1_gain, ln1_bias, ln2_gain, ln2_bias)
        input_grad, start_share, grad_back, grad_in, grad_three, vectors = spread_out(
            x, act, cot, normed, pre, qkv, mem, mixed_grad.reshape(docs, L, width), mixed, log_total, hidden, mem_rows,
            branch, w_qkv, residual_grad.reshape(docs, L, width), data_map, carry_map, has_memory, ln1_gain, small
        )
        grad_qkv, grad_out = grad_three[:, : 3 * width], grad_three[:, 3 * width :]
    return (
        result.reshape(docs, 1, L, width),
        input_grad.reshape(docs, 1, L, width),
        start_share,
        grad_qkv,
        grad_out,
        grad_in,
        grad_back,
    ) + tuple(vectors[i] for i in (0, 1, 2, 8, 3, 4, 5, 6, 7))


def solution(mesh):
    rows = P("batch", "seg", None, None)
    in_specs = (rows, P("batch", None, "seg"), P("batch"), P("batch", "seg", None)) + (P(),) * 13 + (rows,)
    out_specs = (rows, rows, P("batch", None, "seg")) + (P("batch", None),) * 4 + (P("batch"),) * 9
    return jax.shard_map(shards, mesh=mesh, in_specs=in_specs, out_specs=out_specs, check_vma=False)
```

```python
import functools

import jax
import jax.numpy as jnp
from jax import lax
from jax.experimental import pallas as pl
from jax.experimental.pallas import tpu as pltpu
from jax.sharding import PartitionSpec as P

HEADS = 12
HD = 64
NB = 256
L = 512
STICKY = 512
GRID = 4096

EPSILON = 1e-05
RIDGE = 0.5
HI = lax.Precision.HIGHEST
F32 = jnp.float32
BF16 = jnp.bfloat16
EXP2_SCALE = HD**-0.5 * 1.4426950408889634
LEAF = 32
PIVOTS = 4


def dot_hi(a, b, ca, cb):
    return lax.dot_general(a, b, (((ca,), (cb,)), ((), ())), precision=HI, preferred_element_type=F32)

def bumps(times):
    centers = (lax.broadcasted_iota(jnp.int32, (NB, 1), 0).astype(F32) + 0.5) / NB
    scaled = (times - centers) * NB
    return jnp.exp(-0.5 * scaled * scaled)

def small_inverse(s):
    p = len(s)
    s = [list(r) for r in s]
    for k in range(p):
        inv = 1.0 / s[k][k]
        row = [inv if j == k else s[k][j] * inv for j in range(p)]
        for i in range(p):
            if i != k:
                f = s[i][k]
                s[i] = [-f * row[j] if j == k else s[i][j] - f * row[j] for j in range(p)]
        s[k] = row
    return s


def leaf_inverse(d):
    n = d.shape[0]
    rows = lax.broadcasted_iota(jnp.int32, (n, n), 0)
    lanes = lax.broadcasted_iota(jnp.int32, (1, n), 1)
    for k in range(0, n, PIVOTS):
        cols = [jnp.broadcast_to(d[:, k + j : k + j + 1], (n, n)) for j in range(PIVOTS)]
        inv = small_inverse([[cols[j][k + i : k + i + 1] for j in range(PIVOTS)] for i in range(PIVOTS)])
        old = [d[k + j : k + j + 1] for j in range(PIVOTS)]
        inside = (lanes >= k) & (lanes < k + PIVOTS)
        fresh = []
        for i in range(PIVOTS):
            r = inv[i][0] * old[0]
            for j in range(1, PIVOTS):
                r = r + inv[i][j] * old[j]
            for j in range(PIVOTS):
                r = jnp.where(lanes == k + j, inv[i][j], r)
            fresh.append(r)
        out = jnp.where(inside, 0.0, d)
        for i in range(PIVOTS):
            out = out - cols[i] * fresh[i]
        for i in range(PIVOTS):
            out = jnp.where(rows == k + i, fresh[i], out)
        d = out
    return d


def maps_kernel(docs, sticky_ref, carry_ref, data_ref, a_ref):
    new_times = 0.5 + 0.5 * (lax.broadcasted_iota(jnp.int32, (1, L), 1).astype(F32) + 0.5) / L
    fresh = bumps(new_times)
    eye = (lax.broadcasted_iota(jnp.int32, (NB, NB), 0) == lax.broadcasted_iota(jnp.int32, (NB, NB), 1)).astype(F32)
    base = dot_hi(fresh, fresh, 1, 1) + RIDGE * eye
    for d in range(docs):
        old = (sticky_ref[pl.ds(d, 1), :].astype(F32) + 0.5) / GRID
        f1 = bumps(0.5 * old)
        a_ref[d] = base + dot_hi(f1, f1, 1, 1)
        carry_ref[d] = dot_hi(f1, bumps(old), 1, 1)
    lanes = lax.broadcasted_iota(jnp.int32, (1, NB), 1) // LEAF
    for j in range(NB // LEAF):
        sl = pl.ds(j * LEAF, LEAF)
        leaves = [leaf_inverse(a_ref[d, sl, sl]) for d in range(docs)]
        for d in range(docs):
            p = leaves[d]
            mine = lanes == j
            row = dot_hi(p, a_ref[d, sl, :], 1, 0)
            wide = jnp.concatenate([p] * (NB // LEAF), 1)
            row = jnp.where(mine, wide, row)
            col = a_ref[d, :, sl]
            rest = jnp.where(mine, 0.0, a_ref[d])
            a_ref[d] = rest - dot_hi(col, row, 1, 0)
            a_ref[d, sl, :] = row
    for d in range(docs):
        x = a_ref[d]
        carry_ref[d] = dot_hi(x, carry_ref[d], 1, 0)
        data_ref[d] = dot_hi(x, fresh, 1, 0)

def memory_maps(sticky):
    docs = sticky.shape[0]
    return pl.pallas_call(functools.partial(maps_kernel, docs),
        out_shape=[jax.ShapeDtypeStruct((docs, NB, NB), F32), jax.ShapeDtypeStruct((docs, NB, L), F32)],
        scratch_shapes=[pltpu.VMEM((docs, NB, NB), F32)],
        compiler_params=pltpu.CompilerParams(vmem_limit_bytes=32 << 20),
        cost_estimate=pl.CostEstimate(flops=docs * 10**10, bytes_accessed=docs * 10**6, transcendentals=0),
    )(sticky)


def nt(a, b):
    return lax.dot_general(a, b, (((1,), (1,)), ((), ())), preferred_element_type=F32)

def tn(a, b):
    return lax.dot_general(a, b, (((0,), (0,)), ((), ())), preferred_element_type=F32)

def nn(a, b):
    return jnp.dot(a, b, preferred_element_type=F32)

def head_lanes(h):
    return lax.broadcasted_iota(jnp.int32, (1, 2 * HD), 1) // HD == h

def causal():
    half = L // 2
    return lax.broadcasted_iota(jnp.int32, (half, half), 0) <= lax.broadcasted_iota(jnp.int32, (half, half), 1)

def attend_core(q_ref, k_ref, v_ref, mk_ref, mv_ref, out_ref, peak_ref):
    half = L // 2
    q = q_ref[...]; k = k_ref[...]; v = v_ref[...]; mk = mk_ref[...]; mv = mv_ref[...]
    seen = causal()
    outs = []
    for h in range(2):
        qh = jnp.where(head_lanes(h), q, jnp.zeros_like(q))
        s00 = jnp.where(seen, nt(k[:half], qh[:half]), -1e30)
        s01 = nt(k[:half], qh[half:])
        s11 = jnp.where(seen, nt(k[half:], qh[half:]), -1e30)
        sm = nt(mk, qh)
        sides = []
        for side, parts in enumerate(([s00, sm[:, :half]], [s01, s11, sm[:, half:]])):
            peak = functools.reduce(jnp.maximum, [jnp.max(p, 0, keepdims=True) for p in parts])
            ps = [jnp.exp2((p - peak) * EXP2_SCALE) for p in parts]
            total = functools.reduce(jnp.add, [jnp.sum(p, 0, keepdims=True) for p in ps])
            vs = [v[:half], mv] if side == 0 else [v[:half], v[half:], mv]
            o = functools.reduce(jnp.add, [tn(a, p.astype(BF16)) for a, p in zip(vs, ps)])
            sides.append(o * (1.0 / total))
            peak_ref[h, pl.ds(side * half, half)] = (peak * EXP2_SCALE + jnp.log2(total))[0]
        outs.append(jnp.concatenate(sides, 1))
    lanes = lax.broadcasted_iota(jnp.int32, (2 * HD, 1), 0) // HD == 0
    out_ref[...] = jnp.where(lanes, outs[0], outs[1]).T.astype(BF16)


def attend_tokens(q_ref, k_ref, v_ref, out_ref, peak_ref, total_ref):
    half = L // 2
    q = q_ref[...]
    k = k_ref[...]
    v = v_ref[...]
    seen = causal()
    outs = []
    for h in range(2):
        qh = jnp.where(head_lanes(h), q, jnp.zeros_like(q))
        s00 = jnp.where(seen, nt(k[:half], qh[:half]), -1e30)
        s01 = nt(k[:half], qh[half:])
        s11 = jnp.where(seen, nt(k[half:], qh[half:]), -1e30)
        sides = []
        for side, parts in enumerate(([s00], [s01, s11])):
            peak = functools.reduce(jnp.maximum, [jnp.max(p, 0, keepdims=True) for p in parts])
            ps = [jnp.exp2((p - peak) * EXP2_SCALE) for p in parts]
            total = functools.reduce(jnp.add, [jnp.sum(p, 0, keepdims=True) for p in ps])
            vs = [v[:half], v[half:]]
            sides.append(functools.reduce(jnp.add, [tn(a, p.astype(BF16)) for a, p in zip(vs, ps)]))
            cols = pl.ds(side * half, half)
            peak_ref[h : h + 1, cols] = peak
            total_ref[h : h + 1, cols] = total
        outs.append(jnp.concatenate(sides, 1))
    lanes = lax.broadcasted_iota(jnp.int32, (2 * HD, 1), 0) // HD == 0
    out_ref[...] = jnp.where(lanes, outs[0], outs[1])


def attend_memory(q_ref, mk_ref, mv_ref, tokens_ref, peak_ref, total_ref, out_ref, lse_ref):
    q = q_ref[...]
    mk = mk_ref[...]
    mv = mv_ref[...]
    lanes = lax.broadcasted_iota(jnp.int32, (2 * HD, 1), 0) // HD == 0
    found = []
    for h in range(2):
        s = nt(mk, jnp.where(head_lanes(h), q, jnp.zeros_like(q)))
        old = peak_ref[h : h + 1]
        peak = jnp.maximum(old, jnp.max(s, 0, keepdims=True))
        p = jnp.exp2((s - peak) * EXP2_SCALE)
        shrink = jnp.exp2((old - peak) * EXP2_SCALE)
        total = total_ref[h : h + 1] * shrink + jnp.sum(p, 0, keepdims=True)
        lse_ref[h : h + 1] = peak * EXP2_SCALE + jnp.log2(total)
        rate = 1.0 / total
        found.append((tn(mv, p.astype(BF16)) * rate, shrink * rate))
    (o0, r0), (o1, r1) = found
    out_ref[...] = (jnp.where(lanes, o0, o1) + tokens_ref[...] * jnp.where(lanes, r0, r1)).T.astype(BF16)


def attend_kernel(q_ref, k_ref, v_ref, mk_ref, mv_ref, out_ref, peak_ref):
    attend_core(*(r.at[0] for r in (q_ref, k_ref, v_ref, mk_ref, mv_ref, out_ref)), peak_ref.at[0, 0])

def attend(qkv, mem):
    docs, _, w3 = qkv.shape
    w = w3 // 3
    pairs = w // 128
    tok = lambda o: pl.BlockSpec((1, L, 128), lambda d, i: (d, 0, o * pairs + i))
    me = lambda o: pl.BlockSpec((1, NB, 128), lambda d, i: (d, 0, o * pairs + i))
    return pl.pallas_call(attend_kernel, grid=(docs, pairs),
        in_specs=[tok(0), tok(1), tok(2), me(0), me(1)],
        out_specs=[tok(0), pl.BlockSpec((1, 1, 2, L), lambda d, i: (d, i, 0, 0))],
        out_shape=[jax.ShapeDtypeStruct((docs, L, w), BF16), jax.ShapeDtypeStruct((docs, pairs, 2, L), F32)],
        compiler_params=pltpu.CompilerParams(vmem_limit_bytes=48 << 20),
        cost_estimate=pl.CostEstimate(flops=docs * pairs * 8 * 768 * 512 * 128, bytes_accessed=docs * L * w * 10, transcendentals=docs * 12 * 768 * 512),
    )(qkv, qkv, qkv, mem, mem)

def grads_core(q_ref, k_ref, v_ref, mk_ref, mv_ref, g_ref, o_ref, peak_ref, dtok_ref, dmem_ref):
    half = L // 2
    q = q_ref[0]; k = k_ref[0]; v = v_ref[0]; mk = mk_ref[0]; mv = mv_ref[0]; g = g_ref[0]
    scale = HD ** -0.5
    seen = causal()
    go = g.astype(F32) * o_ref[0].astype(F32)
    pick = (lax.broadcasted_iota(jnp.int32, (8, 2 * HD), 1) // HD == lax.broadcasted_iota(jnp.int32, (8, 2 * HD), 0)).astype(F32)
    delta = lax.dot_general(pick, go, (((1,), (1,)), ((), ())), precision=lax.Precision.HIGHEST, preferred_element_type=F32)
    first = head_lanes(0)
    res = []
    for h in range(2):
        mine = head_lanes(h)
        qh = jnp.where(mine, q, jnp.zeros_like(q))
        gh = jnp.where(mine, g, jnp.zeros_like(g))
        lse = peak_ref[0, 0, pl.ds(h, 1), :]
        dh = delta[h:h + 1]
        def tile(kk, vv, lo, hi, mask):
            s = nt(kk, qh[lo:hi])
            p = jnp.exp2(s * EXP2_SCALE - lse[:, lo:hi])
            if mask:
                p = jnp.where(seen, p, 0.0)
            dp = nt(vv, gh[lo:hi])
            return p.astype(BF16), (p * (dp - dh[:, lo:hi])).astype(BF16)
        p00, t00 = tile(k[:half], v[:half], 0, half, True)
        p01, t01 = tile(k[:half], v[:half], half, L, False)
        p11, t11 = tile(k[half:], v[half:], half, L, True)
        pm, tm = tile(mk, mv, 0, L, False)
        dv0 = nn(p00, g[:half]) + nn(p01, g[half:])
        dv1 = nn(p11, g[half:])
        dvm = nn(pm, g)
        dk0 = nn(t00, q[:half]) + nn(t01, q[half:])
        dk1 = nn(t11, q[half:])
        dkm = nn(tm, q)
        dq0 = tn(k[:half], t00) + tn(mk, tm[:, :half])
        dq1 = tn(k[:half], t01) + tn(k[half:], t11) + tn(mk, tm[:, half:])
        res.append((jnp.concatenate([dq0, dq1], 1), jnp.concatenate([dk0, dk1], 0), jnp.concatenate([dv0, dv1], 0), dkm, dvm))
    rows = lax.broadcasted_iota(jnp.int32, (2 * HD, 1), 0) // HD == 0
    dq = (jnp.where(rows, res[0][0], res[1][0]).T * scale).astype(BF16)
    dk, dv, dkm, dvm = [jnp.where(first, a, b) for a, b in zip(res[0][1:], res[1][1:])]
    dk = (dk * scale).astype(BF16); dkm = (dkm * scale).astype(BF16)
    dv = dv.astype(BF16); dvm = dvm.astype(BF16)
    dtok_ref[0, 0] = dq; dtok_ref[1, 0] = dk; dtok_ref[2, 0] = dv
    dmem_ref[0, 0] = dkm; dmem_ref[1, 0] = dvm
    qs = jnp.sum(dq.astype(F32), 0, keepdims=True)
    vs = jnp.sum(dv.astype(F32), 0, keepdims=True) + jnp.sum(dvm.astype(F32), 0, keepdims=True)
    return qs, vs


def grads_kernel(*refs):
    qs, vs = grads_core(*refs[:-1])
    r = lax.broadcasted_iota(jnp.int32, (8, 128), 0)
    refs[-1][0] = jnp.where(r == 0, qs, jnp.where(r == 1, vs, 0.0))

def attend_grads(qkv, mem, g, mixed, lse):
    docs, _, w3 = qkv.shape
    w = w3 // 3
    pairs = w // 128
    tok = lambda o: pl.BlockSpec((1, L, 128), lambda d, i: (d, 0, o * pairs + i))
    me = lambda o: pl.BlockSpec((1, NB, 128), lambda d, i: (d, 0, o * pairs + i))
    return pl.pallas_call(grads_kernel, grid=(docs, pairs),
        in_specs=[tok(0), tok(1), tok(2), me(0), me(1), tok(0), tok(0), pl.BlockSpec((1, 1, 2, L), lambda d, i: (d, i, 0, 0))],
        out_specs=[pl.BlockSpec((3, 1, L, 128), lambda d, i: (0, d, 0, i)), pl.BlockSpec((2, 1, NB, 128), lambda d, i: (0, d, 0, i)), pl.BlockSpec((1, 8, 128), lambda d, i: (d, 0, i))],
        out_shape=[jax.ShapeDtypeStruct((3, docs, L, w), BF16), jax.ShapeDtypeStruct((2, docs, NB, w), BF16), jax.ShapeDtypeStruct((docs, 8, w), F32)],
        compiler_params=pltpu.CompilerParams(vmem_limit_bytes=48 << 20),
        cost_estimate=pl.CostEstimate(flops=docs * pairs * 20 * 768 * 512 * 128, bytes_accessed=docs * L * w * 16, transcendentals=docs * 12 * 768 * 512),
    )(qkv, qkv, qkv, mem, mem, g, mixed, lse)


def mm(a, b):
    return jnp.dot(a, b, preferred_element_type=F32)


def normalised(values):
    center = jnp.mean(values, -1, keepdims=True)
    shifted = values - center
    rate = lax.rsqrt(jnp.mean(shifted * shifted, -1, keepdims=True) + EPSILON)
    return shifted * rate, rate


def norm_back(unit, rate, scaled_grad):
    inner = jnp.mean(scaled_grad * unit, -1, keepdims=True)
    return rate * (scaled_grad - jnp.mean(scaled_grad, -1, keepdims=True) - unit * inner)


def whole(shape):
    return pl.BlockSpec(shape, lambda *_: (0,) * len(shape), pipeline_mode=pl.Buffered(1))


def col_sums(values):
    return jnp.sum(values, 0, keepdims=True)


def project_kernel(x_ref, w_ref, bias_ref, gain_ref, offset_ref, hidden_ref, qkv_ref):
    unit, _ = normalised(x_ref[0].astype(F32))
    hidden = (unit * gain_ref[...] + offset_ref[...]).astype(BF16)
    hidden_ref[0] = hidden
    qkv_ref[0] = (mm(hidden, w_ref[...]) + bias_ref[...]).astype(BF16)


def project(x, w_qkv, bias, gain, offset):
    docs, _, w = x.shape
    tile = 256
    rows = lambda c: pl.BlockSpec((1, tile, c), lambda d, i: (d, i, 0))
    return pl.pallas_call(
        project_kernel,
        grid=(docs, L // tile),
        in_specs=[rows(w), whole(w_qkv.shape), whole((1, 3 * w)), whole((1, w)), whole((1, w))],
        out_specs=[rows(w), rows(3 * w)],
        out_shape=[jax.ShapeDtypeStruct((docs, L, w), BF16), jax.ShapeDtypeStruct((docs, L, 3 * w), BF16)],
        compiler_params=pltpu.CompilerParams(vmem_limit_bytes=40 << 20),
        cost_estimate=pl.CostEstimate(flops=docs * L * w * w * 6, bytes_accessed=docs * L * w * 10, transcendentals=0),
    )(x, w_qkv, bias[None], gain[None], offset[None])


def renew_kernel(carry_ref, data_ref, memory_ref, hidden_ref, out_ref):
    out_ref[0] = dot_hi(carry_ref[0], memory_ref[0], 1, 0) + dot_hi(data_ref[0], hidden_ref[0].astype(F32), 1, 0)


def renew(carry_map, data_map, memory, hidden):
    docs, _, w = hidden.shape
    one = lambda r, c: pl.BlockSpec((1, r, c), lambda d: (d, 0, 0))
    return pl.pallas_call(
        renew_kernel,
        grid=(docs,),
        in_specs=[one(NB, NB), one(NB, L), one(NB, w), one(L, w)],
        out_specs=one(NB, w),
        out_shape=jax.ShapeDtypeStruct((docs, NB, w), F32),
        compiler_params=pltpu.CompilerParams(vmem_limit_bytes=40 << 20),
        cost_estimate=pl.CostEstimate(flops=docs * 6 * NB * 768 * w * 2, bytes_accessed=docs * NB * w * 8, transcendentals=0),
    )(carry_map, data_map, memory, hidden)


def recall_kernel(memory_ref, w_ref, bias_ref, low_ref, out_ref):
    low = memory_ref[...].astype(BF16)
    low_ref[...] = low
    out_ref[...] = (mm(low, w_ref[...]) + bias_ref[...]).astype(BF16)


def recall(memory, w_qkv, bias):
    rows, w = memory.shape
    tile = w
    return pl.pallas_call(
        recall_kernel,
        grid=(2,),
        in_specs=[whole((rows, w)), pl.BlockSpec((w, tile), lambda i: (0, 1 + i)), pl.BlockSpec((1, tile), lambda i: (0, 1 + i))],
        out_specs=[pl.BlockSpec((rows, w), lambda i: (0, 0)), pl.BlockSpec((rows, tile), lambda i: (0, i))],
        out_shape=[jax.ShapeDtypeStruct((rows, w), BF16), jax.ShapeDtypeStruct((rows, 2 * w), BF16)],
        compiler_params=pltpu.CompilerParams(vmem_limit_bytes=40 << 20),
        cost_estimate=pl.CostEstimate(flops=rows * w * w * 4, bytes_accessed=rows * w * 10, transcendentals=0),
    )(memory, w_qkv, bias[None])


GELU_RATE = 0.7978845608028654
GELU_CUBE = 0.044715


def feed_core(x_ref, mixed_ref, cot_ref, w_out_ref, w_in_ref, w_back_ref, vectors, in_bias,
              result_ref, normed_ref, act_ref, pre_ref, rgrad_ref, branch_ref, mgrad_ref):
    out_bias, back_bias, gain, offset = (ref[...] for ref in vectors)
    cot = cot_ref[...]
    residual = x_ref[...].astype(F32) + (mm(mixed_ref[...], w_out_ref[...]) + out_bias)
    unit, rate = normalised(residual)
    normed = (unit * gain + offset).astype(BF16)
    normed_ref[...] = normed
    result = residual + back_bias
    ngrad = None
    chunk = 768
    wide = []
    for c in range(0, w_in_ref.shape[1], chunk):
        sl = pl.ds(c, chunk)
        v = mm(normed, w_in_ref[:, sl]) + in_bias(c // chunk)
        square = v * v
        t = jnp.tanh(GELU_RATE * v * (1.0 + GELU_CUBE * square))
        half = 0.5 * (1.0 + t)
        act = (v * half).astype(BF16)
        slope = half + (0.5 * GELU_RATE) * v * (1.0 - t * t) * (1.0 + 3.0 * GELU_CUBE * square)
        act_ref[:, sl] = act
        result = result + mm(act, w_back_ref[sl, :])
        pre = (nt(cot, w_back_ref[sl, :]) * slope).astype(BF16)
        pre_ref[:, sl] = pre
        wide.append(col_sums(pre.astype(F32)))
        part = nt(pre, w_in_ref[:, sl])
        ngrad = part if ngrad is None else ngrad + part
    result_ref[...] = result.astype(BF16)
    rgrad = cot.astype(F32) + norm_back(unit, rate, ngrad * gain)
    rgrad_ref[...] = rgrad
    branch = rgrad.astype(BF16)
    branch_ref[...] = branch
    mgrad_ref[...] = nt(branch, w_out_ref[...]).astype(BF16)
    sums = [col_sums(cot.astype(F32)), col_sums(branch.astype(F32)), col_sums(ngrad * unit), col_sums(ngrad)]
    return wide, sums


def feed_kernel(x_ref, mixed_ref, cot_ref, w_out_ref, w_in_ref, w_back_ref, rows_ref, in_bias_ref, *out_refs):
    vectors = [rows_ref.at[pl.ds(i, 1)] for i in range(4)]
    in_bias = lambda k: in_bias_ref[:, pl.ds(k * 768, 768)]
    wide, sums = feed_core(x_ref, mixed_ref, cot_ref, w_out_ref, w_in_ref, w_back_ref, vectors, in_bias, *out_refs[:7])
    wide_ref, sums_ref = out_refs[7:]
    w = x_ref.shape[1]
    sums = jnp.concatenate(sums + [jnp.zeros((4, w), F32)], 0)
    wide = jnp.concatenate(wide, 1)

    @pl.when(pl.program_id(0) == 0)
    def _():
        sums_ref[...] = sums
        wide_ref[...] = wide

    @pl.when(pl.program_id(0) > 0)
    def _():
        sums_ref[...] += sums
        wide_ref[...] += wide


def feed(x, mixed, cot, w_out, w_in, w_back, rows4, in_bias):
    n, w = x.shape
    ff = w_in.shape[1]
    tile = 256
    rows = lambda c: pl.BlockSpec((tile, c), lambda i: (i, 0))
    arr = lambda c, t: jax.ShapeDtypeStruct((n, c), t)
    return pl.pallas_call(
        feed_kernel,
        grid=(n // tile,),
        in_specs=[rows(w), rows(w), rows(w), whole(w_out.shape), whole(w_in.shape), whole(w_back.shape), whole((4, w)), whole((1, ff))],
        out_specs=[rows(w), rows(w), rows(ff), rows(ff), rows(w), rows(w), rows(w),
                   pl.BlockSpec((1, ff), lambda i: (0, 0)), pl.BlockSpec((8, w), lambda i: (0, 0))],
        out_shape=[arr(w, BF16), arr(w, BF16), arr(ff, BF16), arr(ff, BF16), arr(w, F32), arr(w, BF16), arr(w, BF16),
                   jax.ShapeDtypeStruct((1, ff), F32), jax.ShapeDtypeStruct((8, w), F32)],
        compiler_params=pltpu.CompilerParams(vmem_limit_bytes=56 << 20),
        cost_estimate=pl.CostEstimate(flops=n * (4 * w * ff + 2 * w * w) * 2, bytes_accessed=n * ff * 4 + 2 * w * ff * 4, transcendentals=n * ff),
    )(x, mixed, cot, w_out, w_in, w_back, rows4, in_bias[None])


def local_kernel(g_ref, w_ref, out_ref):
    part = nt(g_ref[0], w_ref[...])

    @pl.when(pl.program_id(0) == 0)
    def _():
        out_ref[...] = part

    @pl.when(pl.program_id(0) == 1)
    def _():
        out_ref[...] += part


def local_memory_grad(memory_proj, w_qkv):
    _, rows, w = memory_proj.shape
    return pl.pallas_call(
        local_kernel,
        grid=(2,),
        in_specs=[pl.BlockSpec((1, rows, w), lambda i: (i, 0, 0)), pl.BlockSpec((w, w), lambda i: (0, 1 + i))],
        out_specs=pl.BlockSpec((rows, w), lambda i: (0, 0)),
        out_shape=jax.ShapeDtypeStruct((rows, w), F32),
        compiler_params=pltpu.CompilerParams(vmem_limit_bytes=40 << 20),
        cost_estimate=pl.CostEstimate(flops=rows * w * w * 4, bytes_accessed=rows * w * 10, transcendentals=0),
    )(memory_proj, w_qkv)


def entry_kernel(x_ref, rgrad_ref, proj_ref, data_ref, inc_ref, w_ref, gain_ref, out_ref, sums_ref):
    w = x_ref.shape[2]
    hgrad = dot_hi(data_ref[0], inc_ref[0], 0, 0)
    for p in range(3):
        hgrad = hgrad + nt(proj_ref[p, 0], w_ref[:, pl.ds(p * w, w)])
    unit, rate = normalised(x_ref[0].astype(F32))
    out_ref[0] = (rgrad_ref[0] + norm_back(unit, rate, hgrad * gain_ref[...])).astype(BF16)
    sums = jnp.concatenate([col_sums(hgrad * unit), col_sums(hgrad), jnp.zeros((6, w), F32)], 0)
    start = (pl.program_id(0) == 0) & (pl.program_id(1) == 0)

    @pl.when(start)
    def _():
        sums_ref[...] = sums

    @pl.when(jnp.logical_not(start))
    def _():
        sums_ref[...] += sums


def entry_grads(x, rgrad, token_proj, data_map, incoming, w_qkv, gain):
    docs, _, w = x.shape
    tile = 256
    rows = pl.BlockSpec((1, tile, w), lambda d, i: (d, i, 0))
    return pl.pallas_call(
        entry_kernel,
        grid=(docs, L // tile),
        in_specs=[rows, rows, pl.BlockSpec((3, 1, tile, w), lambda d, i: (0, d, i, 0)),
                  pl.BlockSpec((1, NB, tile), lambda d, i: (d, 0, i)), pl.BlockSpec((1, NB, w), lambda d, i: (d, 0, 0)),
                  whole(w_qkv.shape), whole((1, w))],
        out_specs=[rows, pl.BlockSpec((8, w), lambda d, i: (0, 0))],
        out_shape=[jax.ShapeDtypeStruct((docs, L, w), BF16), jax.ShapeDtypeStruct((8, w), F32)],
        compiler_params=pltpu.CompilerParams(vmem_limit_bytes=40 << 20),
        cost_estimate=pl.CostEstimate(flops=docs * L * w * w * 6 + docs * L * NB * w * 12, bytes_accessed=docs * L * w * 14, transcendentals=0),
    )(x, rgrad, token_proj, data_map, incoming, w_qkv, gain[None])


MESH = pl.DeviceIdType.MESH
GROUPS = 3
STAGES = 5


AXES = ("z1", "z0", "x")


class Part:
    def __init__(self, me, held, out, cols, order, got, sems):
        self.me, self.held, self.out, self.got, self.sems = me, held, out, got, sems
        self.cols, self.order = cols, order
        self.stage = 0

    def span(self, which):
        count = self.held.shape[3] // 2
        return pl.ds(pl.multiple_of(which * count, 8), count)

    def at(self, axis, flip, index):
        done = self.order[: self.stage]
        where, free = [], 0
        for name in AXES:
            if name in done or name == axis:
                which = self.me[name]
                where.append(1 - which if flip and name == axis else which)
            elif index is None:
                where.append(slice(None))
            else:
                where.append(index[free])
                free += 1
        rows = slice(None)
        if "seg" in done or axis == "seg":
            which = self.me["seg"]
            rows = self.span(1 - which if flip and axis == "seg" else which)
        return self.held.at[(*where, rows, pl.ds(*self.cols))]

    def send(self):
        last = self.stage == 4
        to = "seg" if last else self.order[self.stage]
        source = self.at(None if last else to, not last, None)
        target = self.out.at[self.span(self.me["seg"]), pl.ds(*self.cols)] if last else self.got[self.stage]
        send, recv, local = self.sems
        self.copy = pltpu.make_async_remote_copy(
            src_ref=source, dst_ref=target, send_sem=send.at[self.stage], recv_sem=recv.at[self.stage],
            device_id=self.me["ids"][to], device_id_type=MESH)
        self.copy.start()
        if last:
            self.own = pltpu.make_async_copy(source, target, local)
            self.own.start()

    def advance(self):
        self.copy.wait()
        if self.stage == 4:
            self.own.wait()
            return
        got = self.got[self.stage]
        axis = self.order[self.stage]
        lead = len(got.shape) - 2

        def add(i, _):
            index = tuple((i >> (lead - 1 - k)) & 1 for k in range(lead))
            ref = self.at(axis, False, index)
            ref[...] += got[index]
            return 0

        lax.fori_loop(0, 1 << lead, add, 0)
        self.stage += 1
        self.send()


ORDERS = {
    "A": ("x", "seg", "z0", "z1"),
    "B": ("seg", "x", "z0", "z1"),
    "C": ("z0", "x", "seg", "z1"),
    "D": ("x", "z0", "seg", "z1"),
    "E": ("z0", "seg", "x", "z1"),
    "F": ("x", "z0", "z1", "seg"),
    "H": ("z0", "x", "z1", "seg"),
    "I": ("seg", "z0", "x", "z1"),
}
UNIT = 384
PLAN = ((("D", 4), ("I", 4)), (("H", 4), ("A", 4)), (("C", 4), ("A", 4)))
SCRIPT = (
    "back", "in", "att0", "1D", "1I", "att1", "local", "2H", "2A", "three",
    "1D", "1I", "entry", "1D", "1I", "2H", "2A", "3C", "s1",
    "3A", "3C", "3A", "1D", "1I", "s2", "2A", "3C", "1D", "1I",
    "2H", "s3", "2H", "3A", "2A", "2H", "3C", "s4", "2A", "3A",
    "3C", "3A", "s5",
)


def landing(rows, cols, order):
    shapes = []
    for stage, axis in enumerate(order):
        done = order[: stage + 1]
        lead = sum(name not in done for name in AXES)
        shapes.append((2,) * lead + (rows // 2 if "seg" in done else rows, cols))
    return [pltpu.VMEM(shape, F32) for shape in shapes]


def tail_kernel(docs, bits, *refs):
    (act, cot, normed, pre, qkv, mem, mgrad, mixed, lse, hidden, mem_rows, mixed_rows, branch, w_qkv, x, rgrad,
     data_map, carry_map, has, vec, small_in) = refs[:21]
    o_back, o_in, o_three, o_input, o_start, small, tok, memp = refs[21:29]
    h1, h2, h3, rc, slots, slot1, acc1, acc2, lg, inc, rsmall = refs[29:40]
    count = sum(len(p) for p in PLAN)
    gots = refs[40 : 40 + count * 4]
    send, recv, local, csend, crecv, misc_send, misc_recv, ssend, srecv, credit = refs[40 + count * 4 :]
    b, s = lax.axis_index("batch"), lax.axis_index("seg")
    n, w = cot.shape
    ff = act.shape[1]

    def flip(distance):
        return b + distance * (1 - 2 * ((b // distance) % 2))

    ids = {"core": (flip(1), s), "x": (flip(2), s), "z0": (flip(4), s), "z1": (flip(8), s), "seg": (b, 1 - s)}
    me = {"core": b % 2, "x": (b // 2) % 2, "z0": (b // 4) % 2, "z1": (b // 8) % 2, "seg": s, "ids": ids}
    mine = me["core"]

    @pl.when(s == 1)
    def _():
        inc[...] = jnp.zeros_like(inc)

    small[...] = small_in[...]
    barrier = pltpu.get_barrier_semaphore()
    for who in ids.values():
        pl.semaphore_signal(barrier, inc=1, device_id=who, device_id_type=MESH)
    pl.semaphore_wait(barrier, len(ids))

    def core_copy(g, i, slot, target):
        return pltpu.make_async_remote_copy(
            src_ref=slot, dst_ref=target, send_sem=csend.at[g, i], recv_sem=crecv.at[g, i], device_id=ids["core"], device_id_type=MESH)

    parts = {}
    for g, held in enumerate((h1, h2, h3)):
        first = 0
        for kind, units in PLAN[g]:
            i = len(parts)
            sems = (send.at[i], recv.at[i], local.at[i])
            out = (o_back, o_in, o_three)[g]
            parts[str(g + 1) + kind] = Part(me, held, out, (first, units * UNIT), ORDERS[kind], gots[4 * i : 4 * i + 4], sems)
            first += units * UNIT

    def send_group(g):
        for name, part in parts.items():
            if name[0] == str(g + 1):
                part.send()

    own2 = w // 16

    def core_slice(g, i, tile):
        cols = pl.ds(pl.multiple_of(i * tile, 128), tile)
        return core_copy(g, i, slots.at[i % 2, :, :, pl.ds(0, tile)], rc.at[:, :, cols])

    def pass_rows(g, i, held, tile):
        cols = pl.ds(pl.multiple_of(i * tile, 128), tile)

        @pl.when(i >= 2)
        def _():
            core_slice(g, i - 2, tile).wait_send()

        for k in range(8):
            slots[i % 2, k, :, 0:tile] = acc2[pl.ds(pl.multiple_of((2 * k + 1 - mine) * own2, 8), own2), 0:tile]
        core_slice(g, i, tile).start()
        for k in range(8):
            held[k // 4, k // 2 % 2, k % 2, :, cols] = acc2[pl.ds(pl.multiple_of((2 * k + mine) * own2, 8), own2), 0:tile]

    def took_core(g, copy, steps, held):
        copy(steps - 2).wait_send()
        copy(steps - 1).wait_send()

        def took(i, _):
            copy(i).wait_recv()
            return 0

        def add(k, _):
            held[k // 4, k // 2 % 2, k % 2] += rc[k]
            return 0

        lax.fori_loop(0, steps, took, 0)
        lax.fori_loop(0, 8, add, 0)
        if g < 2:
            pl.semaphore_signal(credit, inc=1, device_id=ids["core"], device_id_type=MESH)
        send_group(g)

    own1 = ff // 16

    def copy1(i):
        return core_copy(0, i, slot1.at[i % 2], rc.at[i])

    def back_body(act_ref, cot_ref):
        i = pl.program_id(0)
        acc1[...] = tn(act_ref[...], cot_ref[...])

        @pl.when(i >= 2)
        def _():
            copy1(i - 2).wait_send()

        for q in range(own1 // own2):
            cols = pl.ds(q * w, w)
            slot1[i % 2, :, cols] = acc1[pl.ds(pl.multiple_of((1 - mine) * own1 + q * own2, 8), own2)]
        copy1(i).start()
        for q in range(own1 // own2):
            cols = pl.ds(q * w, w)
            h1[i // 4, i // 2 % 2, i % 2, :, cols] = acc1[pl.ds(pl.multiple_of(mine * own1 + q * own2, 8), own2)]

    def do_back():
        pltpu.emit_pipeline(
            back_body, grid=(8,),
            in_specs=[pl.BlockSpec((n, 2 * own1), lambda i: (0, i)), pl.BlockSpec((n, w), lambda i: (0, 0))],
            out_specs=[],
        )(act, cot)
        took_core(0, copy1, 8, h1)

    tile2 = acc2.shape[1]

    def in_body(normed_ref, pre_ref):
        acc2[...] = tn(normed_ref[...], pre_ref[...])
        pass_rows(1, pl.program_id(0), h2, tile2)

    def do_in():
        pl.semaphore_wait(credit, 1)
        pltpu.emit_pipeline(
            in_body, grid=(ff // tile2,),
            in_specs=[pl.BlockSpec((n, w), lambda i: (0, 0)), pl.BlockSpec((n, tile2), lambda i: (0, i))],
            out_specs=[],
        )(normed, pre)
        took_core(1, lambda i: core_slice(1, i, tile2), ff // tile2, h2)

    pairs = w // 128

    def attention(doc):
        def body(*r):
            cols = pl.ds(pl.multiple_of(pl.program_id(0) * 128, 128), 128)
            qs, vs = grads_core(*r)
            small[0:1, cols] += qs
            small[1:2, cols] += vs

        t = lambda o: pl.BlockSpec((1, L, 128), lambda i: (doc, 0, o * pairs + i))
        m = lambda o: pl.BlockSpec((1, NB, 128), lambda i: (doc, 0, o * pairs + i))
        pltpu.emit_pipeline(
            body, grid=(pairs,),
            in_specs=[t(0), t(1), t(2), m(0), m(1), t(0), t(0), pl.BlockSpec((1, 1, 2, L), lambda i: (doc, i, 0, 0))],
            out_specs=[pl.BlockSpec((3, 1, L, 128), lambda i: (0, doc, 0, i)), pl.BlockSpec((2, 1, NB, 128), lambda i: (0, doc, 0, i))],
        )(qkv, qkv, qkv, mem, mem, mgrad, mixed, lse, tok, memp)

    def local_body(g_ref, w_ref):
        total = None
        for d in range(docs):
            part = nt(g_ref[0, d], w_ref[...])
            rows = pl.ds(d * NB, NB)

            @pl.when(pl.program_id(0) == 0)
            def _():
                lg[rows] = part

            @pl.when(pl.program_id(0) == 1)
            def _():
                lg[rows] += part

    def do_local():
        pltpu.emit_pipeline(
            local_body, grid=(2,),
            in_specs=[pl.BlockSpec((1, docs, NB, w), lambda i: (i, 0, 0, 0)), pl.BlockSpec((w, w), lambda i: (0, 1 + i))],
            out_specs=[],
        )(memp, w_qkv)

    upward = pltpu.make_async_remote_copy(
        src_ref=lg, dst_ref=inc, send_sem=misc_send.at[0], recv_sem=misc_recv.at[0], device_id=ids["seg"], device_id_type=MESH)

    def begin_upward():
        @pl.when(s == 1)
        def _():
            upward.start()

    tile3 = w
    per = w // tile3
    m = mem_rows.shape[0]

    def three_body(hidden_ref, mem_ref, mixed_ref, tok_ref, memg_ref, branch_ref):
        part = pl.program_id(0)

        @pl.when(part == 0)
        def _():
            acc2[:, 0:tile3] = sum(tn(hidden_ref[d], tok_ref[0, d]) for d in range(docs))

        @pl.when((part == 1) | (part == 2))
        def _():
            acc2[:, 0:tile3] = sum(tn(hidden_ref[d], tok_ref[0, d]) + tn(mem_ref[d], memg_ref[0, d]) for d in range(docs))

        @pl.when(part == 3)
        def _():
            acc2[:, 0:tile3] = tn(mixed_ref[...], branch_ref[...])

        pass_rows(2, part * per + pl.program_id(1), h3, tile3)

    def do_three():
        pl.semaphore_wait(credit, 1)
        pltpu.emit_pipeline(
            three_body, grid=(4, per),
            in_specs=[pl.BlockSpec((docs, L, w), lambda p, i: (0, 0, 0)), pl.BlockSpec((docs, NB, w), lambda p, i: (0, 0, 0)),
                      pl.BlockSpec((n, w), lambda p, i: (0, 0)),
                      pl.BlockSpec((1, docs, L, tile3), lambda p, i: (jnp.minimum(p, 2), 0, 0, jnp.where(p < 3, i, per - 1))),
                      pl.BlockSpec((1, docs, NB, tile3), lambda p, i: (jnp.clip(p - 1, 0, 1), 0, 0, jnp.where(p < 1, 0, jnp.where(p < 3, i, per - 1)))),
                      pl.BlockSpec((n, tile3), lambda p, i: (0, jnp.where(p < 3, 0, i)))],
            out_specs=[],
        )(hidden, mem_rows, mixed_rows, tok, memp, branch)
        took_core(2, lambda i: core_slice(2, i, tile3), 4 * per, h3)

    tile4 = 256

    def entry_body(x_ref, rgrad_ref, proj_ref, data_ref, w_ref, out_ref):
        d = pl.program_id(0)
        hgrad = dot_hi(data_ref[0], inc[pl.ds(pl.multiple_of(d * NB, NB), NB)], 0, 0)
        for p in range(3):
            hgrad = hgrad + nt(proj_ref[p, 0], w_ref[:, pl.ds(p * w, w)])
        unit, rate = normalised(x_ref[0].astype(F32))
        out_ref[0] = (rgrad_ref[0] + norm_back(unit, rate, hgrad * vec[4:5])).astype(BF16)
        small[4:5] += col_sums(hgrad * unit)
        small[5:6] += col_sums(hgrad)

    rows4 = pl.BlockSpec((1, tile4, w), lambda d, i: (d, i, 0))
    def do_entry():
        @pl.when(s == 0)
        def _():
            upward.wait_recv()

        pltpu.emit_pipeline(
            entry_body, grid=(docs, L // tile4),
            in_specs=[rows4, rows4, pl.BlockSpec((3, 1, tile4, w), lambda d, i: (0, d, i, 0)),
                      pl.BlockSpec((1, NB, tile4), lambda d, i: (d, 0, i)), pl.BlockSpec((w, 3 * w), lambda d, i: (0, 0))],
            out_specs=[rows4],
        )(x, rgrad, tok, data_map, w_qkv, o_input)

    def add_small(k, to):
        copy = pltpu.make_async_remote_copy(
            src_ref=small, dst_ref=rsmall.at[k], send_sem=ssend.at[k], recv_sem=srecv.at[k], device_id=ids[to], device_id_type=MESH)
        copy.start()
        return copy

    def took_small(k, copy):
        copy.wait()
        small[...] += rsmall[k]

    def start_body(carry_ref):
        d = pl.program_id(0)
        rows = pl.ds(pl.multiple_of(d * NB, NB), NB)
        lg[rows] = has[d].astype(F32) * (lg[rows] + dot_hi(carry_ref[0], inc[rows], 0, 0))

    half = w // 2
    stay = pltpu.make_async_copy(lg.at[:, pl.ds(0, half)], o_start, misc_send.at[1])
    leave = pltpu.make_async_remote_copy(
        src_ref=lg.at[:, pl.ds(half, half)], dst_ref=o_start, send_sem=misc_send.at[2], recv_sem=misc_recv.at[1],
        device_id=ids["seg"], device_id_type=MESH)

    def do_start():
        @pl.when(s == 1)
        def _():
            upward.wait_send()

        pltpu.emit_pipeline(
            start_body, grid=(docs,),
            in_specs=[pl.BlockSpec((1, NB, NB), lambda d: (d, 0, 0))],
            out_specs=[],
        )(carry_map)

        @pl.when(s == 0)
        def _():
            stay.start()
            leave.start()

    links = ("core", "x", "seg", "z0", "z1")
    for step in SCRIPT:
        if step == "back":
            do_back()
        elif step == "in":
            do_in()
        elif step[:3] == "att":
            attention(int(step[3:]))
        elif step == "local":
            do_local()
            begin_upward()
        elif step == "three":
            do_three()
        elif step == "entry":
            do_entry()
            tiny = add_small(0, "core")
            do_start()
        elif step[0] == "s":
            k = int(step[1])
            took_small(k - 1, tiny)
            if k < 5:
                tiny = add_small(k, links[k])
        else:
            parts[step].advance()

    @pl.when(s == 0)
    def _():
        stay.wait()
        leave.wait_send()

    @pl.when(s == 1)
    def _():
        leave.wait_recv()


def tail(docs, batch, act, cot, normed, pre, qkv, mem, mgrad, mixed, lse, hidden, mem_rows, branch, w_qkv, x, rgrad,
         data_map, carry_map, has, vec, small):
    n, w = cot.shape
    ff = act.shape[1]
    own1, own2 = ff // batch, w // batch
    ops = [act, cot, normed, pre, qkv, mem, mgrad, mixed, lse, hidden, mem_rows, mixed.reshape(n, w), branch, w_qkv, x, rgrad,
           data_map, carry_map, has, vec, small]
    anywhere = pl.BlockSpec(memory_space=pl.ANY)
    vmem = pl.BlockSpec(memory_space=pltpu.VMEM)
    f = lambda *shape: jax.ShapeDtypeStruct(shape, F32)
    outs = [f(own2, ff), f(own2, ff), f(own2, 4 * w), jax.ShapeDtypeStruct((docs, L, w), BF16), f(docs * NB, w // 2), f(16, w),
            jax.ShapeDtypeStruct((3, docs, L, w), BF16), jax.ShapeDtypeStruct((2, docs, NB, w), BF16)]
    held = [pltpu.VMEM((2, 2, 2, own2, ff), F32)] * GROUPS
    slots = [pltpu.VMEM((8, own2, ff), F32), pltpu.VMEM((2, 8, own2, w), F32), pltpu.VMEM((2, own2, ff), F32)]
    accs = [pltpu.VMEM((2 * own1, w), F32), pltpu.VMEM((w, w), F32)]
    rest = [pltpu.VMEM((docs * NB, w), F32), pltpu.VMEM((docs * NB, w), F32), pltpu.VMEM((5, 16, w), F32)]
    gots = [buffer for plan in PLAN for kind, units in plan for buffer in landing(own2, units * UNIT, ORDERS[kind])]
    count = len(gots) // 4
    dma = pltpu.SemaphoreType.DMA
    sems = [dma((count, STAGES)), dma((count, STAGES)), dma((count,)), dma((GROUPS, 8)), dma((GROUPS, 8)),
            dma((3,)), dma((2,)), dma((5,)), dma((5,)), pltpu.SemaphoreType.REGULAR]
    return pl.pallas_call(
        functools.partial(tail_kernel, docs, 4),
        in_specs=[anywhere] * 18 + [pl.BlockSpec(memory_space=pltpu.SMEM), vmem, vmem],
        out_specs=[anywhere] * 5 + [vmem] + [anywhere] * 2,
        out_shape=outs,
        scratch_shapes=held + slots + accs + rest + gots + sems,
        compiler_params=pltpu.CompilerParams(vmem_limit_bytes=60 << 20, collective_id=0, has_side_effects=True),
        cost_estimate=pl.CostEstimate(flops=10**11, bytes_accessed=10**8, transcendentals=10**7),
    )(*ops)[:6]


def front_kernel(docs, *refs):
    (x, cot, w_qkv_hbm, w_out_hbm, w_in_hbm, w_back_hbm, start, has, sticky, *singles) = refs[:18]
    (result, normed, act, pre, rgrad, branch, mgrad, qkv_out, mem_out, mem_low_out, hidden_out, mixed_out, lse_out,
     carry_out, data_out, small, vec) = refs[18:35]
    (w_qkv, w_out, w_in, w_back, xs, hidden, qkv, memory, fresh, begin, mem, mem_low, mixed, lse, carry, data, a,
     partial, peaks, totals, wsem, osem, bsem, ssem, rsem) = refs[35:]
    b, s = lax.axis_index("batch"), lax.axis_index("seg")
    w = x.shape[2]
    half = w // 2
    q_bias, v_bias, out_bias, back_bias, gain1, offset1, gain2, offset2 = (vec.at[pl.ds(i, 1)] for i in range(8))
    in_bias = lambda k: vec[8 + k : 9 + k]
    for i in range(8):
        vec[i : i + 1] = singles[i][...][None]
    for i in range(w_in_hbm.shape[1] // w):
        vec[8 + i : 9 + i] = singles[8][pl.ds(i * w, w)][None]
    loads = [pltpu.make_async_copy(src, dst, wsem.at[i]) for i, (src, dst) in enumerate(
        [(x, xs), (w_qkv_hbm, w_qkv), (w_out_hbm, w_out), (w_in_hbm, w_in), (w_back_hbm, w_back)])]
    for load in loads:
        load.start()
    own_begin = pltpu.make_async_copy(start, begin.at[0], bsem)
    own_begin.start()
    peer = (b, 1 - s)
    barrier = pltpu.get_barrier_semaphore()
    pl.semaphore_signal(barrier, inc=1, device_id=peer, device_id_type=MESH)
    pl.semaphore_wait(barrier, 1)

    given = pltpu.make_async_remote_copy(
        src_ref=start, dst_ref=begin.at[1], send_sem=ssem.at[docs], recv_sem=rsem.at[docs], device_id=peer, device_id_type=MESH)

    @pl.when(s == 1)
    def _():
        given.start()

    maps_kernel(docs, sticky.at[:, 0], carry, data, a)
    outs = [pltpu.make_async_copy(carry, carry_out, osem.at[0]), pltpu.make_async_copy(data, data_out, osem.at[1])]
    for out in outs:
        out.start()

    loads[0].wait()
    for d in range(docs):
        unit, _ = normalised(xs[d].astype(F32))
        hidden[d] = (unit * gain1[...] + offset1[...]).astype(BF16)
    outs.append(pltpu.make_async_copy(hidden, hidden_out, osem.at[2]))
    outs[-1].start()
    own_begin.wait()

    @pl.when(s == 0)
    def _():
        given.wait_recv()
        for d in range(docs):
            flag = has[d].astype(F32)
            memory[d, :, 0:half] = flag * begin[0, d]
            memory[d, :, half:w] = flag * begin[1, d]

    def carried(d):
        return pltpu.make_async_remote_copy(
            src_ref=fresh.at[d], dst_ref=memory.at[d], send_sem=ssem.at[d], recv_sem=rsem.at[d], device_id=peer, device_id_type=MESH)

    @pl.when(s == 0)
    def _():
        for d in range(docs):
            fresh[d] = dot_hi(carry[d], memory[d], 1, 0) + dot_hi(data[d], hidden[d].astype(F32), 1, 0)
            carried(d).start()

    loads[1].wait()
    zero = jnp.zeros((1, w), F32)
    for d in range(docs):
        for p, bias in enumerate((q_bias[...], zero, v_bias[...])):
            cols = pl.ds(p * w, w)
            qkv[d, :, cols] = (mm(hidden[d], w_qkv[:, cols]) + bias).astype(BF16)
    outs.append(pltpu.make_async_copy(qkv, qkv_out, osem.at[3]))
    outs[-1].start()
    small[...] = jnp.zeros_like(small)
    vectors = (out_bias, back_bias, gain2, offset2)
    tile = 256
    pairs = w // 128

    def columns(p, i):
        return pl.ds(pl.multiple_of(p * w + i * 128, 128), 128)

    def early(k, _):
        d, i = k // pairs, k % pairs
        attend_tokens(qkv.at[d, :, columns(0, i)], qkv.at[d, :, columns(1, i)], qkv.at[d, :, columns(2, i)],
                      partial.at[d, i], peaks.at[d, i], totals.at[d, i])
        return 0

    lax.fori_loop(0, docs * pairs, early, 0)
    for load in loads[2:]:
        load.wait()
    for d in range(docs):
        @pl.when(s == 1)
        def _():
            carried(d).wait_recv()

        low = memory[d].astype(BF16)
        mem_low[d] = low
        for p, bias in enumerate((zero, v_bias[...])):
            mem[d, :, pl.ds(p * w, w)] = (mm(low, w_qkv[:, pl.ds((p + 1) * w, w)]) + bias).astype(BF16)

        def late(i, _):
            attend_memory(qkv.at[d, :, columns(0, i)], mem.at[d, :, columns(0, i)], mem.at[d, :, columns(1, i)],
                          partial.at[d, i], peaks.at[d, i], totals.at[d, i], mixed.at[d, :, columns(0, i)], lse.at[d, i])
            return 0

        lax.fori_loop(0, pairs, late, 0)

        def feed_body(x_ref, cot_ref, *out_refs):
            rows = pl.ds(pl.multiple_of(pl.program_id(0) * tile, tile), tile)
            wide, sums = feed_core(x_ref, mixed.at[d, rows], cot_ref, w_out, w_in, w_back, vectors, in_bias, *out_refs)
            small[2:3] += sums[1]
            small[3:4] += sums[0]
            small[6:7] += sums[2]
            small[7:8] += sums[3]
            for k, part in enumerate(wide):
                small[8 + k : 9 + k] += part

        first = d * (L // tile)
        rows = lambda c: pl.BlockSpec((tile, c), lambda i: (first + i, 0))
        ff = w_in.shape[1]
        pltpu.emit_pipeline(
            feed_body, grid=(L // tile,),
            in_specs=[pl.BlockSpec((tile, w), lambda i: (i, 0)), rows(w)],
            out_specs=[rows(w), rows(w), rows(ff), rows(ff), rows(w), rows(w), rows(w)],
        )(x.at[d], cot, result, normed, act, pre, rgrad, branch, mgrad)
    for i, (src, dst) in enumerate([(mem, mem_out), (mem_low, mem_low_out), (mixed, mixed_out), (lse, lse_out)]):
        outs.append(pltpu.make_async_copy(src, dst, osem.at[4 + i]))
        outs[-1].start()
    for out in outs:
        out.wait()

    @pl.when(s == 0)
    def _():
        for d in range(docs):
            carried(d).wait_send()

    @pl.when(s == 1)
    def _():
        given.wait_send()


def front(x, cot, w_qkv, w_out, w_in, w_back, start, has, sticky, *singles):
    docs, _, w = x.shape
    n = docs * L
    ff = w_in.shape[1]
    anywhere = pl.BlockSpec(memory_space=pl.ANY)
    vmem = pl.BlockSpec(memory_space=pltpu.VMEM)
    arr = jax.ShapeDtypeStruct
    lse_shape = (docs, w // 128, 2, L)
    kept = [(docs, L, 3 * w), (docs, NB, 2 * w), (docs, NB, w), (docs, L, w), (docs, L, w)]
    outs = [arr((n, c), t) for c, t in ((w, BF16), (w, BF16), (ff, BF16), (ff, BF16), (w, F32), (w, BF16), (w, BF16))]
    outs += [arr(shape, BF16) for shape in kept]
    outs += [arr(lse_shape, F32), arr((docs, NB, NB), F32), arr((docs, NB, L), F32), arr((16, w), F32), arr((16, w), F32)]
    v = pltpu.VMEM
    scratch = [v(w_qkv.shape, BF16), v(w_out.shape, BF16), v(w_in.shape, BF16), v(w_back.shape, BF16), v((docs, L, w), BF16),
               v((docs, L, w), BF16), v(kept[0], BF16), v((docs, NB, w), F32), v((docs, NB, w), F32), v((2, docs, NB, w // 2), F32),
               v(kept[1], BF16), v(kept[2], BF16), v((docs, L, w), BF16), v(lse_shape, F32), v((docs, NB, NB), F32),
               v((docs, NB, L), F32), v((docs, NB, NB), F32), v((docs, w // 128, 128, L), F32), v(lse_shape, F32), v(lse_shape, F32)]
    dma = pltpu.SemaphoreType.DMA
    scratch += [dma((5,)), dma((8,)), dma, dma((docs + 1,)), dma((docs + 1,))]
    return pl.pallas_call(
        functools.partial(front_kernel, docs),
        in_specs=[anywhere] * 7 + [pl.BlockSpec(memory_space=pltpu.SMEM)] + [vmem] * 10,
        out_specs=[anywhere] * 15 + [vmem] * 2,
        out_shape=outs,
        scratch_shapes=scratch,
        compiler_params=pltpu.CompilerParams(vmem_limit_bytes=60 << 20, collective_id=1, has_side_effects=True),
        cost_estimate=pl.CostEstimate(flops=10**11, bytes_accessed=10**8, transcendentals=10**7),
    )(x, cot, w_qkv, w_out, w_in, w_back, start, has, sticky, *singles)


def hand_over_kernel(back, wide, three, entry, start, result, small, *refs):
    outs, stages, sem = refs[:16], refs[16:23], refs[23]
    w = three.shape[1] // 4
    b = lax.axis_index("batch")
    pairs = [(back, outs[5]), (wide, outs[4]), (three.at[:, pl.ds(0, 3 * w)], outs[2]), (three.at[:, pl.ds(3 * w, w)], outs[3]),
             (entry, outs[1]), (result, outs[0]), (start, outs[6])]
    copies = [pltpu.make_async_copy(src, stage, sem.at[0, i]) for i, ((src, _), stage) in enumerate(zip(pairs, stages))]
    order = (4, 5, 2, 6, 1, 0, 3)
    for i in order:
        copies[i].start()
    short = back.shape[0]
    away = []
    for i in order:
        copies[i].wait()
        if i == 0:
            pieces = [(stages[0].at[:, pl.ds(q * w, w)], outs[5].at[pl.ds(q * short, short)], 7 + q) for q in range(4)]
        else:
            pieces = [(stages[i], pairs[i][1], i)]
        for src, dst, k in pieces:
            away.append(pltpu.make_async_copy(src, dst, sem.at[1, k]))
            away[-1].start()
    own = w // 16
    rows = lax.broadcasted_iota(jnp.int32, (w, 256), 0)
    cols = lax.broadcasted_iota(jnp.int32, (w, 256), 1)
    pick = (rows == cols + b * own) & (cols < own)
    mine = dot_hi(small[...], jnp.where(pick, 1.0, 0.0), 1, 0)
    pick = (rows == cols + (b % 4) * (4 * own)) & (cols < 4 * own)
    row = lax.broadcasted_iota(jnp.int32, (16, 1), 0) == 8 + b // 4
    long = dot_hi(jnp.where(row, small[...], 0.0), jnp.where(pick, 1.0, 0.0), 1, 0)
    long = jnp.sum(long, 0, keepdims=True)
    for i in range(8):
        outs[7 + i][...] = mine[i, :own]
    outs[15][...] = long[0, : 4 * own]
    for out in away:
        out.wait()


def hand_over(back, wide, three, entry, start, result, small):
    w = three.shape[1] // 4
    anywhere = pl.BlockSpec(memory_space=pl.ANY)
    vmem = pl.BlockSpec(memory_space=pltpu.VMEM)
    arr = lambda a: jax.ShapeDtypeStruct(a.shape, a.dtype)
    rows = three.shape[0]
    stages = [(back.shape, F32), (wide.shape, F32), ((rows, 3 * w), F32), ((rows, w), F32), (entry.shape, BF16), (result.shape, BF16),
              (start.shape, F32)]
    return pl.pallas_call(
        hand_over_kernel,
        in_specs=[anywhere] * 6 + [vmem],
        out_specs=[anywhere] * 7 + [vmem] * 9,
        out_shape=[arr(result), arr(entry), jax.ShapeDtypeStruct((rows, 3 * w), F32), jax.ShapeDtypeStruct((rows, w), F32), arr(wide),
                   jax.ShapeDtypeStruct((4 * rows, w), F32), arr(start)] + [jax.ShapeDtypeStruct((w // 16,), F32)] * 8 + [jax.ShapeDtypeStruct((w // 4,), F32)],
        scratch_shapes=[pltpu.VMEM(a, t) for a, t in stages] + [pltpu.SemaphoreType.DMA((2, 11))],
        compiler_params=pltpu.CompilerParams(vmem_limit_bytes=60 << 20),
        cost_estimate=pl.CostEstimate(flops=10**7, bytes_accessed=10**7, transcendentals=0),
    )(back, wide, three, entry, start, result, small)


def outer(a, b):
    return lax.dot_general(a, b, (((0,), (0,)), ((), ())), preferred_element_type=F32)


def passed(block, distance):
    n = lax.axis_size("seg")
    return lax.ppermute(block, "seg", [(i - distance, i) for i in range(n) if 0 <= i - distance < n])


def swap(block, axis, distance):
    n = lax.axis_size(axis)
    return lax.ppermute(block, axis, [(i, i ^ distance) for i in range(n)])


def halve(block, axis, distance, dim):
    bit = (lax.axis_index(axis) // distance) % 2
    send = lax.dynamic_index_in_dim(block, 1 - bit, dim, keepdims=False)
    keep = lax.dynamic_index_in_dim(block, bit, dim, keepdims=False)
    return keep + swap(send, axis, distance)


def spread(work, seg_place, first):
    n, s = lax.axis_size("batch"), lax.axis_size("seg")
    bits = n.bit_length() - 1
    _, own, cols = work.shape
    split = s if seg_place < bits and own % s == 0 else 1
    work = work.reshape((2,) * (bits - first) + (split, own // split, cols))
    for k in range(first, bits + 1):
        if k == seg_place:
            if split == 1:
                d = 1
                while d < s:
                    work = work + swap(work, "seg", d)
                    d *= 2
            else:
                left = bits - k
                work = work.reshape((2,) * left + (2,) * (s.bit_length() - 1) + (own // split, cols))
                d = 1
                while d < s:
                    work = halve(work, "seg", d, work.ndim - 3)
                    d *= 2
        if k < bits:
            work = halve(work, "batch", 1 << k, bits - 1 - k)
    if split > 1:
        d = s // 2
        while d >= 1:
            bit = (lax.axis_index("seg") // d) % 2
            other = swap(work, "seg", d)
            work = jnp.where(bit == 0, jnp.concatenate([work, other], 0), jnp.concatenate([other, work], 0))
            d //= 2
    return work.reshape(own, cols)


def forward(x, cot, w_qkv, w_out, w_in, w_back, start_memory, has_memory, sticky,
            q_bias, v_bias, out_bias, in_bias, back_bias, ln1_gain, ln1_bias, ln2_gain, ln2_bias):
    docs, _, width = x.shape
    n = docs * L
    chain = lax.axis_size("seg")
    is_first = lax.axis_index("seg") == 0
    flags = has_memory.astype(F32)[:, None, None]

    parts = [start_memory] + [lax.ppermute(start_memory, "seg", [(i, 0)]) for i in range(1, chain)]
    own_start = jnp.where(is_first, flags * jnp.concatenate(parts, 2), 0.0)

    carry_map, data_map = memory_maps(sticky)
    bias = jnp.concatenate([q_bias, jnp.zeros_like(q_bias), v_bias])
    hidden, qkv = project(x, w_qkv, bias, ln1_gain, ln1_bias)

    memory = own_start
    for i in range(chain - 1):
        memory = passed(renew(carry_map, data_map, memory, hidden), 1) + own_start

    mem_rows, mem = recall(memory.reshape(docs * NB, width), w_qkv, bias)
    mem = mem.reshape(docs, NB, 2 * width)
    mixed, log_total = attend(qkv, mem)
    rows4 = jnp.stack([out_bias, back_bias, ln2_gain, ln2_bias])
    result, normed, act, pre, residual_grad, branch, mixed_grad, wide, sums = feed(
        x.reshape(n, width), mixed.reshape(n, width), cot, w_out, w_in, w_back, rows4, in_bias
    )
    small = [sums[1:2], sums[0:1], jnp.zeros((2, width), F32), sums[2:4], wide.reshape(4, width)]
    small = jnp.concatenate([jnp.zeros((2, width), F32)] + small + [jnp.zeros((4, width), F32)], 0)
    return (result, normed, act, pre, residual_grad, branch, mixed_grad, qkv, mem, mem_rows, hidden, mixed, log_total,
            carry_map, data_map, small)


def spread_out(x, act, cot, normed, pre, qkv, mem, mgrad, mixed, lse, hidden, mem_rows, branch, w_qkv, rgrad, data_map, carry_map, has_memory, gain, small):
    docs, _, width = x.shape
    n = docs * L
    batch, chain = lax.axis_size("batch"), lax.axis_size("seg")
    is_first = lax.axis_index("seg") == 0
    flags = has_memory.astype(F32)[:, None, None]
    grad_back = spread(outer(act, cot).reshape(batch, -1, width), 2, 0)
    grad_in = spread(outer(normed, pre).reshape(batch, width // batch, -1), 1, 0)
    token_proj, memory_proj, attn_sums = attend_grads(qkv, mem, mgrad, mixed, lse)
    memory_proj = memory_proj.reshape(2, docs * NB, width)
    local_grad = local_memory_grad(memory_proj, w_qkv).reshape(docs, NB, width)
    carry_back = carry_map.swapaxes(1, 2)
    incoming = jnp.zeros_like(local_grad)
    for i in range(chain - 1):
        sent = local_grad if i == 0 else jnp.matmul(carry_back, incoming, precision=HI) + local_grad
        incoming = passed(sent, -1)
    hidden_rows = hidden.reshape(n, width)
    three = [outer(hidden_rows, token_proj[i].reshape(n, width)) for i in range(3)]
    three = [three[0]] + [three[i + 1] + outer(mem_rows, memory_proj[i]) for i in range(2)]
    three = jnp.concatenate(three + [outer(mixed.reshape(n, width), branch)], 1)
    grad_three = spread(three.reshape(batch, width // batch, -1), 2, 0)
    input_grad, entry_sums = entry_grads(
        x, rgrad, token_proj, data_map, incoming, w_qkv, gain
    )
    start_grad = jnp.where(is_first, flags * (local_grad + jnp.matmul(carry_back, incoming, precision=HI)), 0.0)
    own = width // chain
    start_share = start_grad[:, :, :own]
    for i in range(1, chain):
        start_share = start_share + lax.ppermute(start_grad[:, :, i * own : (i + 1) * own], "seg", [(0, i)])

    wide = small[8:12].reshape(-1)
    packed = jnp.concatenate(
        [g.reshape(batch, 1, -1)
         for g in (jnp.sum(attn_sums[:, 0], 0), jnp.sum(attn_sums[:, 1], 0), small[2], small[3], entry_sums[0], entry_sums[1],
                   small[6], small[7], wide)], 2)
    packed = spread(packed, batch.bit_length() - 1, 0)[0]
    own = width // batch
    vectors = [packed[i * own : (i + 1) * own] for i in range(8)] + [packed[8 * own :]]
    return input_grad, start_share, grad_back, grad_in, grad_three, vectors


def shards(
    tokens,
    start_memory,
    has_memory,
    sticky,
    w_qkv,
    w_out,
    w_in,
    w_back,
    q_bias,
    v_bias,
    out_bias,
    in_bias,
    back_bias,
    ln1_gain,
    ln1_bias,
    ln2_gain,
    ln2_bias,
    cotangent,
):
    width = w_qkv.shape[0]
    docs = tokens.shape[0]
    n = docs * L
    chain = lax.axis_size("seg")
    batch = lax.axis_size("batch")
    x = tokens[:, 0]
    cot = cotangent[:, 0].reshape(n, width)
    if (batch, chain) == (16, 2):
        (result, normed, act, pre, residual_grad, branch, mixed_grad, qkv, mem, mem_rows, hidden, mixed, log_total,
         carry_map, data_map, small, vec) = front(
            x, cot, w_qkv, w_out, w_in, w_back, start_memory, has_memory, sticky,
            q_bias, v_bias, out_bias, back_bias, ln1_gain, ln1_bias, ln2_gain, ln2_bias, in_bias)
        sums = tail(
            docs, batch, act, cot, normed, pre, qkv, mem, mixed_grad.reshape(docs, L, width), mixed, log_total, hidden,
            mem_rows, branch, w_qkv, x, residual_grad.reshape(docs, L, width), data_map, carry_map, has_memory, vec, small)
        back, wide, three, entry, start, vectors = sums
        result, input_grad, grad_qkv, grad_out, grad_in, grad_back, start_share, *vectors = hand_over(
            back, wide, three, entry, start, result, vectors)
        start_share = start_share.reshape(docs, NB, width // chain)
    else:
        (result, normed, act, pre, residual_grad, branch, mixed_grad, qkv, mem, mem_rows, hidden, mixed, log_total,
         carry_map, data_map, small) = forward(
            x, cot, w_qkv, w_out, w_in, w_back, start_memory, has_memory, sticky[:, 0],
            q_bias, v_bias, out_bias, in_bias, back_bias, ln1_gain, ln1_bias, ln2_gain, ln2_bias)
        input_grad, start_share, grad_back, grad_in, grad_three, vectors = spread_out(
            x, act, cot, normed, pre, qkv, mem, mixed_grad.reshape(docs, L, width), mixed, log_total, hidden, mem_rows,
            branch, w_qkv, residual_grad.reshape(docs, L, width), data_map, carry_map, has_memory, ln1_gain, small
        )
        grad_qkv, grad_out = grad_three[:, : 3 * width], grad_three[:, 3 * width :]
    return (
        result.reshape(docs, 1, L, width),
        input_grad.reshape(docs, 1, L, width),
        start_share,
        grad_qkv,
        grad_out,
        grad_in,
        grad_back,
    ) + tuple(vectors[i] for i in (0, 1, 2, 8, 3, 4, 5, 6, 7))


def solution(mesh):
    rows = P("batch", "seg", None, None)
    in_specs = (rows, P("batch", None, "seg"), P("batch"), P("batch", "seg", None)) + (P(),) * 13 + (rows,)
    out_specs = (rows, rows, P("batch", None, "seg")) + (P("batch", None),) * 4 + (P("batch"),) * 9
    return jax.shard_map(shards, mesh=mesh, in_specs=in_specs, out_specs=out_specs, check_vma=False)
```
